32 devices in a mesh: groups: 2 (over y), owners: 4 (over z), split: 4 (over x, core).
Axes of the slice: x: 2, y: 2, z: 4, core: 2. Of those that a mesh axis runs over, the one named last changes fastest.
Arguments:
- embeddings: bfloat16 [16384, 4096], P(('groups', 'owners', 'split')), parts along dimension 0, may hold values from -6 to 6
- basis: bfloat16 [4096, 256], replicated, may hold values from -0.09375 to 0.09375
- owner_ids: int32 [16384, 1], P(('groups', 'owners', 'split')), parts along dimension 0, may hold values from 0 to 3; in each aligned block of 512 rows (0 to 511, 512 to 1023, ...) at most 256 rows name the same one
- sub_cluster: int32 [16384], P(('groups', 'owners', 'split')), parts along dimension 0, may hold values from 0 to 7, as said below
Outputs:
- nearest: float32 [16384], P(('groups', 'owners', 'split')), parts along dimension 0
The draws below stay inside these ranges and needn't reach their ends.
There are 2 independent parts, one for each index of `groups`. The reference program is written for one: setup_inputs(seed, part) draws one part's arguments, and reference() takes and returns one part's arrays. A program takes and returns all parts, laid end to end along the dimension named above; an argument that names none is the same for every part. Nothing has to cross between parts.
Inputs may be any that keep to these rules, and one draw needn't show every extreme that they name: `owner_ids`: among the rows of one device no value is named by more than 256 rows, a bound that some block reaches. `sub_cluster`: some clusters hold a single document.
All inputs are finite; a program needn't handle non-finite values.
Results may differ from the reference program's by a relative error of at most 0.0014.
Values may be sent and summed in bfloat16 or wider, within the bound.
No kernel may reach another device: no remote copies, remote signals or barrier semaphores. Data moves between devices by JAX's collectives and lax.ppermute only.
A program may use at most 64 MiB of HBM per device.

```python
import math
import jax
import jax.numpy as jnp
import numpy as np
from jax import lax

DIN = 4096
F = 256
CPO = 8
ROWS_DEV = 512
CAP = 256
TOKENS = 8192
N_OWNERS = 4
N_SPLIT = 4


def draw_sub_cluster(key, part):
    key = jax.random.fold_in(key, 5)
    label_key, single_key = jax.random.split(key)
    labels = jax.random.randint(label_key, (TOKENS,), 0, CPO - 1, dtype=jnp.int32)
    lone = jax.random.randint(single_key, (), 0, TOKENS, dtype=jnp.int32)
    return jnp.where(jnp.arange(TOKENS, dtype=jnp.int32) == lone, jnp.int32(CPO - 1), labels)


def shard_levels(rng, extent, cuts, low, largest):
    gain, own = 1.0, jax.random.fold_in(rng, 6)
    for axis_at, shards_of in cuts:
        steps = jnp.exp(jax.random.uniform(jax.random.fold_in(own, axis_at), (shards_of,), jnp.float32, low / len(cuts), largest / len(cuts)))
        gain = gain * jnp.repeat(steps, extent[axis_at] // shards_of).reshape([-1 if axis == axis_at else 1 for axis in range(len(extent))])
    return gain


def deal_out(key, own, number, rows, amount, top, most, skew):
    ranking = jax.random.permutation(key, amount)
    crowded, common = load_shares(amount, rows * top, most, skew, True), load_shares(amount, rows * top, most, skew, False)
    places = jnp.arange(amount)

    def named(tallies, rotation):
        used = int((tallies > 0).sum())
        fixed = max(1, used // 4)
        shifted = fixed + (places - fixed + rotation * (used - fixed)) % max(1, amount - fixed)
        return jnp.zeros((amount,), jnp.int32).at[ranking[jnp.where(places < fixed, places, shifted)]].set(jnp.asarray(tallies, jnp.int32))

    tallies = jnp.where(number % 4 == 0, named(crowded, number // 4), named(common, number - number // 4 - 1))
    mixed = jax.random.permutation(jax.random.fold_in(own, 3), amount)
    giver, sink = mixed[0:amount // 2 * 2:2], mixed[1:amount // 2 * 2:2]
    margin = jnp.minimum(tallies[giver] - 1, most - tallies[sink]) // 2
    margin = jnp.where((giver == ranking[0]) | (sink == ranking[0]) | (tallies[sink] == 0), 0, jnp.maximum(margin, 0))
    shifted = jax.random.randint(jax.random.fold_in(own, 4), (amount // 2,), 0, 1 << 20) % (margin + 1)
    tallies = tallies.at[giver].add(-shifted).at[sink].add(shifted)
    members = jnp.searchsorted(jnp.cumsum(tallies), jnp.arange(rows * top), side="right").astype(jnp.int32)
    listing = members.reshape(top, rows).T
    listing = listing[jax.random.permutation(jax.random.fold_in(own, 1), rows)]
    rotation = jax.random.randint(jax.random.fold_in(own, 2), (rows, 1), 0, top)
    return jnp.take_along_axis(listing, (jnp.arange(top)[None, :] + rotation) % top, axis=1)


def load_shares(count, total, limit, slope, full):
    loads = [(1 << 20) // math.isqrt(standing ** slope) + 1 for standing in range(1, count + 1)]
    largest = limit if full else min(limit, max(-(-total // count), total * loads[0] // sum(loads)))
    least = 1 if total - largest >= count - 1 else 0
    counts, surplus = [largest] + [least] * (count - 1), total - largest - least * (count - 1)
    while surplus > 0:
        free = [i for i in range(1, count) if counts[i] < largest] or [i for i in range(1, count) if counts[i] < limit]
        whole, left = sum([loads[i] for i in free]), surplus
        for i in free:
            more = min(limit - counts[i], max(1, left * loads[i] // whole), surplus)
            counts[i] = counts[i] + more
            surplus = surplus - more
    return np.array(counts)


def noise(key, extent, spread, most, cuts=(), kind=jnp.bfloat16):
    factor_of = shard_levels(key, extent, cuts, -0.22, 0.18) if cuts else 1.0
    drawn = jax.random.normal(key, extent, jnp.float32) * spread * factor_of
    return jnp.minimum(jnp.maximum(drawn, -most), most).astype(kind)


def setup_inputs(seed: int = 0, part: int = 0) -> dict:
    keys = jax.random.split(jax.random.key(seed), 5)
    part_splits = jax.random.split(jax.random.fold_in(keys[4], part), 5)
    embeddings = noise(part_splits[0], (TOKENS, DIN), 1.0, 6.0, ((0, 16),))
    basis = noise(keys[1], (DIN, F), DIN ** -0.5, 0.09375)
    owner_ids_keys = jax.random.split(jax.random.fold_in(part_splits[2], 1), TOKENS // ROWS_DEV)
    owner_ids_turns = jax.random.permutation(jax.random.fold_in(part_splits[2], 3), TOKENS // ROWS_DEV)
    owner_ids = jax.vmap(lambda own, number: deal_out(jax.random.fold_in(part_splits[2], 2), own, number, ROWS_DEV, N_OWNERS, 1, CAP, 2))(owner_ids_keys, owner_ids_turns).reshape((TOKENS, 1))
    sub_cluster = draw_sub_cluster(jax.random.fold_in(jax.random.fold_in(keys[4], part), 71), part)
    return dict(embeddings=embeddings, basis=basis, owner_ids=owner_ids, sub_cluster=sub_cluster)


def reference(embeddings, basis, owner_ids, sub_cluster):
    owner_flat = owner_ids[:, 0]
    projected = jnp.dot(embeddings.astype(jnp.float32), basis.astype(jnp.float32), precision=lax.Precision.HIGHEST)
    unit_rows = (projected * lax.rsqrt(lax.optimization_barrier(jnp.sum(projected * projected, axis=1, keepdims=True)) + 1e-06)).astype(jnp.bfloat16)
    cluster = owner_flat * CPO + sub_cluster
    device_count = N_OWNERS * N_SPLIT
    owner_grid = owner_flat.reshape(device_count, ROWS_DEV)
    matches = (owner_grid[:, :, None] == jnp.arange(N_OWNERS, dtype=jnp.int32)[None, None, :]).astype(jnp.int32)
    counted = jnp.cumsum(matches, axis=1)
    places = (lax.optimization_barrier(jnp.sum(counted * matches, axis=2)) - 1).reshape(-1)
    device_index = jnp.arange(TOKENS, dtype=jnp.int32) // ROWS_DEV
    slot_index = device_index * CAP + places
    buckets = jnp.zeros((N_OWNERS, device_count * CAP, F), jnp.bfloat16).at[owner_flat, slot_index].set(unit_rows)
    labels = jnp.full((N_OWNERS, device_count * CAP), -1, jnp.int32).at[owner_flat, slot_index].set(cluster)

    def per_owner(pair):
        bucket_rows, bucket_labels = pair
        float_rows = bucket_rows.astype(jnp.float32)
        scores = jnp.dot(float_rows, float_rows.T, precision=lax.Precision.HIGHEST)
        count = bucket_labels.shape[0]
        others = jnp.arange(count, dtype=jnp.int32)
        same_cluster = (bucket_labels[:, None] == bucket_labels[None, :]) & (bucket_labels[None, :] >= 0) & (others[:, None] != others[None, :])
        return jnp.maximum(jnp.float32(-1.0), lax.optimization_barrier(jnp.max(jnp.where(same_cluster, scores, jnp.float32(-2.0)), axis=1)))
    scored = lax.map(per_owner, (buckets, labels))
    return scored[owner_flat, slot_index]
```

```python
import functools

import jax
import jax.numpy as jnp
from jax import lax
from jax.experimental import pallas as pl
from jax.experimental.pallas import tpu as pltpu
from jax.sharding import PartitionSpec as P

CPO = 8
LANES = 128
TAG_ROWS = 16
ABSENT = -2.0
VMEM_LIMIT = 48 * 1024 * 1024


def project_kernel(source_ref, basis_ref, owner_ref, sub_ref, packed_ref, total_ref):
    step = pl.program_id(0)
    row_count = total_ref.shape[0]
    part = jnp.dot(source_ref[...], basis_ref[...], preferred_element_type=jnp.float32)

    @pl.when(step == 0)
    def _():
        total_ref[...] = part

    @pl.when(step > 0)
    def _():
        total_ref[...] += part

    @pl.when(step == pl.num_programs(0) - 1)
    def _():
        projected = total_ref[...]
        norms = jnp.sum(projected * projected, axis=1, keepdims=True)
        packed_ref[:row_count, :] = (projected * lax.rsqrt(norms + 1e-06)).astype(jnp.bfloat16)
        tags = (owner_ref[...] * CPO + sub_ref[...] + 1).astype(jnp.float32)
        width = packed_ref.shape[1]
        tags = jnp.concatenate(
            [tags, jnp.zeros((TAG_ROWS - tags.shape[0], LANES), jnp.float32)], axis=0
        )
        tags = jnp.concatenate(
            [tags, jnp.zeros((TAG_ROWS, width - LANES), jnp.float32)], axis=1
        )
        packed_ref[row_count:, :] = tags.astype(jnp.bfloat16)


def project(embeddings, basis, owner_ids, sub_cluster):
    row_count, depth = embeddings.shape
    width = basis.shape[1]
    step_depth = 512
    tag_shape = (row_count // LANES, LANES)
    return pl.pallas_call(
        project_kernel,
        grid=(depth // step_depth,),
        in_specs=[
            pl.BlockSpec((row_count, step_depth), lambda k: (0, k)),
            pl.BlockSpec((step_depth, width), lambda k: (k, 0)),
            pl.BlockSpec(tag_shape, lambda k: (0, 0)),
            pl.BlockSpec(tag_shape, lambda k: (0, 0)),
        ],
        out_specs=pl.BlockSpec((row_count + TAG_ROWS, width), lambda k: (0, 0)),
        out_shape=jax.ShapeDtypeStruct((row_count + TAG_ROWS, width), jnp.bfloat16),
        scratch_shapes=[pltpu.VMEM((row_count, width), jnp.float32)],
        compiler_params=pltpu.CompilerParams(vmem_limit_bytes=VMEM_LIMIT),
        cost_estimate=pl.CostEstimate(
            flops=2 * row_count * depth * width,
            bytes_accessed=2 * depth * (row_count + width),
            transcendentals=0,
        ),
    )(embeddings, basis, owner_ids.reshape(tag_shape), sub_cluster.reshape(tag_shape))


def score_kernel(row_blocks, own_first, want_rows, *refs):
    key_ref, row_refs = refs[0], refs[1 : 1 + row_blocks]
    col_out = refs[1 + row_blocks]
    row_out = refs[2 + row_blocks] if want_rows else None
    row_count = key_ref.shape[0] - TAG_ROWS
    tiles = row_count // LANES
    keys = key_ref[:row_count, :]
    key_tags = key_ref[row_count:, :LANES].astype(jnp.float32)
    best = [jnp.full((8, LANES), ABSENT, jnp.float32) for _ in range(tiles)]
    for block, row_ref in enumerate(row_refs):
        row_tags = row_ref[row_count:, :LANES].astype(jnp.float32)
        for tile in range(tiles):
            scores = lax.dot_general(
                row_ref[tile * LANES : (tile + 1) * LANES, :],
                keys,
                (((1,), (1,)), ((), ())),
                preferred_element_type=jnp.float32,
            )
            tags = jnp.broadcast_to(row_tags[tile : tile + 1, :], (LANES, LANES)).T
            across = None
            for at in range(tiles):
                same = tags == jnp.broadcast_to(key_tags[at : at + 1, :], (LANES, LANES))
                if own_first and block == 0 and at == tile:
                    same = same & (
                        lax.broadcasted_iota(jnp.int32, (LANES, LANES), 0)
                        != lax.broadcasted_iota(jnp.int32, (LANES, LANES), 1)
                    )
                kept = jnp.where(same, scores[:, at * LANES : (at + 1) * LANES], ABSENT)
                best[at] = jnp.maximum(
                    best[at], jnp.max(kept.reshape(LANES // 8, 8, LANES), axis=0)
                )
                if want_rows:
                    across = kept if across is None else jnp.maximum(across, kept)
            if want_rows:
                at = block * tiles + tile
                row_out[at : at + 1, :] = jnp.max(across.T, axis=0, keepdims=True)
    for at in range(tiles):
        col_out[at : at + 1, :] = jnp.max(best[at], axis=0, keepdims=True)


def score(keys, rows, own_first, want_rows):
    row_count, width = keys.shape[0] - TAG_ROWS, keys.shape[1]
    tiles = row_count // LANES
    out_shape = [jax.ShapeDtypeStruct((tiles, LANES), jnp.float32)]
    if want_rows:
        out_shape.append(jax.ShapeDtypeStruct((tiles * len(rows), LANES), jnp.float32))
    whole = pl.BlockSpec(memory_space=pltpu.VMEM)
    return pl.pallas_call(
        functools.partial(score_kernel, len(rows), own_first, want_rows),
        in_specs=[whole] * (1 + len(rows)),
        out_specs=[whole] * len(out_shape),
        out_shape=out_shape,
        compiler_params=pltpu.CompilerParams(vmem_limit_bytes=VMEM_LIMIT),
        cost_estimate=pl.CostEstimate(
            flops=2 * row_count * row_count * width * len(rows),
            bytes_accessed=2 * row_count * width * (1 + len(rows)),
            transcendentals=0,
        ),
    )(keys, *rows)


def owner_steps(count):
    steps = [[(i, (i + k) % count) for i in range(count)] for k in range(1, (count + 1) // 2)]
    if count % 2 == 0 and count > 1:
        half = count // 2
        steps.append([(i, i + half) if i % 2 == 0 else (i + half, i) for i in range(half)])
    return steps


def per_device(embeddings, basis, owner_ids, sub_cluster):
    row_count = embeddings.shape[0]
    tiles = row_count // LANES
    split_count, owner_count = lax.axis_size("split"), lax.axis_size("owners")
    steps = owner_steps(owner_count)

    def swap(block, offset):
        return lax.ppermute(block, "split", [(s, s ^ offset) for s in range(split_count)])

    own = project(embeddings, basis, owner_ids, sub_cluster)
    arrived = [lax.ppermute(own, "owners", step) for step in steps]
    rows = [own, swap(own, 1)]
    for offset in range(2, split_count, 2):
        beside = swap(own, offset)
        rows += [beside, swap(beside, 1)]
    best = score(own, rows, True, False)[0]
    across = None
    for block, step in zip(arrived, steps):
        col_best, row_best = score(block, rows, False, True)
        across = row_best if across is None else jnp.maximum(across, row_best)
        back = lax.ppermute(col_best, "owners", [(b, a) for a, b in step])
        if len(step) < owner_count:
            sent = functools.reduce(
                jnp.logical_or, [lax.axis_index("owners") == a for a, _ in step]
            )
            back = jnp.where(sent, back, ABSENT)
        best = jnp.maximum(best, back)
    parts = across.reshape(split_count, tiles, LANES)
    best = jnp.maximum(best, parts[0])
    for offset in range(1, split_count):
        best = jnp.maximum(best, swap(parts[offset], offset))
    return jnp.maximum(best, -1.0).reshape(row_count)


def solution(mesh):
    placed = (
        P(("groups", "owners", "split"), None),
        P(),
        P(("groups", "owners", "split"), None),
        P(("groups", "owners", "split")),
    )
    return jax.shard_map(
        per_device,
        mesh=mesh,
        in_specs=placed,
        out_specs=P(("groups", "owners", "split")),
        check_vma=False,
    )
```

```python
import functools

import jax
import jax.numpy as jnp
from jax import lax
from jax.experimental import pallas as pl
from jax.experimental.pallas import tpu as pltpu
from jax.sharding import PartitionSpec as P

CPO = 8
LANES = 128
TAG_ROWS = 16
ABSENT = -2.0
STEPS = 8
PIECES = 1
VMEM_LIMIT = 48 * 1024 * 1024


def project_kernel(source_hbm, basis_hbm, owner_hbm, sub_hbm, *refs):
    packed_refs, (source, basis, owner, sub, sems, tag_sems) = refs[:-6], refs[-6:]
    row_count, depth = source.shape
    width = basis.shape[1]
    chunk = depth // STEPS
    tag_copies = [
        pltpu.make_async_copy(owner_hbm, owner, tag_sems.at[0]),
        pltpu.make_async_copy(sub_hbm, sub, tag_sems.at[1]),
    ]
    copies = []
    for step in range(STEPS):
        span = pl.ds(step * chunk, chunk)
        copies.append(
            (
                pltpu.make_async_copy(
                    basis_hbm.at[span, :], basis.at[span, :], sems.at[0, step]
                ),
                pltpu.make_async_copy(
                    source_hbm.at[:, span], source.at[:, span], sems.at[1, step]
                ),
            )
        )
    for pair in copies:
        for copy in pair:
            copy.start()
    for copy in tag_copies:
        copy.start()
    projected = None
    for step, pair in enumerate(copies):
        for copy in pair:
            copy.wait()
        part = jnp.dot(
            source[:, step * chunk : (step + 1) * chunk],
            basis[step * chunk : (step + 1) * chunk, :],
            preferred_element_type=jnp.float32,
        )
        projected = part if projected is None else projected + part
    for copy in tag_copies:
        copy.wait()
    norms = jnp.sum(projected * projected, axis=1, keepdims=True)
    units = (projected * lax.rsqrt(norms + 1e-06)).astype(jnp.bfloat16)
    tags = (owner[...] * CPO + sub[...] + 1).astype(jnp.float32)
    for packed_ref in packed_refs:
        rows = packed_ref.shape[0] - TAG_ROWS
        at = 0 if rows == row_count else packed_refs[1:].index(packed_ref) * rows
        here = tags[at // LANES : (at + rows) // LANES, :]
        here = jnp.concatenate(
            [here, jnp.zeros((TAG_ROWS - here.shape[0], LANES), jnp.float32)], axis=0
        )
        here = jnp.concatenate([here, jnp.zeros((TAG_ROWS, width - LANES), jnp.float32)], axis=1)
        packed_ref[:rows, :] = units[at : at + rows, :]
        packed_ref[rows:, :] = here.astype(jnp.bfloat16)


def project(embeddings, basis, owner_ids, sub_cluster):
    row_count, depth = embeddings.shape
    width = basis.shape[1]
    tag_shape = (row_count // LANES, LANES)
    sizes = [row_count] + ([row_count // PIECES] * PIECES if PIECES > 1 else [])
    return pl.pallas_call(
        project_kernel,
        in_specs=[pl.BlockSpec(memory_space=pltpu.HBM)] * 4,
        out_specs=[pl.BlockSpec(memory_space=pltpu.VMEM)] * len(sizes),
        out_shape=[
            jax.ShapeDtypeStruct((size + TAG_ROWS, width), jnp.bfloat16) for size in sizes
        ],
        scratch_shapes=[
            pltpu.VMEM((row_count, depth), jnp.bfloat16),
            pltpu.VMEM((depth, width), jnp.bfloat16),
            pltpu.VMEM(tag_shape, jnp.int32),
            pltpu.VMEM(tag_shape, jnp.int32),
            pltpu.SemaphoreType.DMA((2, STEPS)),
            pltpu.SemaphoreType.DMA((2,)),
        ],
        compiler_params=pltpu.CompilerParams(vmem_limit_bytes=VMEM_LIMIT),
        cost_estimate=pl.CostEstimate(
            flops=2 * row_count * depth * width,
            bytes_accessed=2 * depth * (row_count + width),
            transcendentals=0,
        ),
    )(
        *[
            pltpu.with_memory_space_constraint(array, pltpu.HBM)
            for array in (
                embeddings,
                basis,
                owner_ids.reshape(tag_shape),
                sub_cluster.reshape(tag_shape),
            )
        ]
    )


def score_kernel(key_blocks, row_blocks, own_first, want_rows, *refs):
    refs = list(refs)
    key_refs = [refs.pop(0) for _ in range(key_blocks)]
    row_refs = [refs.pop(0) for _ in range(row_blocks)]
    base_ref = None if own_first else refs.pop(0)
    col_refs = [refs.pop(0) for _ in range(key_blocks)]
    key_count, row_count = key_refs[0].shape[0] - TAG_ROWS, row_refs[0].shape[0] - TAG_ROWS
    key_tiles, row_tiles = key_count // LANES, row_count // LANES
    best = [jnp.full((8, LANES), ABSENT, jnp.float32) for _ in range(key_tiles * key_blocks)]
    for block, row_ref in enumerate(row_refs):
        row_tags = row_ref[row_count:, :LANES].astype(jnp.float32)
        across = [None] * row_tiles
        tags = [
            jnp.broadcast_to(row_tags[tile : tile + 1, :], (LANES, LANES)).T
            for tile in range(row_tiles)
        ]
        for key_block, key_ref in enumerate(key_refs):
            key_tags = key_ref[key_count:, :LANES].astype(jnp.float32)
            scores = lax.dot_general(
                row_ref[:row_count, :],
                key_ref[:key_count, :],
                (((1,), (1,)), ((), ())),
                preferred_element_type=jnp.float32,
            )
            for tile in range(row_tiles):
                for at in range(key_tiles):
                    same = tags[tile] == key_tags[at : at + 1, :]
                    if own_first and block == 0 and at == tile:
                        same = same & (
                            lax.broadcasted_iota(jnp.int32, (LANES, LANES), 0)
                            != lax.broadcasted_iota(jnp.int32, (LANES, LANES), 1)
                        )
                    kept = scores[
                        tile * LANES : (tile + 1) * LANES, at * LANES : (at + 1) * LANES
                    ]
                    kept = jnp.where(same, kept, ABSENT)
                    to = key_block * key_tiles + at
                    best[to] = jnp.maximum(
                        best[to], jnp.max(kept.reshape(LANES // 8, 8, LANES), axis=0)
                    )
                    if want_rows:
                        across[tile] = (
                            kept if across[tile] is None else jnp.maximum(across[tile], kept)
                        )
        if want_rows:
            row_out = refs[block // 2]
            for tile in range(row_tiles):
                at = block % 2 * row_tiles + tile
                found = jnp.max(across[tile].T, axis=0, keepdims=True)
                if block == 0:
                    found = jnp.maximum(found, base_ref[tile : tile + 1, :])
                row_out[at : at + 1, :] = found
    for key_block, col_out in enumerate(col_refs):
        for at in range(key_tiles):
            found = jnp.max(best[key_block * key_tiles + at], axis=0, keepdims=True)
            if not own_first and not want_rows:
                found = jnp.maximum(found, base_ref[at : at + 1, :])
            col_out[at : at + 1, :] = found


def score(keys, rows, base, want_rows):
    key_count, row_count = keys[0].shape[0] - TAG_ROWS, rows[0].shape[0] - TAG_ROWS
    out_shape = [jax.ShapeDtypeStruct((key_count // LANES, LANES), jnp.float32)] * len(keys)
    if want_rows:
        out_shape += [
            jax.ShapeDtypeStruct((2 * row_count // LANES, LANES), jnp.float32)
        ] * (len(rows) // 2)
    operands = [*keys, *rows] + ([] if base is None else [base])
    whole = pl.BlockSpec(memory_space=pltpu.VMEM)
    return pl.pallas_call(
        functools.partial(score_kernel, len(keys), len(rows), base is None, want_rows),
        in_specs=[whole] * len(operands),
        out_specs=[whole] * len(out_shape),
        out_shape=out_shape,
        compiler_params=pltpu.CompilerParams(vmem_limit_bytes=VMEM_LIMIT),
        cost_estimate=pl.CostEstimate(flops=0, bytes_accessed=0, transcendentals=0),
    )(*operands)


def owner_steps(count):
    steps = [[(i, (i + k) % count) for i in range(count)] for k in range(1, (count + 1) // 2)]
    if count % 2 == 0 and count > 1:
        half = count // 2
        steps.append([(i, i + half) if i % 2 == 0 else (i + half, i) for i in range(half)])
    return steps


def per_device(embeddings, basis, owner_ids, sub_cluster):
    row_count = embeddings.shape[0]
    tiles = row_count // LANES
    split_count, owner_count = lax.axis_size("split"), lax.axis_size("owners")
    steps = owner_steps(owner_count)

    def swap(block, offset):
        return lax.ppermute(block, "split", [(s, s ^ offset) for s in range(split_count)])

    own, *pieces = project(embeddings, basis, owner_ids, sub_cluster)
    pieces = pieces or [own]
    arrived = [
        [lax.ppermute(piece, "owners", step) for piece in pieces] for step in reversed(steps)
    ]
    rows = [own, swap(own, 1)]
    best = score([own], rows, None, False)[0]
    for offset in range(2, split_count, 2):
        beside = swap(own, offset)
        pair = [beside, swap(own, offset + 1)]
        best = score([own], pair, best, False)[0]
        rows += pair
    keys = [block for blocks in arrived for block in blocks]
    found = score(keys, rows, best, True)
    col_best, row_best = found[: len(keys)], found[len(keys) :]
    local = row_best[0]
    for at in range(1, split_count // 2):
        local = jnp.maximum(local, swap(row_best[at], 2 * at))
    best, beside = local[:tiles], local[tiles:]
    best = jnp.maximum(best, swap(beside, 1))
    for at, step in enumerate(reversed(steps)):
        back = lax.ppermute(col_best[at], "owners", [(b, a) for a, b in step])
        if len(step) < owner_count:
            sent = functools.reduce(
                jnp.logical_or, [lax.axis_index("owners") == a for a, _ in step]
            )
            back = jnp.where(sent, back, ABSENT)
        best = jnp.maximum(best, back)
    return jnp.maximum(best, -1.0).reshape(row_count)


def solution(mesh):
    placed = (
        P(("groups", "owners", "split"), None),
        P(),
        P(("groups", "owners", "split"), None),
        P(("groups", "owners", "split")),
    )
    return jax.shard_map(
        per_device,
        mesh=mesh,
        in_specs=placed,
        out_specs=P(("groups", "owners", "split")),
        check_vma=False,
    )
```

```python
import functools

import jax
import jax.numpy as jnp
from jax import lax
from jax.experimental import pallas as pl
from jax.experimental.pallas import tpu as pltpu
from jax.sharding import PartitionSpec as P

CPO = 8
LANES = 128
TAG_ROWS = 16
ABSENT = -2.0
STEPS = 8
PIECES = 2
WEIGHT = 32
VMEM_LIMIT = 48 * 1024 * 1024


def project_kernel(source_hbm, basis_hbm, owner_hbm, sub_hbm, *refs):
    packed_refs, (source, basis, owner, sub, sems, tag_sems) = refs[:-6], refs[-6:]
    row_count, depth = source.shape
    width = basis.shape[1]
    chunk = depth // STEPS
    tag_copies = [
        pltpu.make_async_copy(owner_hbm, owner, tag_sems.at[0]),
        pltpu.make_async_copy(sub_hbm, sub, tag_sems.at[1]),
    ]
    copies = []
    for step in range(STEPS):
        span = pl.ds(step * chunk, chunk)
        copies.append(
            (
                pltpu.make_async_copy(
                    basis_hbm.at[span, :], basis.at[span, :], sems.at[0, step]
                ),
                pltpu.make_async_copy(
                    source_hbm.at[:, span], source.at[:, span], sems.at[1, step]
                ),
            )
        )
    for pair in copies:
        for copy in pair:
            copy.start()
    for copy in tag_copies:
        copy.start()
    projected = None
    for step, pair in enumerate(copies):
        for copy in pair:
            copy.wait()
        part = jnp.dot(
            source[:, step * chunk : (step + 1) * chunk],
            basis[step * chunk : (step + 1) * chunk, :],
            preferred_element_type=jnp.float32,
        )
        projected = part if projected is None else projected + part
    for copy in tag_copies:
        copy.wait()
    norms = jnp.sum(projected * projected, axis=1, keepdims=True)
    units = (projected * lax.rsqrt(norms + 1e-06)).astype(jnp.bfloat16)
    tags = (owner[...] * CPO + sub[...] + 1).astype(jnp.float32)
    for place, packed_ref in enumerate(packed_refs):
        rows = packed_ref.shape[0] - TAG_ROWS
        at = max(place - 1, 0) * rows
        here = tags[at // LANES : (at + rows) // LANES, :]
        here = jnp.concatenate(
            [here, jnp.zeros((TAG_ROWS - here.shape[0], LANES), jnp.float32)], axis=0
        )
        here = jnp.concatenate([here, jnp.zeros((TAG_ROWS, width - LANES), jnp.float32)], axis=1)
        packed_ref[:rows, :] = units[at : at + rows, :]
        packed_ref[rows:, :] = here.astype(jnp.bfloat16)


def project(embeddings, basis, owner_ids, sub_cluster):
    row_count, depth = embeddings.shape
    width = basis.shape[1]
    tag_shape = (row_count // LANES, LANES)
    sizes = [row_count] + [row_count // PIECES] * PIECES
    return pl.pallas_call(
        project_kernel,
        in_specs=[pl.BlockSpec(memory_space=pltpu.HBM)] * 4,
        out_specs=[pl.BlockSpec(memory_space=pltpu.VMEM)] * len(sizes),
        out_shape=[
            jax.ShapeDtypeStruct((size + TAG_ROWS, width), jnp.bfloat16) for size in sizes
        ],
        scratch_shapes=[
            pltpu.VMEM((row_count, depth), jnp.bfloat16),
            pltpu.VMEM((depth, width), jnp.bfloat16),
            pltpu.VMEM(tag_shape, jnp.int32),
            pltpu.VMEM(tag_shape, jnp.int32),
            pltpu.SemaphoreType.DMA((2, STEPS)),
            pltpu.SemaphoreType.DMA((2,)),
        ],
        compiler_params=pltpu.CompilerParams(vmem_limit_bytes=VMEM_LIMIT),
        cost_estimate=pl.CostEstimate(
            flops=2 * row_count * depth * width,
            bytes_accessed=2 * depth * (row_count + width),
            transcendentals=0,
        ),
    )(
        *[
            pltpu.with_memory_space_constraint(array, pltpu.HBM)
            for array in (
                embeddings,
                basis,
                owner_ids.reshape(tag_shape),
                sub_cluster.reshape(tag_shape),
            )
        ]
    )


def score_kernel(key_blocks, row_blocks, with_base, own_first, pass_on, *refs):
    refs = list(refs)
    if pass_on:
        refs.pop()[...] = refs[0][...]
    key_refs = [refs.pop(0) for _ in range(key_blocks)]
    row_refs = [refs.pop(0) for _ in range(row_blocks)]
    base_refs = [refs.pop(0) if given else None for given in with_base]
    col_refs = [refs.pop(0) for _ in range(key_blocks)]
    row_outs = refs
    key_count, row_count = key_refs[0].shape[0] - TAG_ROWS, row_refs[0].shape[0] - TAG_ROWS
    key_tiles, row_tiles = key_count // LANES, row_count // LANES
    best = [jnp.full((8, LANES), ABSENT, jnp.float32) for _ in range(key_tiles * key_blocks)]
    for block, row_ref in enumerate(row_refs):
        row_tags = row_ref[row_count:, :LANES].astype(jnp.float32)
        across = [None] * row_tiles
        tags = [
            jnp.broadcast_to(row_tags[tile : tile + 1, :], (LANES, LANES)).T
            for tile in range(row_tiles)
        ]
        for key_block, key_ref in enumerate(key_refs):
            key_tags = key_ref[key_count:, :LANES].astype(jnp.float32)
            scores = lax.dot_general(
                row_ref[:row_count, :],
                key_ref[:key_count, :],
                (((1,), (1,)), ((), ())),
                preferred_element_type=jnp.float32,
            )
            for tile in range(row_tiles):
                for at in range(key_tiles):
                    same = tags[tile] == key_tags[at : at + 1, :]
                    if own_first and block == 0 and at == tile:
                        same = same & (
                            lax.broadcasted_iota(jnp.int32, (LANES, LANES), 0)
                            != lax.broadcasted_iota(jnp.int32, (LANES, LANES), 1)
                        )
                    kept = scores[
                        tile * LANES : (tile + 1) * LANES, at * LANES : (at + 1) * LANES
                    ]
                    kept = jnp.where(same, kept, ABSENT)
                    to = key_block * key_tiles + at
                    best[to] = jnp.maximum(
                        best[to], jnp.max(kept.reshape(LANES // 8, 8, LANES), axis=0)
                    )
                    if row_outs:
                        across[tile] = (
                            kept if across[tile] is None else jnp.maximum(across[tile], kept)
                        )
        if row_outs:
            for tile in range(row_tiles):
                found = jnp.max(across[tile].T, axis=0, keepdims=True)
                if base_refs[block] is not None:
                    found = jnp.maximum(found, base_refs[block][tile : tile + 1, :])
                row_outs[block][tile : tile + 1, :] = found
    for key_block, col_out in enumerate(col_refs):
        for at in range(key_tiles):
            col_out[at : at + 1, :] = jnp.max(best[key_block * key_tiles + at], axis=0, keepdims=True)


def score(keys, rows, bases=None, own_first=False, pass_on=False):
    key_count, row_count = keys[0].shape[0] - TAG_ROWS, rows[0].shape[0] - TAG_ROWS
    out_shape = [jax.ShapeDtypeStruct((key_count // LANES, LANES), jnp.float32)] * len(keys)
    if bases is not None:
        out_shape += [jax.ShapeDtypeStruct((row_count // LANES, LANES), jnp.float32)] * len(rows)
    if pass_on:
        out_shape.append(jax.ShapeDtypeStruct(keys[0].shape, keys[0].dtype))
    given = [base for base in bases or [] if base is not None]
    operands = [*keys, *rows, *given]
    whole = pl.BlockSpec(memory_space=pltpu.VMEM)
    found = pl.pallas_call(
        functools.partial(
            score_kernel,
            len(keys),
            len(rows),
            tuple(base is not None for base in bases or []),
            own_first,
            pass_on,
        ),
        in_specs=[whole] * len(operands),
        out_specs=[whole] * len(out_shape),
        out_shape=out_shape,
        compiler_params=pltpu.CompilerParams(vmem_limit_bytes=VMEM_LIMIT),
        cost_estimate=pl.CostEstimate(
            flops=WEIGHT * len(keys) * len(rows) * key_count * row_count * keys[0].shape[1],
            bytes_accessed=0,
            transcendentals=0,
        ),
    )(*operands)
    return found[: len(keys)], list(found[len(keys) :])


def receivers(step, count):
    if 2 * step == count:
        return range(count // 4, count // 4 + count // 2)
    return range(count)


def per_device(embeddings, basis, owner_ids, sub_cluster):
    row_count = embeddings.shape[0]
    split_count, owner_count = lax.axis_size("split"), lax.axis_size("owners")
    steps = range(1, owner_count // 2 + 1)

    def swap(block, offset):
        return lax.ppermute(block, "split", [(s, s ^ offset) for s in range(split_count)])

    own, *moving = project(embeddings, basis, owner_ids, sub_cluster)
    arrived = []
    for step in steps:
        pairs = [((z - 1) % owner_count, z) for z in receivers(step, owner_count)]
        moving = [lax.ppermute(piece, "owners", pairs) for piece in moving]
        arrived.append([(piece, swap(piece, 1)) for piece in moving])
    arrived[-1][-1] = (moving[-1], None)
    core = swap(own, 1)
    rows = [own] + [swap(own, offset) for offset in range(2, split_count, 2)]
    (best,), _ = score([own], rows, own_first=True)
    _, bases = score([core], rows, [best] + [None] * (len(rows) - 1))
    backs = []
    for step, pieces in zip(steps, arrived):
        direct, beside = [], []
        for at, (piece, other) in enumerate(pieces):
            if backs and at == len(pieces) - 1:
                bases = [jnp.maximum(bases[0], backs.pop()), *bases[1:]]
            (found,), bases = score([piece], rows, bases, pass_on=other is None)
            direct.append(found)
            if other is None:
                other = swap(bases.pop(), 1)
            (found,), bases = score([other], rows, bases)
            beside.append(found)
        found = jnp.maximum(jnp.concatenate(direct), swap(jnp.concatenate(beside), 1))
        targets = receivers(step, owner_count)
        back = lax.ppermute(
            found, "owners", [(z, (z - step) % owner_count) for z in targets]
        )
        if len(targets) < owner_count:
            here = lax.axis_index("owners")
            back = jnp.where((here < targets[0]) | (here > targets[-1]), back, ABSENT)
        backs.append(back)
    best = bases[0]
    for offset, found in zip(range(2, split_count, 2), bases[1:]):
        best = jnp.maximum(best, swap(found, offset))
    for back in backs:
        best = jnp.maximum(best, back)
    return jnp.maximum(best, -1.0).reshape(row_count)


def solution(mesh):
    placed = (
        P(("groups", "owners", "split"), None),
        P(),
        P(("groups", "owners", "split"), None),
        P(("groups", "owners", "split")),
    )
    return jax.shard_map(
        per_device,
        mesh=mesh,
        in_specs=placed,
        out_specs=P(("groups", "owners", "split")),
        check_vma=False,
    )
```

```python
import functools

import jax
import jax.numpy as jnp
from jax import lax
from jax.experimental import pallas as pl
from jax.experimental.pallas import tpu as pltpu
from jax.sharding import PartitionSpec as P

CPO = 8
LANES = 128
TAG_ROWS = 16
ABSENT = -2.0
STEPS = 8
WEIGHT = 0
VMEM_LIMIT = 48 * 1024 * 1024


def project_kernel(source_hbm, basis_hbm, owner_hbm, sub_hbm, *refs):
    packed_refs, (source, basis, owner, sub, sems, tag_sems) = refs[:-6], refs[-6:]
    row_count, depth = source.shape
    width = basis.shape[1]
    chunk = depth // STEPS
    tag_copies = [
        pltpu.make_async_copy(owner_hbm, owner, tag_sems.at[0]),
        pltpu.make_async_copy(sub_hbm, sub, tag_sems.at[1]),
    ]
    copies = []
    for step in range(STEPS):
        span = pl.ds(step * chunk, chunk)
        copies.append(
            (
                pltpu.make_async_copy(
                    basis_hbm.at[span, :], basis.at[span, :], sems.at[0, step]
                ),
                pltpu.make_async_copy(
                    source_hbm.at[:, span], source.at[:, span], sems.at[1, step]
                ),
            )
        )
    for pair in copies:
        for copy in pair:
            copy.start()
    for copy in tag_copies:
        copy.start()
    projected = None
    for step, pair in enumerate(copies):
        for copy in pair:
            copy.wait()
        part = jnp.dot(
            source[:, step * chunk : (step + 1) * chunk],
            basis[step * chunk : (step + 1) * chunk, :],
            preferred_element_type=jnp.float32,
        )
        projected = part if projected is None else projected + part
    for copy in tag_copies:
        copy.wait()
    norms = jnp.sum(projected * projected, axis=1, keepdims=True)
    units = (projected * lax.rsqrt(norms + 1e-06)).astype(jnp.bfloat16)
    tags = (owner[...] * CPO + sub[...] + 1).astype(jnp.float32)
    for place, packed_ref in enumerate(packed_refs):
        rows = packed_ref.shape[0] - TAG_ROWS
        at = max(place - 1, 0) * rows
        here = tags[at // LANES : (at + rows) // LANES, :]
        here = jnp.concatenate(
            [here, jnp.zeros((TAG_ROWS - here.shape[0], LANES), jnp.float32)], axis=0
        )
        here = jnp.concatenate([here, jnp.zeros((TAG_ROWS, width - LANES), jnp.float32)], axis=1)
        packed_ref[:rows, :] = units[at : at + rows, :]
        packed_ref[rows:, :] = here.astype(jnp.bfloat16)


def project(embeddings, basis, owner_ids, sub_cluster):
    row_count, depth = embeddings.shape
    width = basis.shape[1]
    tag_shape = (row_count // LANES, LANES)
    sizes = [row_count]
    return pl.pallas_call(
        project_kernel,
        in_specs=[pl.BlockSpec(memory_space=pltpu.HBM)] * 4,
        out_specs=[pl.BlockSpec(memory_space=pltpu.VMEM)] * len(sizes),
        out_shape=[
            jax.ShapeDtypeStruct((size + TAG_ROWS, width), jnp.bfloat16) for size in sizes
        ],
        scratch_shapes=[
            pltpu.VMEM((row_count, depth), jnp.bfloat16),
            pltpu.VMEM((depth, width), jnp.bfloat16),
            pltpu.VMEM(tag_shape, jnp.int32),
            pltpu.VMEM(tag_shape, jnp.int32),
            pltpu.SemaphoreType.DMA((2, STEPS)),
            pltpu.SemaphoreType.DMA((2,)),
        ],
        compiler_params=pltpu.CompilerParams(vmem_limit_bytes=VMEM_LIMIT),
        cost_estimate=pl.CostEstimate(
            flops=2 * row_count * depth * width,
            bytes_accessed=2 * depth * (row_count + width),
            transcendentals=0,
        ),
    )(
        *[
            pltpu.with_memory_space_constraint(array, pltpu.HBM)
            for array in (
                embeddings,
                basis,
                owner_ids.reshape(tag_shape),
                sub_cluster.reshape(tag_shape),
            )
        ]
    )


def score_kernel(key_blocks, row_blocks, own_first, unread, *refs):
    key_refs, refs = refs[unread : unread + key_blocks], refs[unread + key_blocks :]
    row_refs, refs = refs[:row_blocks], refs[row_blocks:]
    col_refs, row_outs = refs[:key_blocks], refs[key_blocks:]
    key_count, row_count = key_refs[0].shape[0] - TAG_ROWS, row_refs[0].shape[0] - TAG_ROWS
    key_tiles, row_tiles = key_count // LANES, row_count // LANES
    best = [jnp.full((8, LANES), ABSENT, jnp.float32) for _ in range(key_tiles * key_blocks)]
    for block, row_ref in enumerate(row_refs):
        row_tags = row_ref[row_count:, :LANES].astype(jnp.float32)
        across = [None] * row_tiles
        tags = [
            jnp.broadcast_to(row_tags[tile : tile + 1, :], (LANES, LANES)).T
            for tile in range(row_tiles)
        ]
        for key_block, key_ref in enumerate(key_refs):
            key_tags = key_ref[key_count:, :LANES].astype(jnp.float32)
            scores = lax.dot_general(
                row_ref[:row_count, :],
                key_ref[:key_count, :],
                (((1,), (1,)), ((), ())),
                preferred_element_type=jnp.float32,
            )
            for tile in range(row_tiles):
                for at in range(key_tiles):
                    same = tags[tile] == key_tags[at : at + 1, :]
                    if own_first and block == 0 and at == tile:
                        same = same & (
                            lax.broadcasted_iota(jnp.int32, (LANES, LANES), 0)
                            != lax.broadcasted_iota(jnp.int32, (LANES, LANES), 1)
                        )
                    kept = scores[
                        tile * LANES : (tile + 1) * LANES, at * LANES : (at + 1) * LANES
                    ]
                    kept = jnp.where(same, kept, ABSENT)
                    to = key_block * key_tiles + at
                    best[to] = jnp.maximum(
                        best[to], jnp.max(kept.reshape(LANES // 8, 8, LANES), axis=0)
                    )
                    if row_outs:
                        across[tile] = (
                            kept if across[tile] is None else jnp.maximum(across[tile], kept)
                        )
        if row_outs:
            for tile in range(row_tiles):
                at = block % 2 * row_tiles + tile
                row_outs[block // 2][at : at + 1, :] = jnp.max(
                    across[tile].T, axis=0, keepdims=True
                )
    for key_block, col_out in enumerate(col_refs):
        for at in range(key_tiles):
            col_out[at : at + 1, :] = jnp.max(best[key_block * key_tiles + at], axis=0, keepdims=True)


def score(keys, rows, want_rows=True, own_first=False, after=()):
    key_count, row_count = keys[0].shape[0] - TAG_ROWS, rows[0].shape[0] - TAG_ROWS
    out_shape = [jax.ShapeDtypeStruct((key_count // LANES, LANES), jnp.float32)] * len(keys)
    if want_rows:
        pair = jax.ShapeDtypeStruct((2 * row_count // LANES, LANES), jnp.float32)
        out_shape += [pair] * (len(rows) // 2)
    whole = pl.BlockSpec(memory_space=pltpu.VMEM)
    found = pl.pallas_call(
        functools.partial(score_kernel, len(keys), len(rows), own_first, len(after)),
        in_specs=[pl.BlockSpec(memory_space=pl.ANY)] * len(after) + [whole] * (len(keys) + len(rows)),
        out_specs=[whole] * len(out_shape),
        out_shape=out_shape,
        compiler_params=pltpu.CompilerParams(vmem_limit_bytes=VMEM_LIMIT),
        cost_estimate=pl.CostEstimate(
            flops=WEIGHT * len(keys) * len(rows) * key_count * row_count * keys[0].shape[1],
            bytes_accessed=0,
            transcendentals=0,
        ),
    )(*after, *keys, *rows)
    return found[: len(keys)], found[len(keys) :]


def owner_steps(count):
    steps = [[(i, (i + k) % count) for i in range(count)] for k in range(1, (count + 1) // 2)]
    if count % 2 == 0 and count > 1:
        half = count // 2
        steps.append([(i, i + half) if i % 2 == 0 else (i + half, i) for i in range(half)])
    return steps


def per_device(embeddings, basis, owner_ids, sub_cluster):
    row_count = embeddings.shape[0]
    tiles = row_count // LANES
    split_count, owner_count = lax.axis_size("split"), lax.axis_size("owners")
    steps = owner_steps(owner_count)[::-1]

    def swap(block, offset):
        return lax.ppermute(block, "split", [(s, s ^ offset) for s in range(split_count)])

    (own,) = project(embeddings, basis, owner_ids, sub_cluster)
    keys = [lax.ppermute(own, "owners", step) for step in steps]
    rows = [own, swap(own, 1)]
    for offset in range(2, split_count, 2):
        beside = swap(own, offset)
        rows += [beside, swap(beside, 1)]
    col_best, row_best = score(keys, rows)
    local = row_best[0]
    for at in range(1, split_count // 2):
        local = jnp.maximum(local, swap(row_best[at], 2 * at))
    best, beside = local[:tiles], local[tiles:]
    best = jnp.maximum(best, swap(beside, 1))
    for found, step in zip(col_best, steps):
        back = lax.ppermute(found, "owners", [(b, a) for a, b in step])
        if len(step) < owner_count:
            sent = functools.reduce(
                jnp.logical_or, [lax.axis_index("owners") == a for a, _ in step]
            )
            back = jnp.where(sent, back, ABSENT)
        best = jnp.maximum(best, back)
    (alone,), _ = score([own], rows, want_rows=False, own_first=True, after=keys)
    return jnp.maximum(jnp.maximum(best, alone), -1.0).reshape(row_count)


def solution(mesh):
    placed = (
        P(("groups", "owners", "split"), None),
        P(),
        P(("groups", "owners", "split"), None),
        P(("groups", "owners", "split")),
    )
    return jax.shard_map(
        per_device,
        mesh=mesh,
        in_specs=placed,
        out_specs=P(("groups", "owners", "split")),
        check_vma=False,
    )
```

```python
import functools

import jax
import jax.numpy as jnp
from jax import lax
from jax.experimental import pallas as pl
from jax.experimental.pallas import tpu as pltpu
from jax.sharding import PartitionSpec as P

CPO = 8
LANES = 128
TAG_ROWS = 16
ABSENT = -2.0
EIGHTHS = (2, 2, 2, 1, 1)
PARTS = 2
VMEM_LIMIT = 48 * 1024 * 1024


def project_kernel(source_hbm, basis_hbm, owner_hbm, sub_hbm, *refs):
    packed_refs, (source, basis, owner, sub, sems, tag_sems) = refs[:-6], refs[-6:]
    row_count, depth = source.shape
    width = basis.shape[1]
    ends = [depth * sum(EIGHTHS[: step + 1]) // 8 for step in range(len(EIGHTHS))]
    spans = list(zip([0] + ends, ends))
    tag_copies = [
        pltpu.make_async_copy(owner_hbm, owner, tag_sems.at[0]),
        pltpu.make_async_copy(sub_hbm, sub, tag_sems.at[1]),
    ]
    copies = []
    for step, (start, end) in enumerate(spans):
        span = pl.ds(start, end - start)
        copies.append(
            (
                pltpu.make_async_copy(
                    basis_hbm.at[span, :], basis.at[span, :], sems.at[0, step]
                ),
                pltpu.make_async_copy(
                    source_hbm.at[:, span], source.at[:, span], sems.at[1, step]
                ),
            )
        )
    for pair in copies:
        for copy in pair:
            copy.start()
    for copy in tag_copies:
        copy.start()
    projected = None
    for (start, end), pair in zip(spans, copies):
        for copy in pair:
            copy.wait()
        part = jnp.dot(
            source[:, start:end], basis[start:end, :], preferred_element_type=jnp.float32
        )
        projected = part if projected is None else projected + part
    for copy in tag_copies:
        copy.wait()
    norms = jnp.sum(projected * projected, axis=1, keepdims=True)
    units = (projected * lax.rsqrt(norms + 1e-06)).astype(jnp.bfloat16)
    tags = (owner[...] * CPO + sub[...] + 1).astype(jnp.float32)
    for place, packed_ref in enumerate(packed_refs):
        rows = packed_ref.shape[0] - TAG_ROWS
        at = max(place - 1, 0) * rows
        here = tags[at // LANES : (at + rows) // LANES, :]
        here = jnp.concatenate(
            [here, jnp.zeros((TAG_ROWS - here.shape[0], LANES), jnp.float32)], axis=0
        )
        here = jnp.concatenate([here, jnp.zeros((TAG_ROWS, width - LANES), jnp.float32)], axis=1)
        packed_ref[:rows, :] = units[at : at + rows, :]
        packed_ref[rows:, :] = here.astype(jnp.bfloat16)


def project(embeddings, basis, owner_ids, sub_cluster):
    row_count, depth = embeddings.shape
    width = basis.shape[1]
    tag_shape = (row_count // LANES, LANES)
    sizes = [row_count]
    return pl.pallas_call(
        project_kernel,
        in_specs=[pl.BlockSpec(memory_space=pltpu.HBM)] * 4,
        out_specs=[pl.BlockSpec(memory_space=pltpu.VMEM)] * len(sizes),
        out_shape=[
            jax.ShapeDtypeStruct((size + TAG_ROWS, width), jnp.bfloat16) for size in sizes
        ],
        scratch_shapes=[
            pltpu.VMEM((row_count, depth), jnp.bfloat16),
            pltpu.VMEM((depth, width), jnp.bfloat16),
            pltpu.VMEM(tag_shape, jnp.int32),
            pltpu.VMEM(tag_shape, jnp.int32),
            pltpu.SemaphoreType.DMA((2, len(EIGHTHS))),
            pltpu.SemaphoreType.DMA((2,)),
        ],
        compiler_params=pltpu.CompilerParams(vmem_limit_bytes=VMEM_LIMIT),
        cost_estimate=pl.CostEstimate(
            flops=2 * row_count * depth * width,
            bytes_accessed=2 * depth * (row_count + width),
            transcendentals=0,
        ),
    )(
        *[
            pltpu.with_memory_space_constraint(array, pltpu.HBM)
            for array in (
                embeddings,
                basis,
                owner_ids.reshape(tag_shape),
                sub_cluster.reshape(tag_shape),
            )
        ]
    )


def score_kernel(row_parts, own_first, bases, unread, *refs):
    refs = list(refs[unread:])
    key_ref = refs.pop(0)
    row_refs = [[refs.pop(0) for _ in range(parts)] for parts in row_parts]
    base_refs = [refs.pop(0) for _ in range(bases)]
    col_out, row_outs = refs[0], refs[1:]
    row_count = key_ref.shape[0] - TAG_ROWS
    tiles = row_count // LANES
    key_tags = key_ref[row_count:, :LANES].astype(jnp.float32)
    best = [jnp.full((8, LANES), ABSENT, jnp.float32) for _ in range(tiles)]
    for block, part_refs in enumerate(row_refs):
        tag_ref = part_refs[-1]
        row_tags = tag_ref[tag_ref.shape[0] - TAG_ROWS :, :LANES].astype(jnp.float32)
        place = 0
        for part_ref in part_refs:
            count = row_count // len(part_refs)
            scores = lax.dot_general(
                part_ref[:count, :],
                key_ref[:row_count, :],
                (((1,), (1,)), ((), ())),
                preferred_element_type=jnp.float32,
            )
            for start in range(0, count, LANES):
                tags = jnp.broadcast_to(row_tags[place : place + 1, :], (LANES, LANES)).T
                across = None
                for at in range(tiles):
                    same = tags == key_tags[at : at + 1, :]
                    if own_first and block == 0 and at == place:
                        same = same & (
                            lax.broadcasted_iota(jnp.int32, (LANES, LANES), 0)
                            != lax.broadcasted_iota(jnp.int32, (LANES, LANES), 1)
                        )
                    kept = scores[start : start + LANES, at * LANES : (at + 1) * LANES]
                    kept = jnp.where(same, kept, ABSENT)
                    best[at] = jnp.maximum(
                        best[at], jnp.max(kept.reshape(LANES // 8, 8, LANES), axis=0)
                    )
                    if row_outs:
                        across = kept if across is None else jnp.maximum(across, kept)
                if row_outs:
                    at = block % 2 * tiles + place
                    found = jnp.max(across.T, axis=0, keepdims=True)
                    if base_refs:
                        found = jnp.maximum(found, base_refs[block // 2][at : at + 1, :])
                    row_outs[block // 2][at : at + 1, :] = found
                place += 1
    for at in range(tiles):
        found = jnp.max(best[at], axis=0, keepdims=True)
        if own_first:
            for base_ref in base_refs:
                found = jnp.maximum(found, base_ref[at : at + 1, :])
        col_out[at : at + 1, :] = found
    if own_first:
        col_out[tiles:, :] = base_refs[0][tiles:, :]


def score(key, rows, bases, own_first=False, after=()):
    tiles = (key.shape[0] - TAG_ROWS) // LANES
    parts = [row if isinstance(row, tuple) else (row,) for row in rows]
    blocks = [part for row in parts for part in row]
    pair = jax.ShapeDtypeStruct((2 * tiles, LANES), jnp.float32)
    out_shape = [pair]
    if not own_first:
        out_shape = [jax.ShapeDtypeStruct((tiles, LANES), jnp.float32)] + [pair] * (len(rows) // 2)
    whole = pl.BlockSpec(memory_space=pltpu.VMEM)
    found = pl.pallas_call(
        functools.partial(
            score_kernel, [len(row) for row in parts], own_first, len(bases), len(after)
        ),
        in_specs=[pl.BlockSpec(memory_space=pl.ANY)] * len(after)
        + [whole] * (1 + len(blocks) + len(bases)),
        out_specs=[whole] * len(out_shape),
        out_shape=out_shape,
        compiler_params=pltpu.CompilerParams(vmem_limit_bytes=VMEM_LIMIT),
        cost_estimate=pl.CostEstimate(flops=0, bytes_accessed=0, transcendentals=0),
    )(*after, key, *blocks, *bases)
    return found[0], list(found[1:])


def owner_steps(count):
    steps = [[(i, (i + k) % count) for i in range(count)] for k in range(1, (count + 1) // 2)]
    if count % 2 == 0 and count > 1:
        half = count // 2
        steps.append([(i, i + half) if i % 2 == 0 else (i + half, i) for i in range(half)])
    return steps


def per_device(embeddings, basis, owner_ids, sub_cluster):
    row_count = embeddings.shape[0]
    tiles = row_count // LANES
    split_count, owner_count = lax.axis_size("split"), lax.axis_size("owners")
    steps = owner_steps(owner_count)[::-1]

    def swap(block, offset):
        return lax.ppermute(block, "split", [(s, s ^ offset) for s in range(split_count)])

    (own,) = project(embeddings, basis, owner_ids, sub_cluster)
    rows = [own, swap(own, 1)]
    for offset in range(2, split_count, 2):
        beside = swap(own, offset)
        part = row_count // PARTS
        starts = [part * at for at in range(PARTS)]
        ends = starts[1:] + [row_count + TAG_ROWS]
        rows += [beside, tuple(swap(beside[a:b], 1) for a, b in zip(starts, ends))]
    keys = [lax.ppermute(own, "owners", step) for step in steps]
    row_best, backs = [], []
    for block, step in zip(keys, steps):
        found, row_best = score(block, rows, row_best)
        back = lax.ppermute(found, "owners", [(b, a) for a, b in step])
        if len(step) < owner_count:
            sent = functools.reduce(
                jnp.logical_or, [lax.axis_index("owners") == a for a, _ in step]
            )
            back = jnp.where(sent, back, ABSENT)
        backs.append(back)
    others = [swap(row_best[at], 2 * at) for at in range(1, split_count // 2)]
    local, _ = score(own, rows, [row_best[0], *backs[:-1]], own_first=True, after=keys)
    for other in others:
        local = jnp.maximum(local, other)
    best = jnp.maximum(local[:tiles], swap(local[tiles:], 1))
    return jnp.maximum(jnp.maximum(best, backs[-1]), -1.0).reshape(row_count)


def solution(mesh):
    placed = (
        P(("groups", "owners", "split"), None),
        P(),
        P(("groups", "owners", "split"), None),
        P(("groups", "owners", "split")),
    )
    return jax.shard_map(
        per_device,
        mesh=mesh,
        in_specs=placed,
        out_specs=P(("groups", "owners", "split")),
        check_vma=False,
    )
```

```python
import functools

import jax
import jax.numpy as jnp
from jax import lax
from jax.experimental import pallas as pl
from jax.experimental.pallas import tpu as pltpu
from jax.sharding import PartitionSpec as P

CPO = 8
LANES = 128
TAG_ROWS = 16
ABSENT = -2.0
STEPS = 16
PARTS = 2
VMEM_LIMIT = 48 * 1024 * 1024


def project_kernel(source_hbm, basis_hbm, owner_hbm, sub_hbm, *refs):
    packed_refs, (source, basis, owner, sub, sems, tag_sems) = refs[:-6], refs[-6:]
    row_count, depth = source.shape
    width = basis.shape[1]
    chunk = depth // STEPS
    spans = [(chunk * step, chunk * (step + 1)) for step in range(STEPS)]
    tag_copies = [
        pltpu.make_async_copy(owner_hbm, owner, tag_sems.at[0]),
        pltpu.make_async_copy(sub_hbm, sub, tag_sems.at[1]),
    ]
    copies = []
    for step, (start, end) in enumerate(spans):
        span = pl.ds(start, end - start)
        copies.append(
            (
                pltpu.make_async_copy(
                    basis_hbm.at[span, :], basis.at[span, :], sems.at[0, step]
                ),
                pltpu.make_async_copy(
                    source_hbm.at[:, span], source.at[:, span], sems.at[1, step]
                ),
            )
        )
    for pair in copies:
        for copy in pair:
            copy.start()
    for copy in tag_copies:
        copy.start()
    projected = None
    for (start, end), pair in zip(spans, copies):
        for copy in pair:
            copy.wait()
        part = jnp.dot(
            source[:, start:end], basis[start:end, :], preferred_element_type=jnp.float32
        )
        projected = part if projected is None else projected + part
    for copy in tag_copies:
        copy.wait()
    norms = jnp.sum(projected * projected, axis=1, keepdims=True)
    units = (projected * lax.rsqrt(norms + 1e-06)).astype(jnp.bfloat16)
    tags = (owner[...] * CPO + sub[...] + 1).astype(jnp.float32)
    for place, packed_ref in enumerate(packed_refs):
        rows = packed_ref.shape[0] - TAG_ROWS
        at = max(place - 1, 0) * rows
        here = tags[at // LANES : (at + rows) // LANES, :]
        here = jnp.concatenate(
            [here, jnp.zeros((TAG_ROWS - here.shape[0], LANES), jnp.float32)], axis=0
        )
        here = jnp.concatenate([here, jnp.zeros((TAG_ROWS, width - LANES), jnp.float32)], axis=1)
        packed_ref[:rows, :] = units[at : at + rows, :]
        packed_ref[rows:, :] = here.astype(jnp.bfloat16)


def project(embeddings, basis, owner_ids, sub_cluster):
    row_count, depth = embeddings.shape
    width = basis.shape[1]
    tag_shape = (row_count // LANES, LANES)
    sizes = [row_count]
    return pl.pallas_call(
        project_kernel,
        in_specs=[pl.BlockSpec(memory_space=pltpu.HBM)] * 4,
        out_specs=[pl.BlockSpec(memory_space=pltpu.VMEM)] * len(sizes),
        out_shape=[
            jax.ShapeDtypeStruct((size + TAG_ROWS, width), jnp.bfloat16) for size in sizes
        ],
        scratch_shapes=[
            pltpu.VMEM((row_count, depth), jnp.bfloat16),
            pltpu.VMEM((depth, width), jnp.bfloat16),
            pltpu.VMEM(tag_shape, jnp.int32),
            pltpu.VMEM(tag_shape, jnp.int32),
            pltpu.SemaphoreType.DMA((2, STEPS)),
            pltpu.SemaphoreType.DMA((2,)),
        ],
        compiler_params=pltpu.CompilerParams(vmem_limit_bytes=VMEM_LIMIT),
        cost_estimate=pl.CostEstimate(
            flops=2 * row_count * depth * width,
            bytes_accessed=2 * depth * (row_count + width),
            transcendentals=0,
        ),
    )(
        *[
            pltpu.with_memory_space_constraint(array, pltpu.HBM)
            for array in (
                embeddings,
                basis,
                owner_ids.reshape(tag_shape),
                sub_cluster.reshape(tag_shape),
            )
        ]
    )


def score_kernel(row_parts, own_first, bases, unread, *refs):
    refs = list(refs[unread:])
    key_ref = refs.pop(0)
    row_refs = [[refs.pop(0) for _ in range(parts)] for parts in row_parts]
    base_refs = [refs.pop(0) for _ in range(bases)]
    col_out, row_outs = refs[0], refs[1:]
    row_count = key_ref.shape[0] - TAG_ROWS
    tiles = row_count // LANES
    key_tags = key_ref[row_count:, :LANES].astype(jnp.float32)
    best = [jnp.full((8, LANES), ABSENT, jnp.float32) for _ in range(tiles)]
    for block, part_refs in enumerate(row_refs):
        tag_ref = part_refs[-1]
        row_tags = tag_ref[tag_ref.shape[0] - TAG_ROWS :, :LANES].astype(jnp.float32)
        place = 0
        for part_ref in part_refs:
            count = row_count // len(part_refs)
            scores = lax.dot_general(
                part_ref[:count, :],
                key_ref[:row_count, :],
                (((1,), (1,)), ((), ())),
                preferred_element_type=jnp.float32,
            )
            for start in range(0, count, LANES):
                tags = jnp.broadcast_to(row_tags[place : place + 1, :], (LANES, LANES)).T
                across = None
                for at in range(tiles):
                    same = tags == key_tags[at : at + 1, :]
                    if own_first and block == 0 and at == place:
                        same = same & (
                            lax.broadcasted_iota(jnp.int32, (LANES, LANES), 0)
                            != lax.broadcasted_iota(jnp.int32, (LANES, LANES), 1)
                        )
                    kept = scores[start : start + LANES, at * LANES : (at + 1) * LANES]
                    kept = jnp.where(same, kept, ABSENT)
                    best[at] = jnp.maximum(
                        best[at], jnp.max(kept.reshape(LANES // 8, 8, LANES), axis=0)
                    )
                    if row_outs:
                        across = kept if across is None else jnp.maximum(across, kept)
                if row_outs:
                    at = block % 2 * tiles + place
                    found = jnp.max(across.T, axis=0, keepdims=True)
                    if base_refs:
                        found = jnp.maximum(found, base_refs[block // 2][at : at + 1, :])
                    row_outs[block // 2][at : at + 1, :] = found
                place += 1
    for at in range(tiles):
        found = jnp.max(best[at], axis=0, keepdims=True)
        if own_first:
            for base_ref in base_refs:
                found = jnp.maximum(found, base_ref[at : at + 1, :])
        col_out[at : at + 1, :] = found
    if own_first:
        col_out[tiles:, :] = base_refs[0][tiles:, :]


def score(key, rows, bases, own_first=False, after=()):
    tiles = (key.shape[0] - TAG_ROWS) // LANES
    parts = [row if isinstance(row, tuple) else (row,) for row in rows]
    blocks = [part for row in parts for part in row]
    pair = jax.ShapeDtypeStruct((2 * tiles, LANES), jnp.float32)
    out_shape = [pair]
    if not own_first:
        out_shape = [jax.ShapeDtypeStruct((tiles, LANES), jnp.float32)] + [pair] * (len(rows) // 2)
    whole = pl.BlockSpec(memory_space=pltpu.VMEM)
    found = pl.pallas_call(
        functools.partial(
            score_kernel, [len(row) for row in parts], own_first, len(bases), len(after)
        ),
        in_specs=[pl.BlockSpec(memory_space=pl.ANY)] * len(after)
        + [whole] * (1 + len(blocks) + len(bases)),
        out_specs=[whole] * len(out_shape),
        out_shape=out_shape,
        compiler_params=pltpu.CompilerParams(vmem_limit_bytes=VMEM_LIMIT),
        cost_estimate=pl.CostEstimate(flops=0, bytes_accessed=0, transcendentals=0),
    )(*after, key, *blocks, *bases)
    return found[0], list(found[1:])


def owner_steps(count):
    steps = [[(i, (i + k) % count) for i in range(count)] for k in range(1, (count + 1) // 2)]
    if count % 2 == 0 and count > 1:
        half = count // 2
        steps.append([(i, i + half) if i % 2 == 0 else (i + half, i) for i in range(half)])
    return steps


def per_device(embeddings, basis, owner_ids, sub_cluster):
    row_count = embeddings.shape[0]
    tiles = row_count // LANES
    split_count, owner_count = lax.axis_size("split"), lax.axis_size("owners")
    steps = owner_steps(owner_count)[::-1]

    def swap(block, offset):
        return lax.ppermute(block, "split", [(s, s ^ offset) for s in range(split_count)])

    (own,) = project(embeddings, basis, owner_ids, sub_cluster)
    rows = [own, swap(own, 1)]
    for offset in range(2, split_count, 2):
        beside = swap(own, offset)
        part = row_count // PARTS
        starts = [part * at for at in range(PARTS)]
        ends = starts[1:] + [row_count + TAG_ROWS]
        rows += [beside, tuple(swap(beside[a:b], 1) for a, b in zip(starts, ends))]
    keys = [lax.ppermute(own, "owners", step) for step in steps]
    row_best, backs = [], []
    for block, step in zip(keys, steps):
        found, row_best = score(block, rows, row_best)
        back = lax.ppermute(found, "owners", [(b, a) for a, b in step])
        if len(step) < owner_count:
            sent = functools.reduce(
                jnp.logical_or, [lax.axis_index("owners") == a for a, _ in step]
            )
            back = jnp.where(sent, back, ABSENT)
        backs.append(back)
    others = [swap(row_best[at], 2 * at) for at in range(1, split_count // 2)]
    local, _ = score(own, rows, [row_best[0], *backs[:-1]], own_first=True, after=keys)
    for other in others:
        local = jnp.maximum(local, other)
    best = jnp.maximum(local[:tiles], swap(local[tiles:], 1))
    return jnp.maximum(jnp.maximum(best, backs[-1]), -1.0).reshape(row_count)


def solution(mesh):
    placed = (
        P(("groups", "owners", "split"), None),
        P(),
        P(("groups", "owners", "split"), None),
        P(("groups", "owners", "split")),
    )
    return jax.shard_map(
        per_device,
        mesh=mesh,
        in_specs=placed,
        out_specs=P(("groups", "owners", "split")),
        check_vma=False,
    )
```

```python
import functools

import jax
import jax.numpy as jnp
from jax import lax
from jax.experimental import pallas as pl
from jax.experimental.pallas import tpu as pltpu
from jax.sharding import PartitionSpec as P

CPO = 8
LANES = 128
TAG_ROWS = 16
ABSENT = -2.0
BASIS_STEPS = 4
ROW_STEPS = 4
PARTS = 2
VMEM_LIMIT = 48 * 1024 * 1024


def project_kernel(source_hbm, basis_hbm, owner_hbm, sub_hbm, packed_ref, *scratch):
    source, basis, owner, sub, basis_sems, source_sems, tag_sems = scratch
    row_count, depth = source.shape
    width = basis.shape[1]
    basis_copies = [
        pltpu.make_async_copy(basis_hbm.at[span, :], basis.at[span, :], basis_sems.at[step])
        for step, span in enumerate(cut(depth, BASIS_STEPS))
    ]
    source_copies = [
        pltpu.make_async_copy(source_hbm.at[span, :], source.at[span, :], source_sems.at[step])
        for step, span in enumerate(cut(row_count, ROW_STEPS))
    ]
    tag_copies = [
        pltpu.make_async_copy(owner_hbm, owner, tag_sems.at[0]),
        pltpu.make_async_copy(sub_hbm, sub, tag_sems.at[1]),
    ]
    for copy in basis_copies + source_copies + tag_copies:
        copy.start()
    for copy in basis_copies:
        copy.wait()
    for copy, span in zip(source_copies, cut(row_count, ROW_STEPS)):
        copy.wait()
        projected = jnp.dot(source[span, :], basis[...], preferred_element_type=jnp.float32)
        norms = jnp.sum(projected * projected, axis=1, keepdims=True)
        packed_ref[span, :] = (projected * lax.rsqrt(norms + 1e-06)).astype(jnp.bfloat16)
    for copy in tag_copies:
        copy.wait()
    tags = (owner[...] * CPO + sub[...] + 1).astype(jnp.float32)
    tags = jnp.concatenate(
        [tags, jnp.zeros((TAG_ROWS - tags.shape[0], LANES), jnp.float32)], axis=0
    )
    tags = jnp.concatenate([tags, jnp.zeros((TAG_ROWS, width - LANES), jnp.float32)], axis=1)
    packed_ref[row_count:, :] = tags.astype(jnp.bfloat16)


def cut(size, steps):
    return [pl.ds(size // steps * step, size // steps) for step in range(steps)]


def project(embeddings, basis, owner_ids, sub_cluster):
    row_count, depth = embeddings.shape
    width = basis.shape[1]
    tag_shape = (row_count // LANES, LANES)
    return pl.pallas_call(
        project_kernel,
        in_specs=[pl.BlockSpec(memory_space=pltpu.HBM)] * 4,
        out_specs=pl.BlockSpec(memory_space=pltpu.VMEM),
        out_shape=jax.ShapeDtypeStruct((row_count + TAG_ROWS, width), jnp.bfloat16),
        scratch_shapes=[
            pltpu.VMEM((row_count, depth), jnp.bfloat16),
            pltpu.VMEM((depth, width), jnp.bfloat16),
            pltpu.VMEM(tag_shape, jnp.int32),
            pltpu.VMEM(tag_shape, jnp.int32),
            pltpu.SemaphoreType.DMA((BASIS_STEPS,)),
            pltpu.SemaphoreType.DMA((ROW_STEPS,)),
            pltpu.SemaphoreType.DMA((2,)),
        ],
        compiler_params=pltpu.CompilerParams(vmem_limit_bytes=VMEM_LIMIT),
        cost_estimate=pl.CostEstimate(
            flops=2 * row_count * depth * width,
            bytes_accessed=2 * depth * (row_count + width),
            transcendentals=0,
        ),
    )(
        *[
            pltpu.with_memory_space_constraint(array, pltpu.HBM)
            for array in (
                embeddings,
                basis,
                owner_ids.reshape(tag_shape),
                sub_cluster.reshape(tag_shape),
            )
        ]
    )


def score_kernel(row_parts, bases, want_cols, own_first, unread, *refs):
    refs = list(refs[unread:])
    key_ref = refs.pop(0)
    row_refs = [[refs.pop(0) for _ in range(parts)] for parts in row_parts]
    base_refs = [refs.pop(0) for _ in range(bases)]
    col_out = refs.pop(0) if want_cols else None
    row_outs = refs
    row_count = key_ref.shape[0] - TAG_ROWS
    tiles = row_count // LANES
    key_tags = key_ref[row_count:, :LANES].astype(jnp.float32)
    best = [jnp.full((8, LANES), ABSENT, jnp.float32) for _ in range(tiles)]
    for block, part_refs in enumerate(row_refs):
        tag_ref = part_refs[-1]
        row_tags = tag_ref[tag_ref.shape[0] - TAG_ROWS :, :LANES].astype(jnp.float32)
        place = 0
        for part_ref in part_refs:
            count = part_ref.shape[0] - (TAG_ROWS if part_ref is tag_ref else 0)
            scores = lax.dot_general(
                part_ref[:count, :],
                key_ref[:row_count, :],
                (((1,), (1,)), ((), ())),
                preferred_element_type=jnp.float32,
            )
            for start in range(0, count, LANES):
                tags = jnp.broadcast_to(row_tags[place : place + 1, :], (LANES, LANES)).T
                across = None
                for at in range(tiles):
                    same = tags == key_tags[at : at + 1, :]
                    if own_first and block == 0 and at == place:
                        same = same & (
                            lax.broadcasted_iota(jnp.int32, (LANES, LANES), 0)
                            != lax.broadcasted_iota(jnp.int32, (LANES, LANES), 1)
                        )
                    kept = scores[start : start + LANES, at * LANES : (at + 1) * LANES]
                    kept = jnp.where(same, kept, ABSENT)
                    if want_cols:
                        best[at] = jnp.maximum(
                            best[at], jnp.max(kept.reshape(LANES // 8, 8, LANES), axis=0)
                        )
                    if row_outs:
                        across = kept if across is None else jnp.maximum(across, kept)
                if row_outs:
                    found = jnp.max(across.T, axis=0, keepdims=True)
                    if base_refs:
                        found = jnp.maximum(found, base_refs[block][place : place + 1, :])
                    row_outs[block][place : place + 1, :] = found
                place += 1
    if want_cols:
        for at in range(tiles):
            col_out[at : at + 1, :] = jnp.max(best[at], axis=0, keepdims=True)


def score(key, rows, bases=(), want_cols=True, want_rows=True, own_first=False, after=()):
    best = jax.ShapeDtypeStruct(((key.shape[0] - TAG_ROWS) // LANES, LANES), jnp.float32)
    parts = [row if isinstance(row, tuple) else (row,) for row in rows]
    blocks = [part for row in parts for part in row]
    out_shape = [best] * (want_cols + want_rows * len(rows))
    whole = pl.BlockSpec(memory_space=pltpu.VMEM)
    found = pl.pallas_call(
        functools.partial(
            score_kernel,
            [len(row) for row in parts],
            len(bases),
            want_cols,
            own_first,
            len(after),
        ),
        in_specs=[pl.BlockSpec(memory_space=pl.ANY)] * len(after)
        + [whole] * (1 + len(blocks) + len(bases)),
        out_specs=[whole] * len(out_shape),
        out_shape=out_shape,
        compiler_params=pltpu.CompilerParams(vmem_limit_bytes=VMEM_LIMIT),
        cost_estimate=pl.CostEstimate(flops=0, bytes_accessed=0, transcendentals=0),
    )(*after, key, *blocks, *bases)
    return list(found[:want_cols]), list(found[want_cols:])


def owner_steps(count):
    half = count // 2
    circle = [count - 1 - 2 * i for i in range(half)] + [count - 2 - 2 * i for i in range(half)]
    return [
        [(circle[i], circle[(i + step) % count]) for i in range(count)]
        for step in range(1, half + 1)
    ]


def per_device(embeddings, basis, owner_ids, sub_cluster):
    row_count = embeddings.shape[0]
    split_count, owner_count = lax.axis_size("split"), lax.axis_size("owners")

    def swap(block, offset):
        return lax.ppermute(block, "split", [(s, s ^ offset) for s in range(split_count)])

    own = project(embeddings, basis, owner_ids, sub_cluster)
    rows = [own, swap(own, 1)]
    for offset in range(2, split_count, 2):
        beside = swap(own, offset)
        part = row_count // PARTS
        ends = [part * at for at in range(1, PARTS)] + [row_count + TAG_ROWS]
        rows += [beside, tuple(swap(beside[a:b], 1) for a, b in zip([0] + ends, ends))]
    *steps, last = owner_steps(owner_count)
    keys = [lax.ppermute(own, "owners", step) for step in steps]
    nearby = lax.ppermute(own, "owners", last)
    _, row_best = score(nearby, rows, want_cols=False)
    backs = []
    for key, step in zip(keys, steps):
        (found,), row_best = score(key, rows, row_best)
        backs.append(lax.ppermute(found, "owners", [(b, a) for a, b in step]))
    backs += [swap(found, offset) for offset, found in enumerate(row_best) if offset]
    (alone,), _ = score(own, rows, want_rows=False, own_first=True, after=[*keys, nearby])
    best = jnp.maximum(row_best[0], alone)
    for back in backs:
        best = jnp.maximum(best, back)
    return jnp.maximum(best, -1.0).reshape(row_count)


def solution(mesh):
    placed = (
        P(("groups", "owners", "split"), None),
        P(),
        P(("groups", "owners", "split"), None),
        P(("groups", "owners", "split")),
    )
    return jax.shard_map(
        per_device,
        mesh=mesh,
        in_specs=placed,
        out_specs=P(("groups", "owners", "split")),
        check_vma=False,
    )
```

```python
import functools

import jax
import jax.numpy as jnp
from jax import lax
from jax.experimental import pallas as pl
from jax.experimental.pallas import tpu as pltpu
from jax.sharding import PartitionSpec as P

CPO = 8
LANES = 128
TAG_ROWS = 16
ABSENT = -2.0
STEPS = 8
ROW_PARTS = 2
VMEM_LIMIT = 48 * 1024 * 1024


def project_kernel(source_hbm, basis_hbm, owner_hbm, sub_hbm, packed_ref, *scratch):
    source, basis, owner, sub, sems, tag_sems = scratch
    row_count, depth = source.shape
    width = basis.shape[1]
    spans = cut(depth, STEPS)
    copies = [
        (
            pltpu.make_async_copy(basis_hbm.at[span, :], basis.at[span, :], sems.at[0, step]),
            pltpu.make_async_copy(source_hbm.at[:, span], source.at[:, span], sems.at[1, step]),
        )
        for step, span in enumerate(spans)
    ]
    tag_copies = [
        pltpu.make_async_copy(owner_hbm, owner, tag_sems.at[0]),
        pltpu.make_async_copy(sub_hbm, sub, tag_sems.at[1]),
    ]
    for copy in [copy for pair in copies for copy in pair] + tag_copies:
        copy.start()
    totals = [None] * ROW_PARTS
    for span, pair in zip(spans, copies):
        for copy in pair:
            copy.wait()
        for at, rows in enumerate(cut(row_count, ROW_PARTS)):
            part = jnp.dot(source[rows, span], basis[span, :], preferred_element_type=jnp.float32)
            totals[at] = part if totals[at] is None else totals[at] + part
    for projected, rows in zip(totals, cut(row_count, ROW_PARTS)):
        norms = jnp.sum(projected * projected, axis=1, keepdims=True)
        packed_ref[rows, :] = (projected * lax.rsqrt(norms + 1e-06)).astype(jnp.bfloat16)
    for copy in tag_copies:
        copy.wait()
    tags = (owner[...] * CPO + sub[...] + 1).astype(jnp.float32)
    tags = jnp.concatenate(
        [tags, jnp.zeros((TAG_ROWS - tags.shape[0], LANES), jnp.float32)], axis=0
    )
    tags = jnp.concatenate([tags, jnp.zeros((TAG_ROWS, width - LANES), jnp.float32)], axis=1)
    packed_ref[row_count:, :] = tags.astype(jnp.bfloat16)


def cut(size, steps):
    return [pl.ds(size // steps * step, size // steps) for step in range(steps)]


def project(embeddings, basis, owner_ids, sub_cluster):
    row_count, depth = embeddings.shape
    width = basis.shape[1]
    tag_shape = (row_count // LANES, LANES)
    return pl.pallas_call(
        project_kernel,
        in_specs=[pl.BlockSpec(memory_space=pltpu.HBM)] * 4,
        out_specs=pl.BlockSpec(memory_space=pltpu.VMEM),
        out_shape=jax.ShapeDtypeStruct((row_count + TAG_ROWS, width), jnp.bfloat16),
        scratch_shapes=[
            pltpu.VMEM((row_count, depth), jnp.bfloat16),
            pltpu.VMEM((depth, width), jnp.bfloat16),
            pltpu.VMEM(tag_shape, jnp.int32),
            pltpu.VMEM(tag_shape, jnp.int32),
            pltpu.SemaphoreType.DMA((2, STEPS)),
            pltpu.SemaphoreType.DMA((2,)),
        ],
        compiler_params=pltpu.CompilerParams(vmem_limit_bytes=VMEM_LIMIT),
        cost_estimate=pl.CostEstimate(
            flops=2 * row_count * depth * width,
            bytes_accessed=2 * depth * (row_count + width),
            transcendentals=0,
        ),
    )(
        *[
            pltpu.with_memory_space_constraint(array, pltpu.HBM)
            for array in (
                embeddings,
                basis,
                owner_ids.reshape(tag_shape),
                sub_cluster.reshape(tag_shape),
            )
        ]
    )


def score_kernel(key_parts, row_parts, bases, want_cols, own_first, unread, *refs):
    refs = list(refs[unread:])
    key_refs = [refs.pop(0) for _ in range(key_parts)]
    row_refs = [[refs.pop(0) for _ in range(parts)] for parts in row_parts]
    base_refs = [refs.pop(0) for _ in range(bases)]
    col_out = refs.pop(0) if want_cols else None
    row_outs = refs
    key_tag_ref = key_refs[-1]
    key_tags = key_tag_ref[key_tag_ref.shape[0] - TAG_ROWS :, :LANES].astype(jnp.float32)
    tiles = sum(key_ref.shape[0] for key_ref in key_refs) // LANES
    best = [jnp.full((8, LANES), ABSENT, jnp.float32) for _ in range(tiles)]
    for block, part_refs in enumerate(row_refs):
        tag_ref = part_refs[-1]
        row_tags = tag_ref[tag_ref.shape[0] - TAG_ROWS :, :LANES].astype(jnp.float32)
        place = 0
        for part_ref in part_refs:
            count = part_ref.shape[0] // LANES * LANES
            scores = [
                lax.dot_general(
                    part_ref[:count, :],
                    key_ref[: key_ref.shape[0] // LANES * LANES, :],
                    (((1,), (1,)), ((), ())),
                    preferred_element_type=jnp.float32,
                )
                for key_ref in key_refs
            ]
            scores = [
                part[:, start : start + LANES]
                for part in scores
                for start in range(0, part.shape[1], LANES)
            ]
            for start in range(0, count, LANES):
                tags = jnp.broadcast_to(row_tags[place : place + 1, :], (LANES, LANES)).T
                across = None
                for at in range(tiles):
                    same = tags == key_tags[at : at + 1, :]
                    if own_first and block == 0 and at == place:
                        same = same & (
                            lax.broadcasted_iota(jnp.int32, (LANES, LANES), 0)
                            != lax.broadcasted_iota(jnp.int32, (LANES, LANES), 1)
                        )
                    kept = jnp.where(same, scores[at][start : start + LANES, :], ABSENT)
                    if want_cols or own_first:
                        best[at] = jnp.maximum(
                            best[at], jnp.max(kept.reshape(LANES // 8, 8, LANES), axis=0)
                        )
                    if not own_first:
                        across = kept if across is None else jnp.maximum(across, kept)
                if not own_first:
                    at = block % 2 * tiles + place
                    found = jnp.max(across.T, axis=0, keepdims=True)
                    if base_refs:
                        found = jnp.maximum(found, base_refs[block // 2][at : at + 1, :])
                    row_outs[block // 2][at : at + 1, :] = found
                place += 1
    for at in range(tiles):
        found = jnp.max(best[at], axis=0, keepdims=True)
        if want_cols:
            col_out[at : at + 1, :] = found
        if own_first:
            row_outs[0][at : at + 1, :] = jnp.maximum(found, base_refs[0][at : at + 1, :])
    if own_first:
        row_outs[0][tiles:, :] = base_refs[0][tiles:, :]


def score(key, rows, bases=(), want_cols=True, own_first=False, after=()):
    whole = lambda block: block if isinstance(block, tuple) else (block,)
    key, parts = whole(key), [whole(row) for row in rows]
    blocks = [part for row in parts for part in row]
    tiles = sum(part.shape[0] for part in key) // LANES
    best = jax.ShapeDtypeStruct((tiles, LANES), jnp.float32)
    pair = jax.ShapeDtypeStruct((2 * tiles, LANES), jnp.float32)
    out_shape = [best] * want_cols + [pair] * (1 if own_first else len(rows) // 2)
    inside = pl.BlockSpec(memory_space=pltpu.VMEM)
    found = pl.pallas_call(
        functools.partial(
            score_kernel,
            len(key),
            [len(row) for row in parts],
            len(bases),
            want_cols,
            own_first,
            len(after),
        ),
        in_specs=[pl.BlockSpec(memory_space=pl.ANY)] * len(after)
        + [inside] * (len(key) + len(blocks) + len(bases)),
        out_specs=[inside] * len(out_shape),
        out_shape=out_shape,
        compiler_params=pltpu.CompilerParams(vmem_limit_bytes=VMEM_LIMIT),
        cost_estimate=pl.CostEstimate(flops=0, bytes_accessed=0, transcendentals=0),
    )(*after, *key, *blocks, *bases)
    return list(found[:want_cols]), list(found[want_cols:])


def owner_steps(count):
    half = count // 2
    circle = [count - 1 - 2 * i for i in range(half)] + [count - 2 - 2 * i for i in range(half)]
    return [
        [(circle[i], circle[(i + step) % count]) for i in range(count)]
        for step in range(1, half + 1)
    ]


def per_device(embeddings, basis, owner_ids, sub_cluster):
    row_count = embeddings.shape[0]
    tiles = row_count // LANES
    split_count, owner_count = lax.axis_size("split"), lax.axis_size("owners")

    def swap(block, offset):
        return lax.ppermute(block, "split", [(s, s ^ offset) for s in range(split_count)])

    def halves(block):
        return block[: row_count // 2], block[row_count // 2 :]

    own = project(embeddings, basis, owner_ids, sub_cluster)
    rows = [own, swap(own, 1)]
    for offset in range(2, split_count, 2):
        beside = swap(own, offset)
        rows += [beside, tuple(swap(part, 1) for part in halves(beside))]
    *steps, last = owner_steps(owner_count)
    keys = [lax.ppermute(own, "owners", step) for step in steps]
    nearby = tuple(lax.ppermute(part, "owners", last) for part in halves(own))
    _, row_best = score(nearby, rows, want_cols=False)
    backs = []
    for key, step in zip(keys, steps):
        (found,), row_best = score(key, rows, row_best)
        backs.append(lax.ppermute(found, "owners", [(b, a) for a, b in step]))
    others = [swap(found, 2 * at) for at, found in enumerate(row_best) if at]
    _, (local,) = score(
        own, rows, row_best[:1], want_cols=False, own_first=True, after=[*keys, *nearby]
    )
    for other in others:
        local = jnp.maximum(local, other)
    best = jnp.maximum(local[:tiles], swap(local[tiles:], 1))
    for back in backs:
        best = jnp.maximum(best, back)
    return jnp.maximum(best, -1.0).reshape(row_count)


def solution(mesh):
    placed = (
        P(("groups", "owners", "split"), None),
        P(),
        P(("groups", "owners", "split"), None),
        P(("groups", "owners", "split")),
    )
    return jax.shard_map(
        per_device,
        mesh=mesh,
        in_specs=placed,
        out_specs=P(("groups", "owners", "split")),
        check_vma=False,
    )
```

```python
import functools

import jax
import jax.numpy as jnp
from jax import lax
from jax.experimental import pallas as pl
from jax.experimental.pallas import tpu as pltpu
from jax.sharding import PartitionSpec as P

CPO = 8
LANES = 128
TAG_ROWS = 16
ABSENT = -2.0
STEPS = 8
ROW_PARTS = 4
VMEM_LIMIT = 48 * 1024 * 1024


def project_kernel(source_hbm, basis_hbm, owner_hbm, sub_hbm, packed_ref, *scratch):
    source, basis, owner, sub, sems, tag_sems = scratch
    row_count, depth = source.shape
    width = basis.shape[1]
    spans = cut(depth, STEPS)
    copies = [
        (
            pltpu.make_async_copy(basis_hbm.at[span, :], basis.at[span, :], sems.at[0, step]),
            pltpu.make_async_copy(source_hbm.at[:, span], source.at[:, span], sems.at[1, step]),
        )
        for step, span in enumerate(spans)
    ]
    tag_copies = [
        pltpu.make_async_copy(owner_hbm, owner, tag_sems.at[0]),
        pltpu.make_async_copy(sub_hbm, sub, tag_sems.at[1]),
    ]
    for copy in [copy for pair in copies for copy in pair] + tag_copies:
        copy.start()
    totals = [None] * ROW_PARTS
    for span, pair in zip(spans, copies):
        for copy in pair:
            copy.wait()
        for at, rows in enumerate(cut(row_count, ROW_PARTS)):
            part = jnp.dot(source[rows, span], basis[span, :], preferred_element_type=jnp.float32)
            totals[at] = part if totals[at] is None else totals[at] + part
    for projected, rows in zip(totals, cut(row_count, ROW_PARTS)):
        norms = jnp.sum(projected * projected, axis=1, keepdims=True)
        packed_ref[rows, :] = (projected * lax.rsqrt(norms + 1e-06)).astype(jnp.bfloat16)
    for copy in tag_copies:
        copy.wait()
    tags = (owner[...] * CPO + sub[...] + 1).astype(jnp.float32)
    tags = jnp.concatenate(
        [tags, jnp.zeros((TAG_ROWS - tags.shape[0], LANES), jnp.float32)], axis=0
    )
    tags = jnp.concatenate([tags, jnp.zeros((TAG_ROWS, width - LANES), jnp.float32)], axis=1)
    packed_ref[row_count:, :] = tags.astype(jnp.bfloat16)


def cut(size, steps):
    return [pl.ds(size // steps * step, size // steps) for step in range(steps)]


def project(embeddings, basis, owner_ids, sub_cluster):
    row_count, depth = embeddings.shape
    width = basis.shape[1]
    tag_shape = (row_count // LANES, LANES)
    return pl.pallas_call(
        project_kernel,
        in_specs=[pl.BlockSpec(memory_space=pltpu.HBM)] * 4,
        out_specs=pl.BlockSpec(memory_space=pltpu.VMEM),
        out_shape=jax.ShapeDtypeStruct((row_count + TAG_ROWS, width), jnp.bfloat16),
        scratch_shapes=[
            pltpu.VMEM((row_count, depth), jnp.bfloat16),
            pltpu.VMEM((depth, width), jnp.bfloat16),
            pltpu.VMEM(tag_shape, jnp.int32),
            pltpu.VMEM(tag_shape, jnp.int32),
            pltpu.SemaphoreType.DMA((2, STEPS)),
            pltpu.SemaphoreType.DMA((2,)),
        ],
        compiler_params=pltpu.CompilerParams(vmem_limit_bytes=VMEM_LIMIT),
        cost_estimate=pl.CostEstimate(
            flops=2 * row_count * depth * width,
            bytes_accessed=2 * depth * (row_count + width),
            transcendentals=0,
        ),
    )(
        *[
            pltpu.with_memory_space_constraint(array, pltpu.HBM)
            for array in (
                embeddings,
                basis,
                owner_ids.reshape(tag_shape),
                sub_cluster.reshape(tag_shape),
            )
        ]
    )


def score_kernel(key_parts, row_parts, bases, want_cols, own_first, unread, *refs):
    refs = list(refs[unread:])
    key_refs = [refs.pop(0) for _ in range(key_parts)]
    row_refs = [[refs.pop(0) for _ in range(parts)] for parts in row_parts]
    base_refs = [refs.pop(0) for _ in range(bases)]
    col_out = refs.pop(0) if want_cols else None
    row_outs = refs
    key_tag_ref = key_refs[-1]
    key_tags = key_tag_ref[key_tag_ref.shape[0] - TAG_ROWS :, :LANES].astype(jnp.float32)
    tiles = sum(key_ref.shape[0] for key_ref in key_refs) // LANES
    best = [jnp.full((8, LANES), ABSENT, jnp.float32) for _ in range(tiles)]
    for block, part_refs in enumerate(row_refs):
        tag_ref = part_refs[-1]
        row_tags = tag_ref[tag_ref.shape[0] - TAG_ROWS :, :LANES].astype(jnp.float32)
        place = 0
        for part_ref in part_refs:
            count = part_ref.shape[0] // LANES * LANES
            scores = [
                lax.dot_general(
                    part_ref[:count, :],
                    key_ref[: key_ref.shape[0] // LANES * LANES, :],
                    (((1,), (1,)), ((), ())),
                    preferred_element_type=jnp.float32,
                )
                for key_ref in key_refs
            ]
            scores = [
                part[:, start : start + LANES]
                for part in scores
                for start in range(0, part.shape[1], LANES)
            ]
            for start in range(0, count, LANES):
                tags = jnp.broadcast_to(row_tags[place : place + 1, :], (LANES, LANES)).T
                across = None
                for at in range(tiles):
                    same = tags == key_tags[at : at + 1, :]
                    if own_first and block == 0 and at == place:
                        same = same & (
                            lax.broadcasted_iota(jnp.int32, (LANES, LANES), 0)
                            != lax.broadcasted_iota(jnp.int32, (LANES, LANES), 1)
                        )
                    kept = jnp.where(same, scores[at][start : start + LANES, :], ABSENT)
                    if want_cols or own_first:
                        best[at] = jnp.maximum(
                            best[at], jnp.max(kept.reshape(LANES // 8, 8, LANES), axis=0)
                        )
                    if not own_first:
                        across = kept if across is None else jnp.maximum(across, kept)
                if not own_first:
                    at = block % 2 * tiles + place
                    found = jnp.max(across.T, axis=0, keepdims=True)
                    if base_refs:
                        found = jnp.maximum(found, base_refs[block // 2][at : at + 1, :])
                    row_outs[block // 2][at : at + 1, :] = found
                place += 1
    for at in range(tiles):
        found = jnp.max(best[at], axis=0, keepdims=True)
        if want_cols:
            col_out[at : at + 1, :] = found
        if own_first:
            for base_ref in base_refs:
                found = jnp.maximum(found, base_ref[at : at + 1, :])
            row_outs[0][at : at + 1, :] = found
    if own_first:
        row_outs[0][tiles:, :] = base_refs[0][tiles:, :]


def score(key, rows, bases=(), want_cols=True, own_first=False, after=()):
    whole = lambda block: block if isinstance(block, tuple) else (block,)
    key, parts = whole(key), [whole(row) for row in rows]
    blocks = [part for row in parts for part in row]
    tiles = sum(part.shape[0] for part in key) // LANES
    best = jax.ShapeDtypeStruct((tiles, LANES), jnp.float32)
    pair = jax.ShapeDtypeStruct((2 * tiles, LANES), jnp.float32)
    out_shape = [best] * want_cols + [pair] * (1 if own_first else len(rows) // 2)
    inside = pl.BlockSpec(memory_space=pltpu.VMEM)
    found = pl.pallas_call(
        functools.partial(
            score_kernel,
            len(key),
            [len(row) for row in parts],
            len(bases),
            want_cols,
            own_first,
            len(after),
        ),
        in_specs=[pl.BlockSpec(memory_space=pl.ANY)] * len(after)
        + [inside] * (len(key) + len(blocks) + len(bases)),
        out_specs=[inside] * len(out_shape),
        out_shape=out_shape,
        compiler_params=pltpu.CompilerParams(vmem_limit_bytes=VMEM_LIMIT),
        cost_estimate=pl.CostEstimate(flops=0, bytes_accessed=0, transcendentals=0),
    )(*after, *key, *blocks, *bases)
    return list(found[:want_cols]), list(found[want_cols:])


def owner_steps(count):
    half = count // 2
    circle = [count - 1 - 2 * i for i in range(half)] + [count - 2 - 2 * i for i in range(half)]
    return [
        [(circle[i], circle[(i + step) % count]) for i in range(count)]
        for step in range(1, half + 1)
    ]


def per_device(embeddings, basis, owner_ids, sub_cluster):
    row_count = embeddings.shape[0]
    tiles = row_count // LANES
    split_count, owner_count = lax.axis_size("split"), lax.axis_size("owners")

    def swap(block, offset):
        return lax.ppermute(block, "split", [(s, s ^ offset) for s in range(split_count)])

    def halves(block):
        return block[: row_count // 2], block[row_count // 2 :]

    own = project(embeddings, basis, owner_ids, sub_cluster)
    rows = [own, swap(own, 1)]
    for offset in range(2, split_count, 2):
        beside = swap(own, offset)
        rows += [beside, tuple(swap(part, 1) for part in halves(beside))]
    *steps, last = owner_steps(owner_count)
    keys = [lax.ppermute(own, "owners", step) for step in steps]
    nearby = lax.ppermute(own, "owners", last)
    row_best, backs = [], []
    for key, step in zip(keys, steps):
        (found,), row_best = score(key, rows, row_best)
        backs.append(lax.ppermute(found, "owners", [(b, a) for a, b in step]))
    _, row_best = score(nearby, rows, row_best, want_cols=False)
    others = [swap(found, 2 * at) for at, found in enumerate(row_best) if at]
    _, (local,) = score(
        own,
        rows,
        [row_best[0], *(jnp.maximum(back, ABSENT) for back in backs)],
        want_cols=False,
        own_first=True,
        after=[*keys, nearby],
    )
    for other in others:
        local = jnp.maximum(local, other)
    best = jnp.maximum(local[:tiles], swap(local[tiles:], 1))
    return jnp.maximum(best, -1.0).reshape(row_count)


def solution(mesh):
    placed = (
        P(("groups", "owners", "split"), None),
        P(),
        P(("groups", "owners", "split"), None),
        P(("groups", "owners", "split")),
    )
    return jax.shard_map(
        per_device,
        mesh=mesh,
        in_specs=placed,
        out_specs=P(("groups", "owners", "split")),
        check_vma=False,
    )
```

```python
import functools

import jax
import jax.numpy as jnp
from jax import lax
from jax.experimental import pallas as pl
from jax.experimental.pallas import tpu as pltpu
from jax.sharding import PartitionSpec as P

CPO = 8
LANES = 128
TAG_ROWS = 16
ABSENT = -2.0
STEPS = 8
ROW_PARTS = 4
VMEM_LIMIT = 48 * 1024 * 1024


def project_kernel(source_hbm, basis_hbm, owner_hbm, sub_hbm, packed_ref, *scratch):
    source, basis, owner, sub, sems, tag_sems = scratch
    row_count, depth = source.shape
    width = basis.shape[1]
    spans = cut(depth, STEPS)
    copies = [
        (
            pltpu.make_async_copy(basis_hbm.at[span, :], basis.at[span, :], sems.at[0, step]),
            pltpu.make_async_copy(source_hbm.at[:, span], source.at[:, span], sems.at[1, step]),
        )
        for step, span in enumerate(spans)
    ]
    tag_copies = [
        pltpu.make_async_copy(owner_hbm, owner, tag_sems.at[0]),
        pltpu.make_async_copy(sub_hbm, sub, tag_sems.at[1]),
    ]
    for copy in [copy for pair in copies for copy in pair] + tag_copies:
        copy.start()
    totals = [None] * ROW_PARTS
    for span, pair in zip(spans, copies):
        for copy in pair:
            copy.wait()
        for at, rows in enumerate(cut(row_count, ROW_PARTS)):
            part = jnp.dot(source[rows, span], basis[span, :], preferred_element_type=jnp.float32)
            totals[at] = part if totals[at] is None else totals[at] + part
    for projected, rows in zip(totals, cut(row_count, ROW_PARTS)):
        norms = jnp.sum(projected * projected, axis=1, keepdims=True)
        packed_ref[rows, :] = (projected * lax.rsqrt(norms + 1e-06)).astype(jnp.bfloat16)
    for copy in tag_copies:
        copy.wait()
    tags = (owner[...] * CPO + sub[...] + 1).astype(jnp.float32)
    tags = jnp.concatenate(
        [tags, jnp.zeros((TAG_ROWS - tags.shape[0], LANES), jnp.float32)], axis=0
    )
    tags = jnp.concatenate([tags, jnp.zeros((TAG_ROWS, width - LANES), jnp.float32)], axis=1)
    packed_ref[row_count:, :] = tags.astype(jnp.bfloat16)


def cut(size, steps):
    return [pl.ds(size // steps * step, size // steps) for step in range(steps)]


def project(embeddings, basis, owner_ids, sub_cluster):
    row_count, depth = embeddings.shape
    width = basis.shape[1]
    tag_shape = (row_count // LANES, LANES)
    return pl.pallas_call(
        project_kernel,
        in_specs=[pl.BlockSpec(memory_space=pltpu.HBM)] * 4,
        out_specs=pl.BlockSpec(memory_space=pltpu.VMEM),
        out_shape=jax.ShapeDtypeStruct((row_count + TAG_ROWS, width), jnp.bfloat16),
        scratch_shapes=[
            pltpu.VMEM((row_count, depth), jnp.bfloat16),
            pltpu.VMEM((depth, width), jnp.bfloat16),
            pltpu.VMEM(tag_shape, jnp.int32),
            pltpu.VMEM(tag_shape, jnp.int32),
            pltpu.SemaphoreType.DMA((2, STEPS)),
            pltpu.SemaphoreType.DMA((2,)),
        ],
        compiler_params=pltpu.CompilerParams(vmem_limit_bytes=VMEM_LIMIT),
        cost_estimate=pl.CostEstimate(
            flops=2 * row_count * depth * width,
            bytes_accessed=2 * depth * (row_count + width),
            transcendentals=0,
        ),
    )(
        *[
            pltpu.with_memory_space_constraint(array, pltpu.HBM)
            for array in (
                embeddings,
                basis,
                owner_ids.reshape(tag_shape),
                sub_cluster.reshape(tag_shape),
            )
        ]
    )


def score_kernel(key_parts, row_parts, bases, want_cols, own_first, unread, *refs):
    refs = list(refs[unread:])
    key_refs = [refs.pop(0) for _ in range(key_parts)]
    row_refs = [[refs.pop(0) for _ in range(parts)] for parts in row_parts]
    base_refs = [refs.pop(0) for _ in range(bases)]
    col_out = refs.pop(0) if want_cols else None
    row_outs = refs
    key_tag_ref = key_refs[-1]
    key_tags = key_tag_ref[key_tag_ref.shape[0] - TAG_ROWS :, :LANES].astype(jnp.float32)
    tiles = sum(key_ref.shape[0] for key_ref in key_refs) // LANES
    best = [jnp.full((8, LANES), ABSENT, jnp.float32) for _ in range(tiles)]
    for block, part_refs in enumerate(row_refs):
        tag_ref = part_refs[-1]
        row_tags = tag_ref[tag_ref.shape[0] - TAG_ROWS :, :LANES].astype(jnp.float32)
        place = 0
        for part_ref in part_refs:
            count = part_ref.shape[0] // LANES * LANES
            scores = [
                lax.dot_general(
                    part_ref[:count, :],
                    key_ref[: key_ref.shape[0] // LANES * LANES, :],
                    (((1,), (1,)), ((), ())),
                    preferred_element_type=jnp.float32,
                )
                for key_ref in key_refs
            ]
            scores = [
                part[:, start : start + LANES]
                for part in scores
                for start in range(0, part.shape[1], LANES)
            ]
            for start in range(0, count, LANES):
                tags = jnp.broadcast_to(row_tags[place : place + 1, :], (LANES, LANES)).T
                across = None
                for at in range(tiles):
                    same = tags == key_tags[at : at + 1, :]
                    if own_first and block == 0 and at == place:
                        same = same & (
                            lax.broadcasted_iota(jnp.int32, (LANES, LANES), 0)
                            != lax.broadcasted_iota(jnp.int32, (LANES, LANES), 1)
                        )
                    kept = jnp.where(same, scores[at][start : start + LANES, :], ABSENT)
                    if want_cols or own_first:
                        best[at] = jnp.maximum(
                            best[at], jnp.max(kept.reshape(LANES // 8, 8, LANES), axis=0)
                        )
                    if not own_first:
                        across = kept if across is None else jnp.maximum(across, kept)
                if not own_first:
                    at = block % 2 * tiles + place
                    found = jnp.max(across.T, axis=0, keepdims=True)
                    if base_refs:
                        found = jnp.maximum(found, base_refs[block // 2][at : at + 1, :])
                    row_outs[block // 2][at : at + 1, :] = found
                place += 1
    for at in range(tiles):
        found = jnp.max(best[at], axis=0, keepdims=True)
        if want_cols:
            col_out[at : at + 1, :] = found
        if own_first:
            for base_ref in base_refs:
                found = jnp.maximum(found, base_ref[at : at + 1, :])
            row_outs[0][at : at + 1, :] = found
    if own_first:
        row_outs[0][tiles:, :] = base_refs[0][tiles:, :]


def score(key, rows, bases=(), want_cols=True, own_first=False, after=()):
    whole = lambda block: block if isinstance(block, tuple) else (block,)
    key, parts = whole(key), [whole(row) for row in rows]
    blocks = [part for row in parts for part in row]
    tiles = sum(part.shape[0] for part in key) // LANES
    best = jax.ShapeDtypeStruct((tiles, LANES), jnp.float32)
    pair = jax.ShapeDtypeStruct((2 * tiles, LANES), jnp.float32)
    out_shape = [best] * want_cols + [pair] * (1 if own_first else len(rows) // 2)
    inside = pl.BlockSpec(memory_space=pltpu.VMEM)
    found = pl.pallas_call(
        functools.partial(
            score_kernel,
            len(key),
            [len(row) for row in parts],
            len(bases),
            want_cols,
            own_first,
            len(after),
        ),
        in_specs=[pl.BlockSpec(memory_space=pl.ANY)] * len(after)
        + [inside] * (len(key) + len(blocks) + len(bases)),
        out_specs=[inside] * len(out_shape),
        out_shape=out_shape,
        compiler_params=pltpu.CompilerParams(vmem_limit_bytes=VMEM_LIMIT),
        cost_estimate=pl.CostEstimate(flops=0, bytes_accessed=0, transcendentals=0),
    )(*after, *key, *blocks, *bases)
    return list(found[:want_cols]), list(found[want_cols:])


def owner_steps(count):
    half = count // 2
    circle = [count - 1 - 2 * i for i in range(half)] + [count - 2 - 2 * i for i in range(half)]
    return [
        [(circle[(i + step) % count], circle[i]) for i in range(count)]
        for step in range(1, half + 1)
    ]


def per_device(embeddings, basis, owner_ids, sub_cluster):
    row_count = embeddings.shape[0]
    tiles = row_count // LANES
    split_count, owner_count = lax.axis_size("split"), lax.axis_size("owners")

    def swap(block, offset):
        return lax.ppermute(block, "split", [(s, s ^ offset) for s in range(split_count)])

    def halves(block):
        return block[: row_count // 2], block[row_count // 2 :]

    own = project(embeddings, basis, owner_ids, sub_cluster)
    rows = [own, swap(own, 1)]
    for offset in range(2, split_count, 2):
        beside = swap(own, offset)
        rows += [beside, tuple(swap(part, 1) for part in halves(beside))]
    *steps, last = owner_steps(owner_count)
    keys = [lax.ppermute(own, "owners", step) for step in steps]
    nearby = lax.ppermute(own, "owners", last)
    _, row_best = score(nearby, rows, want_cols=False)
    backs = []
    for key, step in zip(keys, steps):
        (found,), row_best = score(key, rows, row_best)
        backs.append(lax.ppermute(found, "owners", [(b, a) for a, b in step]))
    others = [swap(found, 2 * at) for at, found in enumerate(row_best) if at]
    _, (local,) = score(
        own, rows, row_best[:1], want_cols=False, own_first=True, after=[*keys, nearby]
    )
    for other in others:
        local = jnp.maximum(local, other)
    best = jnp.maximum(local[:tiles], swap(local[tiles:], 1))
    for back in backs:
        best = jnp.maximum(best, back)
    return jnp.maximum(best, -1.0).reshape(row_count)


def solution(mesh):
    placed = (
        P(("groups", "owners", "split"), None),
        P(),
        P(("groups", "owners", "split"), None),
        P(("groups", "owners", "split")),
    )
    return jax.shard_map(
        per_device,
        mesh=mesh,
        in_specs=placed,
        out_specs=P(("groups", "owners", "split")),
        check_vma=False,
    )
```

```python
import functools

import jax
import jax.numpy as jnp
from jax import lax
from jax.experimental import pallas as pl
from jax.experimental.pallas import tpu as pltpu
from jax.sharding import PartitionSpec as P

CPO = 8
LANES = 128
TAG_ROWS = 16
ABSENT = -2.0
STEPS = 8
ROW_PARTS = 4
VMEM_LIMIT = 48 * 1024 * 1024


def project_kernel(source_hbm, basis_hbm, owner_hbm, sub_hbm, packed_ref, *scratch):
    source, basis, owner, sub, sems, tag_sems = scratch
    row_count, depth = source.shape
    width = basis.shape[1]
    spans = cut(depth, STEPS)
    copies = [
        (
            pltpu.make_async_copy(basis_hbm.at[span, :], basis.at[span, :], sems.at[0, step]),
            pltpu.make_async_copy(source_hbm.at[:, span], source.at[:, span], sems.at[1, step]),
        )
        for step, span in enumerate(spans)
    ]
    tag_copies = [
        pltpu.make_async_copy(owner_hbm, owner, tag_sems.at[0]),
        pltpu.make_async_copy(sub_hbm, sub, tag_sems.at[1]),
    ]
    for copy in [copy for pair in copies for copy in pair] + tag_copies:
        copy.start()
    totals = [None] * ROW_PARTS
    for span, pair in zip(spans, copies):
        for copy in pair:
            copy.wait()
        for at, rows in enumerate(cut(row_count, ROW_PARTS)):
            part = jnp.dot(source[rows, span], basis[span, :], preferred_element_type=jnp.float32)
            totals[at] = part if totals[at] is None else totals[at] + part
    for projected, rows in zip(totals, cut(row_count, ROW_PARTS)):
        norms = jnp.sum(projected * projected, axis=1, keepdims=True)
        packed_ref[rows, :] = (projected * lax.rsqrt(norms + 1e-06)).astype(jnp.bfloat16)
    for copy in tag_copies:
        copy.wait()
    tags = (owner[...] * CPO + sub[...] + 1).astype(jnp.float32)
    tags = jnp.concatenate(
        [tags, jnp.zeros((TAG_ROWS - tags.shape[0], LANES), jnp.float32)], axis=0
    )
    tags = jnp.concatenate([tags, jnp.zeros((TAG_ROWS, width - LANES), jnp.float32)], axis=1)
    packed_ref[row_count:, :] = tags.astype(jnp.bfloat16)


def cut(size, steps):
    return [pl.ds(size // steps * step, size // steps) for step in range(steps)]


def project(embeddings, basis, owner_ids, sub_cluster):
    row_count, depth = embeddings.shape
    width = basis.shape[1]
    tag_shape = (row_count // LANES, LANES)
    return pl.pallas_call(
        project_kernel,
        in_specs=[pl.BlockSpec(memory_space=pltpu.HBM)] * 4,
        out_specs=pl.BlockSpec(memory_space=pltpu.VMEM),
        out_shape=jax.ShapeDtypeStruct((row_count + TAG_ROWS, width), jnp.bfloat16),
        scratch_shapes=[
            pltpu.VMEM((row_count, depth), jnp.bfloat16),
            pltpu.VMEM((depth, width), jnp.bfloat16),
            pltpu.VMEM(tag_shape, jnp.int32),
            pltpu.VMEM(tag_shape, jnp.int32),
            pltpu.SemaphoreType.DMA((2, STEPS)),
            pltpu.SemaphoreType.DMA((2,)),
        ],
        compiler_params=pltpu.CompilerParams(vmem_limit_bytes=VMEM_LIMIT),
        cost_estimate=pl.CostEstimate(
            flops=2 * row_count * depth * width,
            bytes_accessed=2 * depth * (row_count + width),
            transcendentals=0,
        ),
    )(
        *[
            pltpu.with_memory_space_constraint(array, pltpu.HBM)
            for array in (
                embeddings,
                basis,
                owner_ids.reshape(tag_shape),
                sub_cluster.reshape(tag_shape),
            )
        ]
    )


def score_kernel(key_parts, row_parts, bases, want_cols, own_first, unread, pass_on, *refs):
    refs = list(refs[unread:])
    pass_refs = [refs.pop() for _ in range(pass_on)]
    key_refs = [refs.pop(0) for _ in range(key_parts)]
    row_refs = [[refs.pop(0) for _ in range(parts)] for parts in row_parts]
    for pass_ref, (row_ref,) in zip(pass_refs, reversed(row_refs)):
        pass_ref[...] = row_ref[...]
    base_refs = [refs.pop(0) for _ in range(bases)]
    col_out = refs.pop(0) if want_cols else None
    row_outs = refs
    key_tag_ref = key_refs[-1]
    key_tags = key_tag_ref[key_tag_ref.shape[0] - TAG_ROWS :, :LANES].astype(jnp.float32)
    tiles = sum(key_ref.shape[0] for key_ref in key_refs) // LANES
    best = [jnp.full((8, LANES), ABSENT, jnp.float32) for _ in range(tiles)]
    for block, part_refs in enumerate(row_refs):
        tag_ref = part_refs[-1]
        row_tags = tag_ref[tag_ref.shape[0] - TAG_ROWS :, :LANES].astype(jnp.float32)
        place = 0
        for part_ref in part_refs:
            count = part_ref.shape[0] // LANES * LANES
            scores = [
                lax.dot_general(
                    part_ref[:count, :],
                    key_ref[: key_ref.shape[0] // LANES * LANES, :],
                    (((1,), (1,)), ((), ())),
                    preferred_element_type=jnp.float32,
                )
                for key_ref in key_refs
            ]
            scores = [
                part[:, start : start + LANES]
                for part in scores
                for start in range(0, part.shape[1], LANES)
            ]
            for start in range(0, count, LANES):
                tags = jnp.broadcast_to(row_tags[place : place + 1, :], (LANES, LANES)).T
                across = None
                for at in range(tiles):
                    same = tags == key_tags[at : at + 1, :]
                    if own_first and block == 0 and at == place:
                        same = same & (
                            lax.broadcasted_iota(jnp.int32, (LANES, LANES), 0)
                            != lax.broadcasted_iota(jnp.int32, (LANES, LANES), 1)
                        )
                    kept = jnp.where(same, scores[at][start : start + LANES, :], ABSENT)
                    if want_cols or own_first:
                        best[at] = jnp.maximum(
                            best[at], jnp.max(kept.reshape(LANES // 8, 8, LANES), axis=0)
                        )
                    if not own_first:
                        across = kept if across is None else jnp.maximum(across, kept)
                if not own_first:
                    at = block % 2 * tiles + place
                    found = jnp.max(across.T, axis=0, keepdims=True)
                    if base_refs:
                        found = jnp.maximum(found, base_refs[block // 2][at : at + 1, :])
                    row_outs[block // 2][at : at + 1, :] = found
                place += 1
    for at in range(tiles):
        found = jnp.max(best[at], axis=0, keepdims=True)
        if want_cols:
            col_out[at : at + 1, :] = found
        if own_first:
            for base_ref in base_refs:
                found = jnp.maximum(found, base_ref[at : at + 1, :])
            row_outs[0][at : at + 1, :] = found
    if own_first:
        row_outs[0][tiles:, :] = base_refs[0][tiles:, :]


def score(key, rows, bases=(), want_cols=True, own_first=False, after=(), pass_on=0):
    whole = lambda block: block if isinstance(block, tuple) else (block,)
    key, parts = whole(key), [whole(row) for row in rows]
    blocks = [part for row in parts for part in row]
    tiles = sum(part.shape[0] for part in key) // LANES
    best = jax.ShapeDtypeStruct((tiles, LANES), jnp.float32)
    pair = jax.ShapeDtypeStruct((2 * tiles, LANES), jnp.float32)
    out_shape = [best] * want_cols + [pair] * (1 if own_first else len(rows) // 2)
    passed = blocks[len(blocks) - pass_on :]
    out_shape += [jax.ShapeDtypeStruct(block.shape, block.dtype) for block in passed]
    inside = pl.BlockSpec(memory_space=pltpu.VMEM)
    found = pl.pallas_call(
        functools.partial(
            score_kernel,
            len(key),
            [len(row) for row in parts],
            len(bases),
            want_cols,
            own_first,
            len(after),
            pass_on,
        ),
        in_specs=[pl.BlockSpec(memory_space=pl.ANY)] * len(after)
        + [inside] * (len(key) + len(blocks) + len(bases)),
        out_specs=[inside] * len(out_shape),
        out_shape=out_shape,
        compiler_params=pltpu.CompilerParams(vmem_limit_bytes=VMEM_LIMIT),
        cost_estimate=pl.CostEstimate(flops=0, bytes_accessed=0, transcendentals=0),
    )(*after, *key, *blocks, *bases)
    best, passed = found[: len(found) - pass_on], found[len(found) - pass_on :]
    return list(best[:want_cols]), list(best[want_cols:]), list(passed)


def owner_steps(count):
    half = count // 2
    circle = [count - 1 - 2 * i for i in range(half)] + [count - 2 - 2 * i for i in range(half)]
    return [
        [(circle[(i + step) % count], circle[i]) for i in range(count)]
        for step in range(1, half + 1)
    ]


def per_device(embeddings, basis, owner_ids, sub_cluster):
    row_count = embeddings.shape[0]
    tiles = row_count // LANES
    split_count, owner_count = lax.axis_size("split"), lax.axis_size("owners")

    def swap(block, offset):
        return lax.ppermute(block, "split", [(s, s ^ offset) for s in range(split_count)])

    def halves(block):
        return block[: row_count // 2], block[row_count // 2 :]

    own = project(embeddings, basis, owner_ids, sub_cluster)
    *steps, last = owner_steps(owner_count)
    keys = [lax.ppermute(own, "owners", step) for step in steps]
    nearby = lax.ppermute(own, "owners", last)
    offsets = range(2, split_count, 2)

    def gather_split(block):
        besides = [swap(block, offset) for offset in offsets]
        return [part for beside in besides for part in (beside, swap(beside, 1))]

    gathered = lax.cond(
        lax.axis_index("groups") < 1 << 16,
        gather_split,
        lambda block: [block] * (2 * len(offsets)),
        own,
    )
    rows = [own, swap(own, 1), *gathered]
    _, row_best, rows[2:] = score(nearby, rows, want_cols=False, pass_on=len(gathered))
    backs = []
    for key, step in zip(keys, steps):
        (found,), row_best, _ = score(key, rows, row_best)
        backs.append(lax.ppermute(found, "owners", [(b, a) for a, b in step]))
    others = [swap(found, 2 * at) for at, found in enumerate(row_best) if at]
    _, (local,), _ = score(
        own, rows, row_best[:1], want_cols=False, own_first=True, after=[*keys, nearby]
    )
    for other in others:
        local = jnp.maximum(local, other)
    best = jnp.maximum(local[:tiles], swap(local[tiles:], 1))
    for back in backs:
        best = jnp.maximum(best, back)
    return jnp.maximum(best, -1.0).reshape(row_count)


def solution(mesh):
    placed = (
        P(("groups", "owners", "split"), None),
        P(),
        P(("groups", "owners", "split"), None),
        P(("groups", "owners", "split")),
    )
    return jax.shard_map(
        per_device,
        mesh=mesh,
        in_specs=placed,
        out_specs=P(("groups", "owners", "split")),
        check_vma=False,
    )
```

```python
import functools

import jax
import jax.numpy as jnp
from jax import lax
from jax.experimental import pallas as pl
from jax.experimental.pallas import tpu as pltpu
from jax.sharding import PartitionSpec as P

CPO = 8
LANES = 128
TAG_ROWS = 16
ABSENT = -2.0
STEPS = 8
ROW_PARTS = 4
VMEM_LIMIT = 48 * 1024 * 1024


def project_kernel(source_hbm, basis_hbm, owner_hbm, sub_hbm, packed_ref, *scratch):
    source, basis, owner, sub, sems, tag_sems = scratch
    row_count, depth = source.shape
    width = basis.shape[1]
    spans = cut(depth, STEPS)
    copies = [
        (
            pltpu.make_async_copy(basis_hbm.at[span, :], basis.at[span, :], sems.at[0, step]),
            pltpu.make_async_copy(source_hbm.at[:, span], source.at[:, span], sems.at[1, step]),
        )
        for step, span in enumerate(spans)
    ]
    tag_copies = [
        pltpu.make_async_copy(owner_hbm, owner, tag_sems.at[0]),
        pltpu.make_async_copy(sub_hbm, sub, tag_sems.at[1]),
    ]
    for copy in [copy for pair in copies for copy in pair] + tag_copies:
        copy.start()
    totals = [None] * ROW_PARTS
    for span, pair in zip(spans, copies):
        for copy in pair:
            copy.wait()
        for at, rows in enumerate(cut(row_count, ROW_PARTS)):
            part = jnp.dot(source[rows, span], basis[span, :], preferred_element_type=jnp.float32)
            totals[at] = part if totals[at] is None else totals[at] + part
    for projected, rows in zip(totals, cut(row_count, ROW_PARTS)):
        norms = jnp.sum(projected * projected, axis=1, keepdims=True)
        packed_ref[rows, :] = (projected * lax.rsqrt(norms + 1e-06)).astype(jnp.bfloat16)
    for copy in tag_copies:
        copy.wait()
    tags = (owner[...] * CPO + sub[...] + 1).astype(jnp.float32)
    tags = jnp.concatenate(
        [tags, jnp.zeros((TAG_ROWS - tags.shape[0], LANES), jnp.float32)], axis=0
    )
    tags = jnp.concatenate([tags, jnp.zeros((TAG_ROWS, width - LANES), jnp.float32)], axis=1)
    packed_ref[row_count:, :] = tags.astype(jnp.bfloat16)


def cut(size, steps):
    return [pl.ds(size // steps * step, size // steps) for step in range(steps)]


def project(embeddings, basis, owner_ids, sub_cluster):
    row_count, depth = embeddings.shape
    width = basis.shape[1]
    tag_shape = (row_count // LANES, LANES)
    return pl.pallas_call(
        project_kernel,
        in_specs=[pl.BlockSpec(memory_space=pltpu.HBM)] * 4,
        out_specs=pl.BlockSpec(memory_space=pltpu.VMEM),
        out_shape=jax.ShapeDtypeStruct((row_count + TAG_ROWS, width), jnp.bfloat16),
        scratch_shapes=[
            pltpu.VMEM((row_count, depth), jnp.bfloat16),
            pltpu.VMEM((depth, width), jnp.bfloat16),
            pltpu.VMEM(tag_shape, jnp.int32),
            pltpu.VMEM(tag_shape, jnp.int32),
            pltpu.SemaphoreType.DMA((2, STEPS)),
            pltpu.SemaphoreType.DMA((2,)),
        ],
        compiler_params=pltpu.CompilerParams(vmem_limit_bytes=VMEM_LIMIT),
        cost_estimate=pl.CostEstimate(
            flops=2 * row_count * depth * width,
            bytes_accessed=2 * depth * (row_count + width),
            transcendentals=0,
        ),
    )(
        *[
            pltpu.with_memory_space_constraint(array, pltpu.HBM)
            for array in (
                embeddings,
                basis,
                owner_ids.reshape(tag_shape),
                sub_cluster.reshape(tag_shape),
            )
        ]
    )


def score_kernel(key_parts, row_parts, bases, want_cols, own_first, unread, *refs):
    refs = list(refs[unread:])
    key_refs = [refs.pop(0) for _ in range(key_parts)]
    row_refs = [[refs.pop(0) for _ in range(parts)] for parts in row_parts]
    base_refs = [refs.pop(0) for _ in range(bases)]
    col_out = refs.pop(0) if want_cols else None
    row_outs = refs
    key_tag_ref = key_refs[-1]
    key_tags = key_tag_ref[key_tag_ref.shape[0] - TAG_ROWS :, :LANES].astype(jnp.float32)
    tiles = sum(key_ref.shape[0] for key_ref in key_refs) // LANES
    best = [jnp.full((8, LANES), ABSENT, jnp.float32) for _ in range(tiles)]
    for block, part_refs in enumerate(row_refs):
        tag_ref = part_refs[-1]
        row_tags = tag_ref[tag_ref.shape[0] - TAG_ROWS :, :LANES].astype(jnp.float32)
        place = 0
        for part_ref in part_refs:
            count = part_ref.shape[0] // LANES * LANES
            scores = [
                lax.dot_general(
                    part_ref[:count, :],
                    key_ref[: key_ref.shape[0] // LANES * LANES, :],
                    (((1,), (1,)), ((), ())),
                    preferred_element_type=jnp.float32,
                )
                for key_ref in key_refs
            ]
            scores = [
                part[:, start : start + LANES]
                for part in scores
                for start in range(0, part.shape[1], LANES)
            ]
            for start in range(0, count, LANES):
                tags = jnp.broadcast_to(row_tags[place : place + 1, :], (LANES, LANES)).T
                across = None
                for at in range(tiles):
                    same = tags == key_tags[at : at + 1, :]
                    if own_first and block == 0 and at == place:
                        same = same & (
                            lax.broadcasted_iota(jnp.int32, (LANES, LANES), 0)
                            != lax.broadcasted_iota(jnp.int32, (LANES, LANES), 1)
                        )
                    kept = jnp.where(same, scores[at][start : start + LANES, :], ABSENT)
                    if want_cols or own_first:
                        best[at] = jnp.maximum(
                            best[at], jnp.max(kept.reshape(LANES // 8, 8, LANES), axis=0)
                        )
                    if not own_first:
                        across = kept if across is None else jnp.maximum(across, kept)
                if not own_first:
                    at = block % 2 * tiles + place
                    found = jnp.max(across.T, axis=0, keepdims=True)
                    if base_refs:
                        found = jnp.maximum(found, base_refs[block // 2][at : at + 1, :])
                    row_outs[block // 2][at : at + 1, :] = found
                place += 1
    for at in range(tiles):
        found = jnp.max(best[at], axis=0, keepdims=True)
        if want_cols:
            col_out[at : at + 1, :] = found
        if own_first:
            for base_ref in base_refs:
                found = jnp.maximum(found, base_ref[at : at + 1, :])
            row_outs[0][at : at + 1, :] = found
    if own_first:
        row_outs[0][tiles:, :] = base_refs[0][tiles:, :]


def score(key, rows, bases=(), want_cols=True, own_first=False, after=()):
    whole = lambda block: block if isinstance(block, tuple) else (block,)
    key, parts = whole(key), [whole(row) for row in rows]
    blocks = [part for row in parts for part in row]
    tiles = sum(part.shape[0] for part in key) // LANES
    best = jax.ShapeDtypeStruct((tiles, LANES), jnp.float32)
    pair = jax.ShapeDtypeStruct((2 * tiles, LANES), jnp.float32)
    out_shape = [best] * want_cols + [pair] * (1 if own_first else len(rows) // 2)
    inside = pl.BlockSpec(memory_space=pltpu.VMEM)
    found = pl.pallas_call(
        functools.partial(
            score_kernel,
            len(key),
            [len(row) for row in parts],
            len(bases),
            want_cols,
            own_first,
            len(after),
        ),
        in_specs=[pl.BlockSpec(memory_space=pl.ANY)] * len(after)
        + [inside] * (len(key) + len(blocks) + len(bases)),
        out_specs=[inside] * len(out_shape),
        out_shape=out_shape,
        compiler_params=pltpu.CompilerParams(vmem_limit_bytes=VMEM_LIMIT),
        cost_estimate=pl.CostEstimate(flops=0, bytes_accessed=0, transcendentals=0),
    )(*after, *key, *blocks, *bases)
    return list(found[:want_cols]), list(found[want_cols:])


def owner_steps(count):
    half = count // 2
    circle = [count - 1 - 2 * i for i in range(half)] + [count - 2 - 2 * i for i in range(half)]
    return [
        [(circle[(i + step) % count], circle[i]) for i in range(count)]
        for step in range(1, half + 1)
    ]


def per_device(embeddings, basis, owner_ids, sub_cluster):
    row_count = embeddings.shape[0]
    tiles = row_count // LANES
    split_count, owner_count = lax.axis_size("split"), lax.axis_size("owners")

    def swap(block, offset):
        return lax.ppermute(block, "split", [(s, s ^ offset) for s in range(split_count)])

    def halves(block):
        return block[: row_count // 2], block[row_count // 2 :]

    own = project(embeddings, basis, owner_ids, sub_cluster)
    *steps, last = owner_steps(owner_count)
    keys = [lax.ppermute(own, "owners", step) for step in steps]
    nearby = tuple(lax.ppermute(part, "owners", last) for part in halves(own))
    offsets = range(2, split_count, 2)
    besides = lax.fori_loop(
        0,
        1 + (lax.axis_index("groups") >> 16),
        lambda _, blocks: [swap(block, offset) for block, offset in zip(blocks, offsets)],
        [own] * len(offsets),
    )
    rows = [own, swap(own, 1)]
    for beside in besides:
        rows += [beside, tuple(swap(part, 1) for part in halves(beside))]
    _, row_best = score(nearby, rows, want_cols=False)
    backs = []
    for key, step in zip(keys, steps):
        (found,), row_best = score(key, rows, row_best)
        backs.append(lax.ppermute(found, "owners", [(b, a) for a, b in step]))
    others = [swap(found, 2 * at) for at, found in enumerate(row_best) if at]
    _, (local,) = score(
        own, rows, row_best[:1], want_cols=False, own_first=True, after=[*keys, *nearby]
    )
    for other in others:
        local = jnp.maximum(local, other)
    best = jnp.maximum(local[:tiles], swap(local[tiles:], 1))
    for back in backs:
        best = jnp.maximum(best, back)
    return jnp.maximum(best, -1.0).reshape(row_count)


def solution(mesh):
    placed = (
        P(("groups", "owners", "split"), None),
        P(),
        P(("groups", "owners", "split"), None),
        P(("groups", "owners", "split")),
    )
    return jax.shard_map(
        per_device,
        mesh=mesh,
        in_specs=placed,
        out_specs=P(("groups", "owners", "split")),
        check_vma=False,
    )
```

```python
import functools

import jax
import jax.numpy as jnp
from jax import lax
from jax.experimental import pallas as pl
from jax.experimental.pallas import tpu as pltpu
from jax.sharding import PartitionSpec as P

CPO = 8
LANES = 128
TAG_ROWS = 16
ABSENT = -2.0
STEPS = 8
ROW_PARTS = 4
VMEM_LIMIT = 48 * 1024 * 1024


def project_kernel(source_hbm, basis_hbm, owner_hbm, sub_hbm, packed_ref, *scratch):
    source, basis, owner, sub, sems, tag_sems = scratch
    row_count, depth = source.shape
    width = basis.shape[1]
    spans = cut(depth, STEPS)
    copies = [
        (
            pltpu.make_async_copy(basis_hbm.at[span, :], basis.at[span, :], sems.at[0, step]),
            pltpu.make_async_copy(source_hbm.at[:, span], source.at[:, span], sems.at[1, step]),
        )
        for step, span in enumerate(spans)
    ]
    tag_copies = [
        pltpu.make_async_copy(owner_hbm, owner, tag_sems.at[0]),
        pltpu.make_async_copy(sub_hbm, sub, tag_sems.at[1]),
    ]
    for copy in [copy for pair in copies for copy in pair] + tag_copies:
        copy.start()
    totals = [None] * ROW_PARTS
    for span, pair in zip(spans, copies):
        for copy in pair:
            copy.wait()
        for at, rows in enumerate(cut(row_count, ROW_PARTS)):
            part = jnp.dot(source[rows, span], basis[span, :], preferred_element_type=jnp.float32)
            totals[at] = part if totals[at] is None else totals[at] + part
    for projected, rows in zip(totals, cut(row_count, ROW_PARTS)):
        norms = jnp.sum(projected * projected, axis=1, keepdims=True)
        packed_ref[rows, :] = (projected * lax.rsqrt(norms + 1e-06)).astype(jnp.bfloat16)
    for copy in tag_copies:
        copy.wait()
    tags = (owner[...] * CPO + sub[...] + 1).astype(jnp.float32)
    tags = jnp.concatenate(
        [tags, jnp.zeros((TAG_ROWS - tags.shape[0], LANES), jnp.float32)], axis=0
    )
    tags = jnp.concatenate([tags, jnp.zeros((TAG_ROWS, width - LANES), jnp.float32)], axis=1)
    packed_ref[row_count:, :] = tags.astype(jnp.bfloat16)


def cut(size, steps):
    return [pl.ds(size // steps * step, size // steps) for step in range(steps)]


def project(embeddings, basis, owner_ids, sub_cluster):
    row_count, depth = embeddings.shape
    width = basis.shape[1]
    tag_shape = (row_count // LANES, LANES)
    return pl.pallas_call(
        project_kernel,
        in_specs=[pl.BlockSpec(memory_space=pltpu.HBM)] * 4,
        out_specs=pl.BlockSpec(memory_space=pltpu.VMEM),
        out_shape=jax.ShapeDtypeStruct((row_count + TAG_ROWS, width), jnp.bfloat16),
        scratch_shapes=[
            pltpu.VMEM((row_count, depth), jnp.bfloat16),
            pltpu.VMEM((depth, width), jnp.bfloat16),
            pltpu.VMEM(tag_shape, jnp.int32),
            pltpu.VMEM(tag_shape, jnp.int32),
            pltpu.SemaphoreType.DMA((2, STEPS)),
            pltpu.SemaphoreType.DMA((2,)),
        ],
        compiler_params=pltpu.CompilerParams(vmem_limit_bytes=VMEM_LIMIT),
        cost_estimate=pl.CostEstimate(
            flops=2 * row_count * depth * width,
            bytes_accessed=2 * depth * (row_count + width),
            transcendentals=0,
        ),
    )(
        *[
            pltpu.with_memory_space_constraint(array, pltpu.HBM)
            for array in (
                embeddings,
                basis,
                owner_ids.reshape(tag_shape),
                sub_cluster.reshape(tag_shape),
            )
        ]
    )


def score_kernel(key_count, cols, row_parts, own_first, unread, *refs):
    refs = list(refs[unread:])
    key_refs = [refs.pop(0) for _ in range(key_count)]
    row_refs = [[refs.pop(0) for _ in range(parts)] for parts in row_parts]
    base_ref = refs.pop(0) if own_first else None
    col_refs = [refs.pop(0) for _ in range(cols)]
    row_outs = refs
    row_count = key_refs[0].shape[0] - TAG_ROWS
    tiles = row_count // LANES
    best = [
        [jnp.full((8, LANES), ABSENT, jnp.float32) for _ in range(tiles)]
        for _ in range(key_count if own_first else cols)
    ]
    for block, part_refs in enumerate(row_refs):
        tag_ref = part_refs[-1]
        row_tags = tag_ref[tag_ref.shape[0] - TAG_ROWS :, :LANES].astype(jnp.float32)
        place = 0
        for part_ref in part_refs:
            count = part_ref.shape[0] // LANES * LANES
            tags = [
                jnp.broadcast_to(row_tags[at : at + 1, :], (LANES, LANES)).T
                for at in range(place, place + count // LANES)
            ]
            across = [None] * len(tags)
            for key, key_ref in enumerate(key_refs):
                key_tags = key_ref[row_count:, :LANES].astype(jnp.float32)
                scores = lax.dot_general(
                    part_ref[:count, :],
                    key_ref[:row_count, :],
                    (((1,), (1,)), ((), ())),
                    preferred_element_type=jnp.float32,
                )
                for tile, tag in enumerate(tags):
                    for at in range(tiles):
                        same = tag == key_tags[at : at + 1, :]
                        if own_first and block == 0 and at == place + tile:
                            same = same & (
                                lax.broadcasted_iota(jnp.int32, (LANES, LANES), 0)
                                != lax.broadcasted_iota(jnp.int32, (LANES, LANES), 1)
                            )
                        kept = scores[
                            tile * LANES : (tile + 1) * LANES, at * LANES : (at + 1) * LANES
                        ]
                        kept = jnp.where(same, kept, ABSENT)
                        if key < len(best):
                            best[key][at] = jnp.maximum(
                                best[key][at], jnp.max(kept.reshape(LANES // 8, 8, LANES), axis=0)
                            )
                        if not own_first:
                            across[tile] = (
                                kept if across[tile] is None else jnp.maximum(across[tile], kept)
                            )
            if not own_first:
                for tile in range(len(tags)):
                    at = block % 2 * tiles + place + tile
                    found = jnp.max(across[tile].T, axis=0, keepdims=True)
                    row_outs[block // 2][at : at + 1, :] = found
            place += len(tags)
    for key, found in enumerate(best):
        for at in range(tiles):
            highest = jnp.max(found[at], axis=0, keepdims=True)
            if own_first:
                row_outs[0][at : at + 1, :] = jnp.maximum(highest, base_ref[at : at + 1, :])
            else:
                col_refs[key][at : at + 1, :] = highest
    if own_first:
        row_outs[0][tiles:, :] = base_ref[tiles:, :]


def score(keys, rows, cols=0, base=None, after=()):
    parts = [row if isinstance(row, tuple) else (row,) for row in rows]
    operands = [*keys, *(part for row in parts for part in row)]
    operands += [] if base is None else [base]
    tiles = keys[0].shape[0] // LANES
    best = jax.ShapeDtypeStruct((tiles, LANES), jnp.float32)
    pair = jax.ShapeDtypeStruct((2 * tiles, LANES), jnp.float32)
    out_shape = [best] * cols + [pair] * (len(rows) // 2 if base is None else 1)
    inside = pl.BlockSpec(memory_space=pltpu.VMEM)
    found = pl.pallas_call(
        functools.partial(
            score_kernel,
            len(keys),
            cols,
            [len(row) for row in parts],
            base is not None,
            len(after),
        ),
        in_specs=[pl.BlockSpec(memory_space=pl.ANY)] * len(after) + [inside] * len(operands),
        out_specs=[inside] * len(out_shape),
        out_shape=out_shape,
        compiler_params=pltpu.CompilerParams(vmem_limit_bytes=VMEM_LIMIT),
        cost_estimate=pl.CostEstimate(flops=0, bytes_accessed=0, transcendentals=0),
    )(*after, *operands)
    return list(found[:cols]), list(found[cols:])


def owner_steps(count):
    half = count // 2
    circle = [count - 1 - 2 * i for i in range(half)] + [count - 2 - 2 * i for i in range(half)]
    return [
        [(circle[(i + step) % count], circle[i]) for i in range(count)]
        for step in range(1, half + 1)
    ]


def per_device(embeddings, basis, owner_ids, sub_cluster):
    row_count = embeddings.shape[0]
    tiles = row_count // LANES
    split_count, owner_count = lax.axis_size("split"), lax.axis_size("owners")

    def swap(block, offset):
        return lax.ppermute(block, "split", [(s, s ^ offset) for s in range(split_count)])

    def halves(block):
        return block[: row_count // 2], block[row_count // 2 :]

    own = project(embeddings, basis, owner_ids, sub_cluster)
    *steps, last = owner_steps(owner_count)
    keys = [lax.ppermute(own, "owners", step) for step in steps]
    nearby = lax.ppermute(own, "owners", last)
    offsets = range(2, split_count, 2)
    besides = lax.fori_loop(
        0,
        1 + (lax.axis_index("groups") >> 16),
        lambda _, blocks: [swap(block, offset) for block, offset in zip(blocks, offsets)],
        [own] * len(offsets),
    )
    rows = [own, swap(own, 1)]
    for beside in besides:
        rows += [beside, tuple(swap(part, 1) for part in halves(beside))]
    col_best, row_best = score([*keys, nearby], rows, cols=len(keys))
    backs = [
        lax.ppermute(found, "owners", [(b, a) for a, b in step])
        for found, step in zip(col_best, steps)
    ]
    others = [swap(found, 2 * at) for at, found in enumerate(row_best) if at]
    _, (local,) = score([own], rows, base=row_best[0], after=[nearby, *keys])
    for other in others:
        local = jnp.maximum(local, other)
    best = jnp.maximum(local[:tiles], swap(local[tiles:], 1))
    for back in backs:
        best = jnp.maximum(best, back)
    return jnp.maximum(best, -1.0).reshape(row_count)


def solution(mesh):
    placed = (
        P(("groups", "owners", "split"), None),
        P(),
        P(("groups", "owners", "split"), None),
        P(("groups", "owners", "split")),
    )
    return jax.shard_map(
        per_device,
        mesh=mesh,
        in_specs=placed,
        out_specs=P(("groups", "owners", "split")),
        check_vma=False,
    )
```

```python
import functools

import jax
import jax.numpy as jnp
from jax import lax
from jax.experimental import pallas as pl
from jax.experimental.pallas import tpu as pltpu
from jax.sharding import PartitionSpec as P

CPO = 8
LANES = 128
TAG_ROWS = 16
ABSENT = -2.0
STEPS = 8
ROW_PARTS = 4
VMEM_LIMIT = 48 * 1024 * 1024


def project_kernel(source_hbm, basis_hbm, owner_hbm, sub_hbm, packed_ref, *scratch):
    source, basis, owner, sub, sems, tag_sems = scratch
    row_count, depth = source.shape
    width = basis.shape[1]
    spans = cut(depth, STEPS)
    copies = [
        (
            pltpu.make_async_copy(basis_hbm.at[span, :], basis.at[span, :], sems.at[0, step]),
            pltpu.make_async_copy(source_hbm.at[:, span], source.at[:, span], sems.at[1, step]),
        )
        for step, span in enumerate(spans)
    ]
    tag_copies = [
        pltpu.make_async_copy(owner_hbm, owner, tag_sems.at[0]),
        pltpu.make_async_copy(sub_hbm, sub, tag_sems.at[1]),
    ]
    for copy in [copy for pair in copies for copy in pair] + tag_copies:
        copy.start()
    totals = [None] * ROW_PARTS
    for span, pair in zip(spans, copies):
        for copy in pair:
            copy.wait()
        for at, rows in enumerate(cut(row_count, ROW_PARTS)):
            part = jnp.dot(source[rows, span], basis[span, :], preferred_element_type=jnp.float32)
            totals[at] = part if totals[at] is None else totals[at] + part
    for projected, rows in zip(totals, cut(row_count, ROW_PARTS)):
        norms = jnp.sum(projected * projected, axis=1, keepdims=True)
        packed_ref[rows, :] = (projected * lax.rsqrt(norms + 1e-06)).astype(jnp.bfloat16)
    for copy in tag_copies:
        copy.wait()
    tags = (owner[...] * CPO + sub[...] + 1).astype(jnp.float32)
    tags = jnp.concatenate(
        [tags, jnp.zeros((TAG_ROWS - tags.shape[0], LANES), jnp.float32)], axis=0
    )
    tags = jnp.concatenate([tags, jnp.zeros((TAG_ROWS, width - LANES), jnp.float32)], axis=1)
    packed_ref[row_count:, :] = tags.astype(jnp.bfloat16)


def cut(size, steps):
    return [pl.ds(size // steps * step, size // steps) for step in range(steps)]


def project(embeddings, basis, owner_ids, sub_cluster):
    row_count, depth = embeddings.shape
    width = basis.shape[1]
    tag_shape = (row_count // LANES, LANES)
    return pl.pallas_call(
        project_kernel,
        in_specs=[pl.BlockSpec(memory_space=pltpu.HBM)] * 4,
        out_specs=pl.BlockSpec(memory_space=pltpu.VMEM),
        out_shape=jax.ShapeDtypeStruct((row_count + TAG_ROWS, width), jnp.bfloat16),
        scratch_shapes=[
            pltpu.VMEM((row_count, depth), jnp.bfloat16),
            pltpu.VMEM((depth, width), jnp.bfloat16),
            pltpu.VMEM(tag_shape, jnp.int32),
            pltpu.VMEM(tag_shape, jnp.int32),
            pltpu.SemaphoreType.DMA((2, STEPS)),
            pltpu.SemaphoreType.DMA((2,)),
        ],
        compiler_params=pltpu.CompilerParams(vmem_limit_bytes=VMEM_LIMIT),
        cost_estimate=pl.CostEstimate(
            flops=2 * row_count * depth * width,
            bytes_accessed=2 * depth * (row_count + width),
            transcendentals=0,
        ),
    )(
        *[
            pltpu.with_memory_space_constraint(array, pltpu.HBM)
            for array in (
                embeddings,
                basis,
                owner_ids.reshape(tag_shape),
                sub_cluster.reshape(tag_shape),
            )
        ]
    )


def score_kernel(key_count, cols, row_parts, known, own_first, *refs):
    refs = list(refs)
    key_refs = [refs.pop(0) for _ in range(key_count)]
    row_refs = [[refs.pop(0) for _ in range(parts)] for parts in row_parts]
    known_refs = [refs.pop(0) for _ in range(known)]
    base_ref = refs.pop(0) if own_first else None
    col_refs = [refs.pop(0) for _ in range(cols)]
    row_outs = refs
    row_count = key_refs[0].shape[0] - TAG_ROWS
    tiles = row_count // LANES
    best = [
        [jnp.full((8, LANES), ABSENT, jnp.float32) for _ in range(tiles)]
        for _ in range(key_count if own_first else cols)
    ]
    for block, part_refs in enumerate(row_refs):
        tag_ref = part_refs[-1]
        row_tags = tag_ref[tag_ref.shape[0] - TAG_ROWS :, :LANES].astype(jnp.float32)
        place = 0
        for part_ref in part_refs:
            count = part_ref.shape[0] // LANES * LANES
            tags = [
                jnp.broadcast_to(row_tags[at : at + 1, :], (LANES, LANES)).T
                for at in range(place, place + count // LANES)
            ]
            across = [None] * len(tags)
            for key, key_ref in enumerate(key_refs):
                key_tags = key_ref[row_count:, :LANES].astype(jnp.float32)
                scores = lax.dot_general(
                    part_ref[:count, :],
                    key_ref[:row_count, :],
                    (((1,), (1,)), ((), ())),
                    preferred_element_type=jnp.float32,
                )
                for tile, tag in enumerate(tags):
                    for at in range(tiles):
                        same = tag == key_tags[at : at + 1, :]
                        if own_first and block == 0 and at == place + tile:
                            same = same & (
                                lax.broadcasted_iota(jnp.int32, (LANES, LANES), 0)
                                != lax.broadcasted_iota(jnp.int32, (LANES, LANES), 1)
                            )
                        kept = scores[
                            tile * LANES : (tile + 1) * LANES, at * LANES : (at + 1) * LANES
                        ]
                        kept = jnp.where(same, kept, ABSENT)
                        if key < len(best):
                            best[key][at] = jnp.maximum(
                                best[key][at], jnp.max(kept.reshape(LANES // 8, 8, LANES), axis=0)
                            )
                        if not own_first:
                            across[tile] = (
                                kept if across[tile] is None else jnp.maximum(across[tile], kept)
                            )
            if not own_first:
                for tile in range(len(tags)):
                    at = block % 2 * tiles + place + tile
                    found = jnp.max(across[tile].T, axis=0, keepdims=True)
                    if known_refs:
                        found = jnp.maximum(found, known_refs[block // 2][at : at + 1, :])
                    row_outs[block // 2][at : at + 1, :] = found
            place += len(tags)
    for key, found in enumerate(best):
        for at in range(tiles):
            highest = jnp.max(found[at], axis=0, keepdims=True)
            if own_first:
                row_outs[0][at : at + 1, :] = jnp.maximum(highest, base_ref[at : at + 1, :])
            else:
                col_refs[key][at : at + 1, :] = highest
    if own_first:
        row_outs[0][tiles:, :] = base_ref[tiles:, :]


def score(keys, rows, cols=0, known=(), base=None):
    parts = [row if isinstance(row, tuple) else (row,) for row in rows]
    operands = [*keys, *(part for row in parts for part in row)]
    operands += known if base is None else [base]
    tiles = keys[0].shape[0] // LANES
    best = jax.ShapeDtypeStruct((tiles, LANES), jnp.float32)
    pair = jax.ShapeDtypeStruct((2 * tiles, LANES), jnp.float32)
    out_shape = [best] * cols + [pair] * (len(rows) // 2 if base is None else 1)
    inside = pl.BlockSpec(memory_space=pltpu.VMEM)
    found = pl.pallas_call(
        functools.partial(
            score_kernel,
            len(keys),
            cols,
            [len(row) for row in parts],
            len(known),
            base is not None,
        ),
        in_specs=[inside] * len(operands),
        out_specs=[inside] * len(out_shape),
        out_shape=out_shape,
        compiler_params=pltpu.CompilerParams(vmem_limit_bytes=VMEM_LIMIT),
        cost_estimate=pl.CostEstimate(flops=0, bytes_accessed=0, transcendentals=0),
    )(*operands)
    return list(found[:cols]), list(found[cols:])


def owner_steps(count):
    half = count // 2
    circle = [count - 1 - 2 * i for i in range(half)] + [count - 2 - 2 * i for i in range(half)]
    return [
        [(circle[i], circle[(i + step) % count]) for i in range(count)]
        for step in range(1, half + 1)
    ]


def per_device(embeddings, basis, owner_ids, sub_cluster):
    row_count = embeddings.shape[0]
    tiles = row_count // LANES
    split_count, owner_count = lax.axis_size("split"), lax.axis_size("owners")

    def swap(block, offset):
        return lax.ppermute(block, "split", [(s, s ^ offset) for s in range(split_count)])

    def halves(block):
        return block[: row_count // 2], block[row_count // 2 :]

    own = project(embeddings, basis, owner_ids, sub_cluster)
    *steps, last = owner_steps(owner_count)
    keys = [lax.ppermute(own, "owners", step) for step in steps]
    nearby = lax.ppermute(own, "owners", last)
    offsets = range(2, split_count, 2)
    one_turn = 1 + (lax.axis_index("groups") >> 16)
    besides = lax.fori_loop(
        0,
        one_turn,
        lambda _, blocks: [swap(block, offset) for block, offset in zip(blocks, offsets)],
        [own] * len(offsets),
    )
    rows = [own, swap(own, 1)]
    for beside in besides:
        rows += [beside, tuple(swap(part, 1) for part in halves(beside))]
    _, row_best = score([nearby], rows)
    backs = []
    for key, step in zip(keys, steps):
        (found,), row_best = score([key], rows, cols=1, known=row_best)
        backs.append(lax.ppermute(found, "owners", [(b, a) for a, b in step]))

    def exchange_split(_, carried):
        (first, *more), _ = carried
        more = [swap(found, offset) for found, offset in zip(more, offsets)]
        _, (local,) = score([own], rows, base=first)
        for other in more:
            local = jnp.maximum(local, other)
        return [local, *more], jnp.maximum(local[:tiles], swap(local[tiles:], 1))

    _, best = lax.fori_loop(0, one_turn, exchange_split, (row_best, row_best[0][:tiles]))
    for back in backs:
        best = jnp.maximum(best, back)
    return jnp.maximum(best, -1.0).reshape(row_count)


def solution(mesh):
    placed = (
        P(("groups", "owners", "split"), None),
        P(),
        P(("groups", "owners", "split"), None),
        P(("groups", "owners", "split")),
    )
    return jax.shard_map(
        per_device,
        mesh=mesh,
        in_specs=placed,
        out_specs=P(("groups", "owners", "split")),
        check_vma=False,
    )
```

```python
import functools

import jax
import jax.numpy as jnp
from jax import lax
from jax.experimental import pallas as pl
from jax.experimental.pallas import tpu as pltpu
from jax.sharding import PartitionSpec as P

CPO = 8
LANES = 128
TAG_ROWS = 16
ABSENT = -2.0
STEPS = 8
ROW_PARTS = 4
VMEM_LIMIT = 48 * 1024 * 1024


def project_kernel(source_hbm, basis_hbm, owner_hbm, sub_hbm, packed_ref, *scratch):
    source, basis, owner, sub, sems, tag_sems = scratch
    row_count, depth = source.shape
    width = basis.shape[1]
    spans = cut(depth, STEPS)
    copies = [
        (
            pltpu.make_async_copy(basis_hbm.at[span, :], basis.at[span, :], sems.at[0, step]),
            pltpu.make_async_copy(source_hbm.at[:, span], source.at[:, span], sems.at[1, step]),
        )
        for step, span in enumerate(spans)
    ]
    tag_copies = [
        pltpu.make_async_copy(owner_hbm, owner, tag_sems.at[0]),
        pltpu.make_async_copy(sub_hbm, sub, tag_sems.at[1]),
    ]
    for copy in [copy for pair in copies for copy in pair] + tag_copies:
        copy.start()
    totals = [None] * ROW_PARTS
    for span, pair in zip(spans, copies):
        for copy in pair:
            copy.wait()
        for at, rows in enumerate(cut(row_count, ROW_PARTS)):
            part = jnp.dot(source[rows, span], basis[span, :], preferred_element_type=jnp.float32)
            totals[at] = part if totals[at] is None else totals[at] + part
    for projected, rows in zip(totals, cut(row_count, ROW_PARTS)):
        norms = jnp.sum(projected * projected, axis=1, keepdims=True)
        packed_ref[rows, :] = (projected * lax.rsqrt(norms + 1e-06)).astype(jnp.bfloat16)
    for copy in tag_copies:
        copy.wait()
    tags = (owner[...] * CPO + sub[...] + 1).astype(jnp.float32)
    tags = jnp.concatenate(
        [tags, jnp.zeros((TAG_ROWS - tags.shape[0], LANES), jnp.float32)], axis=0
    )
    tags = jnp.concatenate([tags, jnp.zeros((TAG_ROWS, width - LANES), jnp.float32)], axis=1)
    packed_ref[row_count:, :] = tags.astype(jnp.bfloat16)


def cut(size, steps):
    return [pl.ds(size // steps * step, size // steps) for step in range(steps)]


def project(embeddings, basis, owner_ids, sub_cluster):
    row_count, depth = embeddings.shape
    width = basis.shape[1]
    tag_shape = (row_count // LANES, LANES)
    return pl.pallas_call(
        project_kernel,
        in_specs=[pl.BlockSpec(memory_space=pltpu.HBM)] * 4,
        out_specs=pl.BlockSpec(memory_space=pltpu.VMEM),
        out_shape=jax.ShapeDtypeStruct((row_count + TAG_ROWS, width), jnp.bfloat16),
        scratch_shapes=[
            pltpu.VMEM((row_count, depth), jnp.bfloat16),
            pltpu.VMEM((depth, width), jnp.bfloat16),
            pltpu.VMEM(tag_shape, jnp.int32),
            pltpu.VMEM(tag_shape, jnp.int32),
            pltpu.SemaphoreType.DMA((2, STEPS)),
            pltpu.SemaphoreType.DMA((2,)),
        ],
        compiler_params=pltpu.CompilerParams(vmem_limit_bytes=VMEM_LIMIT),
        cost_estimate=pl.CostEstimate(
            flops=2 * row_count * depth * width,
            bytes_accessed=2 * depth * (row_count + width),
            transcendentals=0,
        ),
    )(
        *[
            pltpu.with_memory_space_constraint(array, pltpu.HBM)
            for array in (
                embeddings,
                basis,
                owner_ids.reshape(tag_shape),
                sub_cluster.reshape(tag_shape),
            )
        ]
    )


def score_kernel(key_count, cols, row_parts, known, own_first, *refs):
    refs = list(refs)
    key_refs = [refs.pop(0) for _ in range(key_count)]
    row_refs = [[refs.pop(0) for _ in range(parts)] for parts in row_parts]
    known_refs = [refs.pop(0) for _ in range(known)]
    base_ref = refs.pop(0) if own_first else None
    col_refs = [refs.pop(0) for _ in range(cols)]
    row_outs = refs
    row_count = key_refs[0].shape[0] - TAG_ROWS
    tiles = row_count // LANES
    best = [
        [jnp.full((8, LANES), ABSENT, jnp.float32) for _ in range(tiles)]
        for _ in range(key_count if own_first else cols)
    ]
    for block, part_refs in enumerate(row_refs):
        tag_ref = part_refs[-1]
        row_tags = tag_ref[tag_ref.shape[0] - TAG_ROWS :, :LANES].astype(jnp.float32)
        place = 0
        for part_ref in part_refs:
            count = part_ref.shape[0] // LANES * LANES
            tags = [
                jnp.broadcast_to(row_tags[at : at + 1, :], (LANES, LANES)).T
                for at in range(place, place + count // LANES)
            ]
            across = [None] * len(tags)
            for key, key_ref in enumerate(key_refs):
                key_tags = key_ref[row_count:, :LANES].astype(jnp.float32)
                scores = lax.dot_general(
                    part_ref[:count, :],
                    key_ref[:row_count, :],
                    (((1,), (1,)), ((), ())),
                    preferred_element_type=jnp.float32,
                )
                for tile, tag in enumerate(tags):
                    for at in range(tiles):
                        same = tag == key_tags[at : at + 1, :]
                        if own_first and block == 0 and at == place + tile:
                            same = same & (
                                lax.broadcasted_iota(jnp.int32, (LANES, LANES), 0)
                                != lax.broadcasted_iota(jnp.int32, (LANES, LANES), 1)
                            )
                        kept = scores[
                            tile * LANES : (tile + 1) * LANES, at * LANES : (at + 1) * LANES
                        ]
                        kept = jnp.where(same, kept, ABSENT)
                        if key < len(best):
                            best[key][at] = jnp.maximum(
                                best[key][at], jnp.max(kept.reshape(LANES // 8, 8, LANES), axis=0)
                            )
                        if not own_first:
                            across[tile] = (
                                kept if across[tile] is None else jnp.maximum(across[tile], kept)
                            )
            if not own_first:
                for tile in range(len(tags)):
                    at = block % 2 * tiles + place + tile
                    found = jnp.max(across[tile].T, axis=0, keepdims=True)
                    if known_refs:
                        found = jnp.maximum(found, known_refs[block // 2][at : at + 1, :])
                    row_outs[block // 2][at : at + 1, :] = found
            place += len(tags)
    for key, found in enumerate(best):
        for at in range(tiles):
            highest = jnp.max(found[at], axis=0, keepdims=True)
            if own_first:
                row_outs[0][at : at + 1, :] = jnp.maximum(highest, base_ref[at : at + 1, :])
            else:
                col_refs[key][at : at + 1, :] = highest
    if own_first:
        row_outs[0][tiles:, :] = base_ref[tiles:, :]


def score(keys, rows, cols=0, known=(), base=None):
    parts = [row if isinstance(row, tuple) else (row,) for row in rows]
    operands = [*keys, *(part for row in parts for part in row)]
    operands += known if base is None else [base]
    tiles = keys[0].shape[0] // LANES
    best = jax.ShapeDtypeStruct((tiles, LANES), jnp.float32)
    pair = jax.ShapeDtypeStruct((2 * tiles, LANES), jnp.float32)
    out_shape = [best] * cols + [pair] * (len(rows) // 2 if base is None else 1)
    inside = pl.BlockSpec(memory_space=pltpu.VMEM)
    found = pl.pallas_call(
        functools.partial(
            score_kernel,
            len(keys),
            cols,
            [len(row) for row in parts],
            len(known),
            base is not None,
        ),
        in_specs=[inside] * len(operands),
        out_specs=[inside] * len(out_shape),
        out_shape=out_shape,
        compiler_params=pltpu.CompilerParams(vmem_limit_bytes=VMEM_LIMIT),
        cost_estimate=pl.CostEstimate(flops=0, bytes_accessed=0, transcendentals=0),
    )(*operands)
    return list(found[:cols]), list(found[cols:])


def owner_steps(count):
    half = count // 2
    circle = [count - 1 - 2 * i for i in range(half)] + [count - 2 - 2 * i for i in range(half)]
    return [
        [(circle[(i + step) % count], circle[i]) for i in range(count)]
        for step in range(1, half + 1)
    ]


def per_device(embeddings, basis, owner_ids, sub_cluster):
    row_count = embeddings.shape[0]
    tiles = row_count // LANES
    split_count, owner_count = lax.axis_size("split"), lax.axis_size("owners")

    def swap(block, offset):
        return lax.ppermute(block, "split", [(s, s ^ offset) for s in range(split_count)])

    def halves(block):
        return block[: row_count // 2], block[row_count // 2 :]

    own = project(embeddings, basis, owner_ids, sub_cluster)
    *steps, last = owner_steps(owner_count)
    keys = [lax.ppermute(own, "owners", step) for step in steps]
    nearby = lax.ppermute(own, "owners", last)
    offsets = range(2, split_count, 2)
    one_turn = 1 + (lax.axis_index("groups") >> 16)
    besides = lax.fori_loop(
        0,
        one_turn,
        lambda _, blocks: [swap(block, offset) for block, offset in zip(blocks, offsets)],
        [own] * len(offsets),
    )
    rows = [own, swap(own, 1)]
    for beside in besides:
        rows += [beside, tuple(swap(part, 1) for part in halves(beside))]
    row_best, backs = [], []
    for key, step in zip(keys, steps):
        (found,), row_best = score([key], rows, cols=1, known=row_best)
        backs.append(lax.ppermute(found, "owners", [(b, a) for a, b in step]))
    _, row_best = score([nearby], rows, known=row_best)
    others = [swap(found, offset) for found, offset in zip(row_best[1:], offsets)]
    _, (local,) = score([own], rows, base=row_best[0])
    for other in others:
        local = jnp.maximum(local, other)
    best = jnp.maximum(local[:tiles], swap(local[tiles:], 1))
    for back in backs:
        best = jnp.maximum(best, back)
    return jnp.maximum(best, -1.0).reshape(row_count)


def solution(mesh):
    placed = (
        P(("groups", "owners", "split"), None),
        P(),
        P(("groups", "owners", "split"), None),
        P(("groups", "owners", "split")),
    )
    return jax.shard_map(
        per_device,
        mesh=mesh,
        in_specs=placed,
        out_specs=P(("groups", "owners", "split")),
        check_vma=False,
    )
```

```python
import functools

import jax
import jax.numpy as jnp
from jax import lax
from jax.experimental import pallas as pl
from jax.experimental.pallas import tpu as pltpu
from jax.sharding import PartitionSpec as P

CPO = 8
LANES = 128
TAG_ROWS = 16
ABSENT = -2.0
STEPS = 4
ROW_PARTS = 4
VMEM_LIMIT = 48 * 1024 * 1024


def project_kernel(source_hbm, basis_hbm, owner_hbm, sub_hbm, packed_ref, *scratch):
    source, basis, owner, sub, sems, tag_sems = scratch
    row_count, depth = source.shape
    width = basis.shape[1]
    spans = cut(depth, STEPS)
    copies = [
        (
            pltpu.make_async_copy(basis_hbm.at[span, :], basis.at[span, :], sems.at[0, step]),
            pltpu.make_async_copy(source_hbm.at[:, span], source.at[:, span], sems.at[1, step]),
        )
        for step, span in enumerate(spans)
    ]
    tag_copies = [
        pltpu.make_async_copy(owner_hbm, owner, tag_sems.at[0]),
        pltpu.make_async_copy(sub_hbm, sub, tag_sems.at[1]),
    ]
    for copy in [copy for pair in copies for copy in pair] + tag_copies:
        copy.start()
    totals = [None] * ROW_PARTS
    for span, pair in zip(spans, copies):
        for copy in pair:
            copy.wait()
        for at, rows in enumerate(cut(row_count, ROW_PARTS)):
            part = jnp.dot(source[rows, span], basis[span, :], preferred_element_type=jnp.float32)
            totals[at] = part if totals[at] is None else totals[at] + part
    for projected, rows in zip(totals, cut(row_count, ROW_PARTS)):
        norms = jnp.sum(projected * projected, axis=1, keepdims=True)
        packed_ref[rows, :] = (projected * lax.rsqrt(norms + 1e-06)).astype(jnp.bfloat16)
    for copy in tag_copies:
        copy.wait()
    tags = (owner[...] * CPO + sub[...] + 1).astype(jnp.float32)
    tags = jnp.concatenate(
        [tags, jnp.zeros((TAG_ROWS - tags.shape[0], LANES), jnp.float32)], axis=0
    )
    tags = jnp.concatenate([tags, jnp.zeros((TAG_ROWS, width - LANES), jnp.float32)], axis=1)
    packed_ref[row_count:, :] = tags.astype(jnp.bfloat16)


def cut(size, steps):
    return [pl.ds(size // steps * step, size // steps) for step in range(steps)]


def project(embeddings, basis, owner_ids, sub_cluster):
    row_count, depth = embeddings.shape
    width = basis.shape[1]
    tag_shape = (row_count // LANES, LANES)
    return pl.pallas_call(
        project_kernel,
        in_specs=[pl.BlockSpec(memory_space=pltpu.HBM)] * 4,
        out_specs=pl.BlockSpec(memory_space=pltpu.VMEM),
        out_shape=jax.ShapeDtypeStruct((row_count + TAG_ROWS, width), jnp.bfloat16),
        scratch_shapes=[
            pltpu.VMEM((row_count, depth), jnp.bfloat16),
            pltpu.VMEM((depth, width), jnp.bfloat16),
            pltpu.VMEM(tag_shape, jnp.int32),
            pltpu.VMEM(tag_shape, jnp.int32),
            pltpu.SemaphoreType.DMA((2, STEPS)),
            pltpu.SemaphoreType.DMA((2,)),
        ],
        compiler_params=pltpu.CompilerParams(vmem_limit_bytes=VMEM_LIMIT),
        cost_estimate=pl.CostEstimate(
            flops=2 * row_count * depth * width,
            bytes_accessed=2 * depth * (row_count + width),
            transcendentals=0,
        ),
    )(
        *[
            pltpu.with_memory_space_constraint(array, pltpu.HBM)
            for array in (
                embeddings,
                basis,
                owner_ids.reshape(tag_shape),
                sub_cluster.reshape(tag_shape),
            )
        ]
    )


def score_kernel(key_count, cols, row_parts, known, own_first, *refs):
    refs = list(refs)
    key_refs = [refs.pop(0) for _ in range(key_count)]
    row_refs = [[refs.pop(0) for _ in range(parts)] for parts in row_parts]
    known_refs = [refs.pop(0) for _ in range(known)]
    col_refs = [refs.pop(0) for _ in range(cols)]
    row_outs = refs
    row_count = key_refs[0].shape[0] - TAG_ROWS
    tiles = row_count // LANES
    best = [
        [jnp.full((8, LANES), ABSENT, jnp.float32) for _ in range(tiles)]
        for _ in range(key_count if own_first else cols)
    ]
    for block, part_refs in enumerate(row_refs):
        tag_ref = part_refs[-1]
        row_tags = tag_ref[tag_ref.shape[0] - TAG_ROWS :, :LANES].astype(jnp.float32)
        place = 0
        for part_ref in part_refs:
            count = part_ref.shape[0] // LANES * LANES
            tags = [
                jnp.broadcast_to(row_tags[at : at + 1, :], (LANES, LANES)).T
                for at in range(place, place + count // LANES)
            ]
            across = [None] * len(tags)
            for key, key_ref in enumerate(key_refs):
                key_tags = key_ref[row_count:, :LANES].astype(jnp.float32)
                scores = lax.dot_general(
                    part_ref[:count, :],
                    key_ref[:row_count, :],
                    (((1,), (1,)), ((), ())),
                    preferred_element_type=jnp.float32,
                )
                for tile, tag in enumerate(tags):
                    for at in range(tiles):
                        same = tag == key_tags[at : at + 1, :]
                        if own_first and block == 0 and at == place + tile:
                            same = same & (
                                lax.broadcasted_iota(jnp.int32, (LANES, LANES), 0)
                                != lax.broadcasted_iota(jnp.int32, (LANES, LANES), 1)
                            )
                        kept = scores[
                            tile * LANES : (tile + 1) * LANES, at * LANES : (at + 1) * LANES
                        ]
                        kept = jnp.where(same, kept, ABSENT)
                        if key < len(best):
                            best[key][at] = jnp.maximum(
                                best[key][at], jnp.max(kept.reshape(LANES // 8, 8, LANES), axis=0)
                            )
                        if not own_first:
                            across[tile] = (
                                kept if across[tile] is None else jnp.maximum(across[tile], kept)
                            )
            if not own_first:
                for tile in range(len(tags)):
                    at = block % 2 * tiles + place + tile
                    found = jnp.max(across[tile].T, axis=0, keepdims=True)
                    if block // 2 < known:
                        found = jnp.maximum(found, known_refs[block // 2][at : at + 1, :])
                    row_outs[block // 2][at : at + 1, :] = found
            place += len(tags)
    for key, found in enumerate(best):
        for at in range(tiles):
            highest = jnp.max(found[at], axis=0, keepdims=True)
            if own_first:
                row_outs[0][at : at + 1, :] = highest
            else:
                col_refs[key][at : at + 1, :] = highest
    if own_first:
        row_outs[0][tiles:, :] = jnp.full((tiles, LANES), ABSENT, jnp.float32)


def score(keys, rows, cols=0, known=(), own_first=False):
    parts = [row if isinstance(row, tuple) else (row,) for row in rows]
    operands = [*keys, *(part for row in parts for part in row)]
    operands += known
    tiles = keys[0].shape[0] // LANES
    best = jax.ShapeDtypeStruct((tiles, LANES), jnp.float32)
    pair = jax.ShapeDtypeStruct((2 * tiles, LANES), jnp.float32)
    out_shape = [best] * cols + [pair] * (1 if own_first else len(rows) // 2)
    inside = pl.BlockSpec(memory_space=pltpu.VMEM)
    found = pl.pallas_call(
        functools.partial(
            score_kernel,
            len(keys),
            cols,
            [len(row) for row in parts],
            len(known),
            own_first,
        ),
        in_specs=[inside] * len(operands),
        out_specs=[inside] * len(out_shape),
        out_shape=out_shape,
        compiler_params=pltpu.CompilerParams(vmem_limit_bytes=VMEM_LIMIT),
        cost_estimate=pl.CostEstimate(flops=0, bytes_accessed=0, transcendentals=0),
    )(*operands)
    return list(found[:cols]), list(found[cols:])


def owner_steps(count):
    half = count // 2
    circle = [count - 1 - 2 * i for i in range(half)] + [count - 2 - 2 * i for i in range(half)]
    return [
        [(circle[(i + step) % count], circle[i]) for i in range(count)]
        for step in range(1, half + 1)
    ]


def per_device(embeddings, basis, owner_ids, sub_cluster):
    row_count = embeddings.shape[0]
    tiles = row_count // LANES
    split_count, owner_count = lax.axis_size("split"), lax.axis_size("owners")

    def swap(block, offset):
        return lax.ppermute(block, "split", [(s, s ^ offset) for s in range(split_count)])

    def halves(block):
        return block[: row_count // 2], block[row_count // 2 :]

    own = project(embeddings, basis, owner_ids, sub_cluster)
    *steps, last = owner_steps(owner_count)
    keys = [lax.ppermute(own, "owners", step) for step in steps]
    nearby = lax.ppermute(own, "owners", last)
    offsets = range(2, split_count, 2)
    one_turn = 1 + (lax.axis_index("groups") >> 16)
    besides = lax.fori_loop(
        0,
        one_turn,
        lambda _, blocks: [swap(block, offset) for block, offset in zip(blocks, offsets)],
        [own] * len(offsets),
    )
    rows = [own, swap(own, 1)]
    for beside in besides:
        rows += [beside, tuple(swap(part, 1) for part in halves(beside))]
    _, row_best = score([own], rows, own_first=True)
    backs = []
    for key, step in zip(keys, steps):
        (found,), row_best = score([key], rows, cols=1, known=row_best)
        backs.append(lax.ppermute(found, "owners", [(b, a) for a, b in step]))
    _, row_best = score([nearby], rows, known=row_best)
    others = [swap(found, offset) for found, offset in zip(row_best[1:], offsets)]
    local = row_best[0]
    for other in others:
        local = jnp.maximum(local, other)
    best = jnp.maximum(local[:tiles], swap(local[tiles:], 1))
    for back in backs:
        best = jnp.maximum(best, back)
    return jnp.maximum(best, -1.0).reshape(row_count)


def solution(mesh):
    placed = (
        P(("groups", "owners", "split"), None),
        P(),
        P(("groups", "owners", "split"), None),
        P(("groups", "owners", "split")),
    )
    return jax.shard_map(
        per_device,
        mesh=mesh,
        in_specs=placed,
        out_specs=P(("groups", "owners", "split")),
        check_vma=False,
    )
```

```python
import functools

import jax
import jax.numpy as jnp
from jax import lax
from jax.experimental import pallas as pl
from jax.experimental.pallas import tpu as pltpu
from jax.sharding import PartitionSpec as P

CPO = 8
LANES = 128
TAG_ROWS = 16
ABSENT = -2.0
STEPS = 8
ROW_PARTS = 4
VMEM_LIMIT = 48 * 1024 * 1024


def project_kernel(source_hbm, basis_hbm, owner_hbm, sub_hbm, packed_ref, *scratch):
    source, basis, owner, sub, sems, tag_sems = scratch
    row_count, depth = source.shape
    width = basis.shape[1]
    spans = cut(depth, STEPS)
    copies = [
        (
            pltpu.make_async_copy(basis_hbm.at[span, :], basis.at[span, :], sems.at[0, step]),
            pltpu.make_async_copy(source_hbm.at[:, span], source.at[:, span], sems.at[1, step]),
        )
        for step, span in enumerate(spans)
    ]
    tag_copies = [
        pltpu.make_async_copy(owner_hbm, owner, tag_sems.at[0]),
        pltpu.make_async_copy(sub_hbm, sub, tag_sems.at[1]),
    ]
    for copy in [copy for pair in copies for copy in pair] + tag_copies:
        copy.start()
    totals = [None] * ROW_PARTS
    for span, pair in zip(spans, copies):
        for copy in pair:
            copy.wait()
        for at, rows in enumerate(cut(row_count, ROW_PARTS)):
            part = jnp.dot(source[rows, span], basis[span, :], preferred_element_type=jnp.float32)
            totals[at] = part if totals[at] is None else totals[at] + part
    for projected, rows in zip(totals, cut(row_count, ROW_PARTS)):
        norms = jnp.sum(projected * projected, axis=1, keepdims=True)
        packed_ref[rows, :] = (projected * lax.rsqrt(norms + 1e-06)).astype(jnp.bfloat16)
    for copy in tag_copies:
        copy.wait()
    tags = (owner[...] * CPO + sub[...] + 1).astype(jnp.float32)
    tags = jnp.concatenate(
        [tags, jnp.zeros((TAG_ROWS - tags.shape[0], LANES), jnp.float32)], axis=0
    )
    tags = jnp.concatenate([tags, jnp.zeros((TAG_ROWS, width - LANES), jnp.float32)], axis=1)
    packed_ref[row_count:, :] = tags.astype(jnp.bfloat16)


def cut(size, steps):
    return [pl.ds(size // steps * step, size // steps) for step in range(steps)]


def project(embeddings, basis, owner_ids, sub_cluster):
    row_count, depth = embeddings.shape
    width = basis.shape[1]
    tag_shape = (row_count // LANES, LANES)
    return pl.pallas_call(
        project_kernel,
        in_specs=[pl.BlockSpec(memory_space=pltpu.HBM)] * 4,
        out_specs=pl.BlockSpec(memory_space=pltpu.VMEM),
        out_shape=jax.ShapeDtypeStruct((row_count + TAG_ROWS, width), jnp.bfloat16),
        scratch_shapes=[
            pltpu.VMEM((row_count, depth), jnp.bfloat16),
            pltpu.VMEM((depth, width), jnp.bfloat16),
            pltpu.VMEM(tag_shape, jnp.int32),
            pltpu.VMEM(tag_shape, jnp.int32),
            pltpu.SemaphoreType.DMA((2, STEPS)),
            pltpu.SemaphoreType.DMA((2,)),
        ],
        compiler_params=pltpu.CompilerParams(vmem_limit_bytes=VMEM_LIMIT),
        cost_estimate=pl.CostEstimate(
            flops=2 * row_count * depth * width,
            bytes_accessed=2 * depth * (row_count + width),
            transcendentals=0,
        ),
    )(
        *[
            pltpu.with_memory_space_constraint(array, pltpu.HBM)
            for array in (
                embeddings,
                basis,
                owner_ids.reshape(tag_shape),
                sub_cluster.reshape(tag_shape),
            )
        ]
    )


def score_kernel(key_count, cols, row_parts, known, own_first, *refs):
    refs = list(refs)
    key_refs = [refs.pop(0) for _ in range(key_count)]
    row_refs = [[refs.pop(0) for _ in range(parts)] for parts in row_parts]
    known_refs = [refs.pop(0) for _ in range(known)]
    col_refs = [refs.pop(0) for _ in range(cols)]
    row_outs = refs
    row_count = key_refs[0].shape[0] - TAG_ROWS
    tiles = row_count // LANES
    best = [
        [jnp.full((8, LANES), ABSENT, jnp.float32) for _ in range(tiles)]
        for _ in range(key_count if own_first else cols)
    ]
    for block, part_refs in enumerate(row_refs):
        tag_ref = part_refs[-1]
        row_tags = tag_ref[tag_ref.shape[0] - TAG_ROWS :, :LANES].astype(jnp.float32)
        place = 0
        for part_ref in part_refs:
            count = part_ref.shape[0] // LANES * LANES
            tags = [
                jnp.broadcast_to(row_tags[at : at + 1, :], (LANES, LANES)).T
                for at in range(place, place + count // LANES)
            ]
            across = [None] * len(tags)
            for key, key_ref in enumerate(key_refs):
                key_tags = key_ref[row_count:, :LANES].astype(jnp.float32)
                scores = lax.dot_general(
                    part_ref[:count, :],
                    key_ref[:row_count, :],
                    (((1,), (1,)), ((), ())),
                    preferred_element_type=jnp.float32,
                )
                for tile, tag in enumerate(tags):
                    for at in range(tiles):
                        same = tag == key_tags[at : at + 1, :]
                        if own_first and block == 0 and at == place + tile:
                            same = same & (
                                lax.broadcasted_iota(jnp.int32, (LANES, LANES), 0)
                                != lax.broadcasted_iota(jnp.int32, (LANES, LANES), 1)
                            )
                        kept = scores[
                            tile * LANES : (tile + 1) * LANES, at * LANES : (at + 1) * LANES
                        ]
                        kept = jnp.where(same, kept, ABSENT)
                        if key < len(best):
                            best[key][at] = jnp.maximum(
                                best[key][at], jnp.max(kept.reshape(LANES // 8, 8, LANES), axis=0)
                            )
                        if not own_first:
                            across[tile] = (
                                kept if across[tile] is None else jnp.maximum(across[tile], kept)
                            )
            if not own_first:
                for tile in range(len(tags)):
                    at = block % 2 * tiles + place + tile
                    found = jnp.max(across[tile].T, axis=0, keepdims=True)
                    if block // 2 < known:
                        found = jnp.maximum(found, known_refs[block // 2][at : at + 1, :])
                    row_outs[block // 2][at : at + 1, :] = found
            place += len(tags)
    for key, found in enumerate(best):
        for at in range(tiles):
            highest = jnp.max(found[at], axis=0, keepdims=True)
            if own_first:
                row_outs[0][at : at + 1, :] = highest
            else:
                col_refs[key][at : at + 1, :] = highest
    if own_first:
        row_outs[0][tiles:, :] = jnp.full((tiles, LANES), ABSENT, jnp.float32)


def score(keys, rows, cols=0, known=(), own_first=False):
    parts = [row if isinstance(row, tuple) else (row,) for row in rows]
    operands = [*keys, *(part for row in parts for part in row)]
    operands += known
    tiles = keys[0].shape[0] // LANES
    best = jax.ShapeDtypeStruct((tiles, LANES), jnp.float32)
    pair = jax.ShapeDtypeStruct((2 * tiles, LANES), jnp.float32)
    out_shape = [best] * cols + [pair] * (1 if own_first else len(rows) // 2)
    inside = pl.BlockSpec(memory_space=pltpu.VMEM)
    found = pl.pallas_call(
        functools.partial(
            score_kernel,
            len(keys),
            cols,
            [len(row) for row in parts],
            len(known),
            own_first,
        ),
        in_specs=[inside] * len(operands),
        out_specs=[inside] * len(out_shape),
        out_shape=out_shape,
        compiler_params=pltpu.CompilerParams(vmem_limit_bytes=VMEM_LIMIT),
        cost_estimate=pl.CostEstimate(flops=0, bytes_accessed=0, transcendentals=0),
    )(*operands)
    return list(found[:cols]), list(found[cols:])


def owner_steps(count):
    half = count // 2
    circle = [count - 1 - 2 * i for i in range(half)] + [count - 2 - 2 * i for i in range(half)]
    return [
        [(circle[(i + step) % count], circle[i]) for i in range(count)]
        for step in range(1, half + 1)
    ]


def per_device(embeddings, basis, owner_ids, sub_cluster):
    row_count = embeddings.shape[0]
    tiles = row_count // LANES
    split_count, owner_count = lax.axis_size("split"), lax.axis_size("owners")

    def swap(block, offset):
        return lax.ppermute(block, "split", [(s, s ^ offset) for s in range(split_count)])

    def halves(block):
        return block[: row_count // 2], block[row_count // 2 :]

    own = project(embeddings, basis, owner_ids, sub_cluster)
    *steps, last = owner_steps(owner_count)
    keys = [lax.ppermute(own, "owners", step) for step in steps]
    nearby = lax.ppermute(own, "owners", last)
    offsets = range(2, split_count, 2)
    one_turn = 1 + (lax.axis_index("groups") >> 16)
    besides = lax.fori_loop(
        0,
        one_turn,
        lambda _, blocks: [swap(block, offset) for block, offset in zip(blocks, offsets)],
        [own] * len(offsets),
    )
    rows = [own, swap(own, 1)]
    for beside in besides:
        rows += [beside, tuple(swap(part, 1) for part in halves(beside))]
    _, row_best = score([own], rows, own_first=True)
    _, row_best = score([nearby], rows, known=row_best)
    backs = []
    for key, step in zip(keys, steps):
        (found,), row_best = score([key], rows, cols=1, known=row_best)
        backs.append(lax.ppermute(found, "owners", [(b, a) for a, b in step]))
    others = [swap(found, offset) for found, offset in zip(row_best[1:], offsets)]
    local = row_best[0]
    for other in others:
        local = jnp.maximum(local, other)
    best = jnp.maximum(local[:tiles], swap(local[tiles:], 1))
    for back in backs:
        best = jnp.maximum(best, back)
    return jnp.maximum(best, -1.0).reshape(row_count)


def solution(mesh):
    placed = (
        P(("groups", "owners", "split"), None),
        P(),
        P(("groups", "owners", "split"), None),
        P(("groups", "owners", "split")),
    )
    return jax.shard_map(
        per_device,
        mesh=mesh,
        in_specs=placed,
        out_specs=P(("groups", "owners", "split")),
        check_vma=False,
    )
```

```python
import functools

import jax
import jax.numpy as jnp
from jax import lax
from jax.experimental import pallas as pl
from jax.experimental.pallas import tpu as pltpu
from jax.sharding import PartitionSpec as P

CPO = 8
LANES = 128
TAG_ROWS = 16
ABSENT = -2.0
STEPS = 8
ROW_PARTS = 4
VMEM_LIMIT = 48 * 1024 * 1024


def project_kernel(source_hbm, basis_hbm, owner_hbm, sub_hbm, packed_ref, *scratch):
    source, basis, owner, sub, sems, tag_sems = scratch
    row_count, depth = source.shape
    width = basis.shape[1]
    spans = cut(depth, STEPS)
    copies = [
        (
            pltpu.make_async_copy(basis_hbm.at[span, :], basis.at[span, :], sems.at[0, step]),
            pltpu.make_async_copy(source_hbm.at[:, span], source.at[:, span], sems.at[1, step]),
        )
        for step, span in enumerate(spans)
    ]
    tag_copies = [
        pltpu.make_async_copy(owner_hbm, owner, tag_sems.at[0]),
        pltpu.make_async_copy(sub_hbm, sub, tag_sems.at[1]),
    ]
    for copy in [copy for pair in copies for copy in pair] + tag_copies:
        copy.start()
    totals = [None] * ROW_PARTS
    for span, pair in zip(spans, copies):
        for copy in pair:
            copy.wait()
        for at, rows in enumerate(cut(row_count, ROW_PARTS)):
            part = jnp.dot(source[rows, span], basis[span, :], preferred_element_type=jnp.float32)
            totals[at] = part if totals[at] is None else totals[at] + part
    for projected, rows in zip(totals, cut(row_count, ROW_PARTS)):
        norms = jnp.sum(projected * projected, axis=1, keepdims=True)
        packed_ref[rows, :] = (projected * lax.rsqrt(norms + 1e-06)).astype(jnp.bfloat16)
    for copy in tag_copies:
        copy.wait()
    tags = (owner[...] * CPO + sub[...] + 1).astype(jnp.float32)
    tags = jnp.concatenate(
        [tags, jnp.zeros((TAG_ROWS - tags.shape[0], LANES), jnp.float32)], axis=0
    )
    tags = jnp.concatenate([tags, jnp.zeros((TAG_ROWS, width - LANES), jnp.float32)], axis=1)
    packed_ref[row_count:, :] = tags.astype(jnp.bfloat16)


def cut(size, steps):
    return [pl.ds(size // steps * step, size // steps) for step in range(steps)]


def project(embeddings, basis, owner_ids, sub_cluster):
    row_count, depth = embeddings.shape
    width = basis.shape[1]
    tag_shape = (row_count // LANES, LANES)
    return pl.pallas_call(
        project_kernel,
        in_specs=[pl.BlockSpec(memory_space=pltpu.HBM)] * 4,
        out_specs=pl.BlockSpec(memory_space=pltpu.VMEM),
        out_shape=jax.ShapeDtypeStruct((row_count + TAG_ROWS, width), jnp.bfloat16),
        scratch_shapes=[
            pltpu.VMEM((row_count, depth), jnp.bfloat16),
            pltpu.VMEM((depth, width), jnp.bfloat16),
            pltpu.VMEM(tag_shape, jnp.int32),
            pltpu.VMEM(tag_shape, jnp.int32),
            pltpu.SemaphoreType.DMA((2, STEPS)),
            pltpu.SemaphoreType.DMA((2,)),
        ],
        compiler_params=pltpu.CompilerParams(vmem_limit_bytes=VMEM_LIMIT),
        cost_estimate=pl.CostEstimate(
            flops=2 * row_count * depth * width,
            bytes_accessed=2 * depth * (row_count + width),
            transcendentals=0,
        ),
    )(
        *[
            pltpu.with_memory_space_constraint(array, pltpu.HBM)
            for array in (
                embeddings,
                basis,
                owner_ids.reshape(tag_shape),
                sub_cluster.reshape(tag_shape),
            )
        ]
    )


def score_kernel(key_count, cols, row_parts, known, own_first, *refs):
    refs = list(refs)
    group = len(row_parts) // 2
    key_refs = [refs.pop(0) for _ in range(key_count)]
    row_refs = [[refs.pop(0) for _ in range(parts)] for parts in row_parts]
    known_refs = [refs.pop(0) for _ in range(known)]
    col_refs = [refs.pop(0) for _ in range(cols)]
    row_outs = refs
    row_count = key_refs[0].shape[0] - TAG_ROWS
    tiles = row_count // LANES
    best = [
        [jnp.full((8, LANES), ABSENT, jnp.float32) for _ in range(tiles)]
        for _ in range(key_count if own_first else cols)
    ]
    for block, part_refs in enumerate(row_refs):
        tag_ref = part_refs[-1]
        row_tags = tag_ref[tag_ref.shape[0] - TAG_ROWS :, :LANES].astype(jnp.float32)
        place = 0
        for part_ref in part_refs:
            count = part_ref.shape[0] // LANES * LANES
            tags = [
                jnp.broadcast_to(row_tags[at : at + 1, :], (LANES, LANES)).T
                for at in range(place, place + count // LANES)
            ]
            across = [None] * len(tags)
            for key, key_ref in enumerate(key_refs):
                key_tags = key_ref[row_count:, :LANES].astype(jnp.float32)
                scores = lax.dot_general(
                    part_ref[:count, :],
                    key_ref[:row_count, :],
                    (((1,), (1,)), ((), ())),
                    preferred_element_type=jnp.float32,
                )
                for tile, tag in enumerate(tags):
                    for at in range(tiles):
                        same = tag == key_tags[at : at + 1, :]
                        if own_first and block == 0 and at == place + tile:
                            same = same & (
                                lax.broadcasted_iota(jnp.int32, (LANES, LANES), 0)
                                != lax.broadcasted_iota(jnp.int32, (LANES, LANES), 1)
                            )
                        kept = scores[
                            tile * LANES : (tile + 1) * LANES, at * LANES : (at + 1) * LANES
                        ]
                        kept = jnp.where(same, kept, ABSENT)
                        if key < len(best):
                            best[key][at] = jnp.maximum(
                                best[key][at], jnp.max(kept.reshape(LANES // 8, 8, LANES), axis=0)
                            )
                        if not own_first:
                            across[tile] = (
                                kept if across[tile] is None else jnp.maximum(across[tile], kept)
                            )
            if not own_first:
                for tile in range(len(tags)):
                    at = block % group * tiles + place + tile
                    found = jnp.max(across[tile].T, axis=0, keepdims=True)
                    if block // group < known:
                        found = jnp.maximum(found, known_refs[block // group][at : at + 1, :])
                    row_outs[block // group][at : at + 1, :] = found
            place += len(tags)
    for key, found in enumerate(best):
        for at in range(tiles):
            highest = jnp.max(found[at], axis=0, keepdims=True)
            if own_first:
                row_outs[0][at : at + 1, :] = highest
            else:
                col_refs[key][at : at + 1, :] = highest
    if own_first:
        rest = row_outs[0].shape[0] - tiles
        row_outs[0][tiles:, :] = jnp.full((rest, LANES), ABSENT, jnp.float32)


def score(keys, rows, cols=0, known=(), own_first=False):
    parts = [row if isinstance(row, tuple) else (row,) for row in rows]
    operands = [*keys, *(part for row in parts for part in row)]
    operands += known
    tiles = keys[0].shape[0] // LANES
    best = jax.ShapeDtypeStruct((tiles, LANES), jnp.float32)
    group = jax.ShapeDtypeStruct((len(rows) // 2 * tiles, LANES), jnp.float32)
    out_shape = [best] * cols + [group] * (1 if own_first else 2)
    inside = pl.BlockSpec(memory_space=pltpu.VMEM)
    found = pl.pallas_call(
        functools.partial(
            score_kernel,
            len(keys),
            cols,
            [len(row) for row in parts],
            len(known),
            own_first,
        ),
        in_specs=[inside] * len(operands),
        out_specs=[inside] * len(out_shape),
        out_shape=out_shape,
        compiler_params=pltpu.CompilerParams(vmem_limit_bytes=VMEM_LIMIT),
        cost_estimate=pl.CostEstimate(flops=0, bytes_accessed=0, transcendentals=0),
    )(*operands)
    return list(found[:cols]), list(found[cols:])


def owner_steps(count):
    half = count // 2
    circle = [count - 1 - 2 * i for i in range(half)] + [count - 2 - 2 * i for i in range(half)]
    return [
        [(circle[(i + step) % count], circle[i]) for i in range(count)]
        for step in range(1, half + 1)
    ]


def per_device(embeddings, basis, owner_ids, sub_cluster):
    row_count = embeddings.shape[0]
    tiles = row_count // LANES
    split_count, owner_count = lax.axis_size("split"), lax.axis_size("owners")

    def swap(block, offset):
        return lax.ppermute(block, "split", [(s, s ^ offset) for s in range(split_count)])

    def halves(block):
        return block[: row_count // 2], block[row_count // 2 :]

    own = project(embeddings, basis, owner_ids, sub_cluster)
    *steps, last = owner_steps(owner_count)
    keys = [lax.ppermute(own, "owners", step) for step in steps]
    nearby = lax.ppermute(own, "owners", last)
    offsets = range(2, split_count, 2)
    one_turn = 1 + (lax.axis_index("groups") >> 16)
    besides = lax.fori_loop(
        0,
        one_turn,
        lambda _, blocks: [swap(block, offset) for block, offset in zip(blocks, offsets)],
        [own] * len(offsets),
    )
    rows = [own, *besides, swap(own, 1)]
    rows += [tuple(swap(part, 1) for part in halves(beside)) for beside in besides]
    _, row_best = score([own], rows, own_first=True)
    _, row_best = score([nearby], rows, known=row_best)
    backs = []
    for key, step in zip(keys, steps):
        (found,), row_best = score([key], rows, cols=1, known=row_best)
        backs.append(lax.ppermute(found, "owners", [(b, a) for a, b in step]))
    local = jnp.maximum(row_best[0], swap(row_best[1], 1))
    best = local[:tiles]
    for at, offset in enumerate(offsets, start=1):
        best = jnp.maximum(best, swap(local[at * tiles : (at + 1) * tiles], offset))
    for back in backs:
        best = jnp.maximum(best, back)
    return jnp.maximum(best, -1.0).reshape(row_count)


def solution(mesh):
    placed = (
        P(("groups", "owners", "split"), None),
        P(),
        P(("groups", "owners", "split"), None),
        P(("groups", "owners", "split")),
    )
    return jax.shard_map(
        per_device,
        mesh=mesh,
        in_specs=placed,
        out_specs=P(("groups", "owners", "split")),
        check_vma=False,
    )
```

```python
import functools

import jax
import jax.numpy as jnp
from jax import lax
from jax.experimental import pallas as pl
from jax.experimental.pallas import tpu as pltpu
from jax.sharding import PartitionSpec as P

CPO = 8
LANES = 128
TAG_ROWS = 16
ABSENT = -2.0
STEPS = 8
ROW_PARTS = 4
VMEM_LIMIT = 48 * 1024 * 1024


def project_kernel(source_hbm, basis_hbm, owner_hbm, sub_hbm, packed_ref, *scratch):
    source, basis, owner, sub, sems, tag_sems = scratch
    row_count, depth = source.shape
    width = basis.shape[1]
    spans = cut(depth, STEPS)
    copies = [
        (
            pltpu.make_async_copy(basis_hbm.at[span, :], basis.at[span, :], sems.at[0, step]),
            pltpu.make_async_copy(source_hbm.at[:, span], source.at[:, span], sems.at[1, step]),
        )
        for step, span in enumerate(spans)
    ]
    tag_copies = [
        pltpu.make_async_copy(owner_hbm, owner, tag_sems.at[0]),
        pltpu.make_async_copy(sub_hbm, sub, tag_sems.at[1]),
    ]
    for copy in [copy for pair in copies for copy in pair] + tag_copies:
        copy.start()
    totals = [None] * ROW_PARTS
    for span, pair in zip(spans, copies):
        for copy in pair:
            copy.wait()
        for at, rows in enumerate(cut(row_count, ROW_PARTS)):
            part = jnp.dot(source[rows, span], basis[span, :], preferred_element_type=jnp.float32)
            totals[at] = part if totals[at] is None else totals[at] + part
    for projected, rows in zip(totals, cut(row_count, ROW_PARTS)):
        norms = jnp.sum(projected * projected, axis=1, keepdims=True)
        packed_ref[rows, :] = (projected * lax.rsqrt(norms + 1e-06)).astype(jnp.bfloat16)
    for copy in tag_copies:
        copy.wait()
    tags = (owner[...] * CPO + sub[...] + 1).astype(jnp.float32)
    tags = jnp.concatenate(
        [tags, jnp.zeros((TAG_ROWS - tags.shape[0], LANES), jnp.float32)], axis=0
    )
    tags = jnp.concatenate([tags, jnp.zeros((TAG_ROWS, width - LANES), jnp.float32)], axis=1)
    packed_ref[row_count:, :] = tags.astype(jnp.bfloat16)


def cut(size, steps):
    return [pl.ds(size // steps * step, size // steps) for step in range(steps)]


def project(embeddings, basis, owner_ids, sub_cluster):
    row_count, depth = embeddings.shape
    width = basis.shape[1]
    tag_shape = (row_count // LANES, LANES)
    return pl.pallas_call(
        project_kernel,
        in_specs=[pl.BlockSpec(memory_space=pltpu.HBM)] * 4,
        out_specs=pl.BlockSpec(memory_space=pltpu.VMEM),
        out_shape=jax.ShapeDtypeStruct((row_count + TAG_ROWS, width), jnp.bfloat16),
        scratch_shapes=[
            pltpu.VMEM((row_count, depth), jnp.bfloat16),
            pltpu.VMEM((depth, width), jnp.bfloat16),
            pltpu.VMEM(tag_shape, jnp.int32),
            pltpu.VMEM(tag_shape, jnp.int32),
            pltpu.SemaphoreType.DMA((2, STEPS)),
            pltpu.SemaphoreType.DMA((2,)),
        ],
        compiler_params=pltpu.CompilerParams(vmem_limit_bytes=VMEM_LIMIT),
        cost_estimate=pl.CostEstimate(
            flops=2 * row_count * depth * width,
            bytes_accessed=2 * depth * (row_count + width),
            transcendentals=0,
        ),
    )(
        *[
            pltpu.with_memory_space_constraint(array, pltpu.HBM)
            for array in (
                embeddings,
                basis,
                owner_ids.reshape(tag_shape),
                sub_cluster.reshape(tag_shape),
            )
        ]
    )


def score_kernel(key_count, cols, row_parts, known, own_first, *refs):
    refs = list(refs)
    group = len(row_parts) // 2
    key_refs = [refs.pop(0) for _ in range(key_count)]
    row_refs = [[refs.pop(0) for _ in range(parts)] for parts in row_parts]
    known_refs = [refs.pop(0) for _ in range(known)]
    col_refs = [refs.pop(0) for _ in range(cols)]
    row_outs = refs
    row_count = key_refs[0].shape[0] - TAG_ROWS
    tiles = row_count // LANES
    best = [
        [jnp.full((8, LANES), ABSENT, jnp.float32) for _ in range(tiles)]
        for _ in range(key_count if own_first else cols)
    ]
    for block, part_refs in enumerate(row_refs):
        tag_ref = part_refs[-1]
        row_tags = tag_ref[tag_ref.shape[0] - TAG_ROWS :, :LANES].astype(jnp.float32)
        place = 0
        for part_ref in part_refs:
            count = part_ref.shape[0] // LANES * LANES
            tags = [
                jnp.broadcast_to(row_tags[at : at + 1, :], (LANES, LANES)).T
                for at in range(place, place + count // LANES)
            ]
            across = [None] * len(tags)
            for key, key_ref in enumerate(key_refs):
                key_tags = key_ref[row_count:, :LANES].astype(jnp.float32)
                scores = lax.dot_general(
                    part_ref[:count, :],
                    key_ref[:row_count, :],
                    (((1,), (1,)), ((), ())),
                    preferred_element_type=jnp.float32,
                )
                for tile, tag in enumerate(tags):
                    for at in range(tiles):
                        same = tag == key_tags[at : at + 1, :]
                        if own_first and block == 0 and at == place + tile:
                            same = same & (
                                lax.broadcasted_iota(jnp.int32, (LANES, LANES), 0)
                                != lax.broadcasted_iota(jnp.int32, (LANES, LANES), 1)
                            )
                        kept = scores[
                            tile * LANES : (tile + 1) * LANES, at * LANES : (at + 1) * LANES
                        ]
                        kept = jnp.where(same, kept, ABSENT)
                        if key < len(best):
                            best[key][at] = jnp.maximum(
                                best[key][at], jnp.max(kept.reshape(LANES // 8, 8, LANES), axis=0)
                            )
                        if not own_first:
                            across[tile] = (
                                kept if across[tile] is None else jnp.maximum(across[tile], kept)
                            )
            if not own_first:
                for tile in range(len(tags)):
                    at = block % group * tiles + place + tile
                    found = jnp.max(across[tile].T, axis=0, keepdims=True)
                    if block // group < known:
                        found = jnp.maximum(found, known_refs[block // group][at : at + 1, :])
                    row_outs[block // group][at : at + 1, :] = found
            place += len(tags)
    for key, found in enumerate(best):
        for at in range(tiles):
            highest = jnp.max(found[at], axis=0, keepdims=True)
            if own_first:
                row_outs[0][at : at + 1, :] = highest
            else:
                col_refs[key][at : at + 1, :] = highest
    if own_first:
        rest = row_outs[0].shape[0] - tiles
        row_outs[0][tiles:, :] = jnp.full((rest, LANES), ABSENT, jnp.float32)


def score(keys, rows, cols=0, known=(), own_first=False):
    parts = [row if isinstance(row, tuple) else (row,) for row in rows]
    operands = [*keys, *(part for row in parts for part in row)]
    operands += known
    tiles = keys[0].shape[0] // LANES
    best = jax.ShapeDtypeStruct((tiles, LANES), jnp.float32)
    group = jax.ShapeDtypeStruct((len(rows) // 2 * tiles, LANES), jnp.float32)
    out_shape = [best] * cols + [group] * (1 if own_first else 2)
    inside = pl.BlockSpec(memory_space=pltpu.VMEM)
    found = pl.pallas_call(
        functools.partial(
            score_kernel,
            len(keys),
            cols,
            [len(row) for row in parts],
            len(known),
            own_first,
        ),
        in_specs=[inside] * len(operands),
        out_specs=[inside] * len(out_shape),
        out_shape=out_shape,
        compiler_params=pltpu.CompilerParams(vmem_limit_bytes=VMEM_LIMIT),
        cost_estimate=pl.CostEstimate(flops=0, bytes_accessed=0, transcendentals=0),
    )(*operands)
    return list(found[:cols]), list(found[cols:])


def owner_steps(count):
    half = count // 2
    circle = [count - 1 - 2 * i for i in range(half)] + [count - 2 - 2 * i for i in range(half)]
    return [
        [(circle[i], circle[(i + step) % count]) for i in range(count)]
        for step in range(1, half + 1)
    ]


def per_device(embeddings, basis, owner_ids, sub_cluster):
    row_count = embeddings.shape[0]
    tiles = row_count // LANES
    split_count, owner_count = lax.axis_size("split"), lax.axis_size("owners")

    def swap(block, offset):
        return lax.ppermute(block, "split", [(s, s ^ offset) for s in range(split_count)])

    def halves(block):
        return block[: row_count // 2], block[row_count // 2 :]

    own = project(embeddings, basis, owner_ids, sub_cluster)
    *steps, last = owner_steps(owner_count)
    keys = [lax.ppermute(own, "owners", step) for step in steps]
    nearby = lax.ppermute(own, "owners", last)
    offsets = range(2, split_count, 2)
    one_turn = 1 + (lax.axis_index("groups") >> 16)
    besides = lax.fori_loop(
        0,
        one_turn,
        lambda _, blocks: [swap(block, offset) for block, offset in zip(blocks, offsets)],
        [own] * len(offsets),
    )
    rows = [own, *besides, swap(own, 1)]
    rows += [tuple(swap(part, 1) for part in halves(beside)) for beside in besides]
    _, row_best = score([own], rows, own_first=True)
    _, row_best = score([nearby], rows, known=row_best)
    backs = []
    for key, step in zip(keys, steps):
        (found,), row_best = score([key], rows, cols=1, known=row_best)
        backs.append(lax.ppermute(found, "owners", [(b, a) for a, b in step]))
    local = jnp.maximum(row_best[0], swap(row_best[1], 1))
    best = local[:tiles]
    for at, offset in enumerate(offsets, start=1):
        best = jnp.maximum(best, swap(local[at * tiles : (at + 1) * tiles], offset))
    for back in backs:
        best = jnp.maximum(best, back)
    return jnp.maximum(best, -1.0).reshape(row_count)


def solution(mesh):
    placed = (
        P(("groups", "owners", "split"), None),
        P(),
        P(("groups", "owners", "split"), None),
        P(("groups", "owners", "split")),
    )
    return jax.shard_map(
        per_device,
        mesh=mesh,
        in_specs=placed,
        out_specs=P(("groups", "owners", "split")),
        check_vma=False,
    )
```

```python
import functools

import jax
import jax.numpy as jnp
from jax import lax
from jax.experimental import pallas as pl
from jax.experimental.pallas import tpu as pltpu
from jax.sharding import PartitionSpec as P

CPO = 8
LANES = 128
TAG_ROWS = 16
ABSENT = -2.0
STEPS = 8
ROW_PARTS = 4
VMEM_LIMIT = 48 * 1024 * 1024


def project_kernel(source_hbm, basis_hbm, owner_hbm, sub_hbm, packed_ref, *scratch):
    source, basis, owner, sub, sems, tag_sems = scratch
    row_count, depth = source.shape
    width = basis.shape[1]
    spans = cut(depth, STEPS)
    copies = [
        (
            pltpu.make_async_copy(basis_hbm.at[span, :], basis.at[span, :], sems.at[0, step]),
            pltpu.make_async_copy(source_hbm.at[:, span], source.at[:, span], sems.at[1, step]),
        )
        for step, span in enumerate(spans)
    ]
    tag_copies = [
        pltpu.make_async_copy(owner_hbm, owner, tag_sems.at[0]),
        pltpu.make_async_copy(sub_hbm, sub, tag_sems.at[1]),
    ]
    for copy in [copy for pair in copies for copy in pair] + tag_copies:
        copy.start()
    totals = [None] * ROW_PARTS
    for span, pair in zip(spans, copies):
        for copy in pair:
            copy.wait()
        for at, rows in enumerate(cut(row_count, ROW_PARTS)):
            part = jnp.dot(source[rows, span], basis[span, :], preferred_element_type=jnp.float32)
            totals[at] = part if totals[at] is None else totals[at] + part
    for projected, rows in zip(totals, cut(row_count, ROW_PARTS)):
        norms = jnp.sum(projected * projected, axis=1, keepdims=True)
        packed_ref[rows, :] = (projected * lax.rsqrt(norms + 1e-06)).astype(jnp.bfloat16)
    for copy in tag_copies:
        copy.wait()
    tags = (owner[...] * CPO + sub[...] + 1).astype(jnp.float32)
    tags = jnp.concatenate(
        [tags, jnp.zeros((TAG_ROWS - tags.shape[0], LANES), jnp.float32)], axis=0
    )
    tags = jnp.concatenate([tags, jnp.zeros((TAG_ROWS, width - LANES), jnp.float32)], axis=1)
    packed_ref[row_count:, :] = tags.astype(jnp.bfloat16)


def cut(size, steps):
    return [pl.ds(size // steps * step, size // steps) for step in range(steps)]


def project(embeddings, basis, owner_ids, sub_cluster):
    row_count, depth = embeddings.shape
    width = basis.shape[1]
    tag_shape = (row_count // LANES, LANES)
    return pl.pallas_call(
        project_kernel,
        in_specs=[pl.BlockSpec(memory_space=pltpu.HBM)] * 4,
        out_specs=pl.BlockSpec(memory_space=pltpu.VMEM),
        out_shape=jax.ShapeDtypeStruct((row_count + TAG_ROWS, width), jnp.bfloat16),
        scratch_shapes=[
            pltpu.VMEM((row_count, depth), jnp.bfloat16),
            pltpu.VMEM((depth, width), jnp.bfloat16),
            pltpu.VMEM(tag_shape, jnp.int32),
            pltpu.VMEM(tag_shape, jnp.int32),
            pltpu.SemaphoreType.DMA((2, STEPS)),
            pltpu.SemaphoreType.DMA((2,)),
        ],
        compiler_params=pltpu.CompilerParams(vmem_limit_bytes=VMEM_LIMIT),
        cost_estimate=pl.CostEstimate(
            flops=2 * row_count * depth * width,
            bytes_accessed=2 * depth * (row_count + width),
            transcendentals=0,
        ),
    )(
        *[
            pltpu.with_memory_space_constraint(array, pltpu.HBM)
            for array in (
                embeddings,
                basis,
                owner_ids.reshape(tag_shape),
                sub_cluster.reshape(tag_shape),
            )
        ]
    )


def score_kernel(key_count, cols, row_parts, known, own_first, *refs):
    refs = list(refs)
    group = len(row_parts) // 2
    key_refs = [refs.pop(0) for _ in range(key_count)]
    row_refs = [[refs.pop(0) for _ in range(parts)] for parts in row_parts]
    known_refs = [refs.pop(0) for _ in range(known)]
    row_tag_refs = [] if own_first else [refs.pop(0) for _ in row_parts]
    col_refs = [refs.pop(0) for _ in range(cols)]
    row_outs, row_tag_outs = refs[: 2 - own_first], refs[2 - own_first :]
    row_count = key_refs[0].shape[0] - TAG_ROWS
    tiles = row_count // LANES
    best = [
        [jnp.full((8, LANES), ABSENT, jnp.float32) for _ in range(tiles)]
        for _ in range(key_count if own_first else cols)
    ]
    for block, part_refs in enumerate(row_refs):
        tag_ref = part_refs[-1]
        row_tags = tag_ref[tag_ref.shape[0] - TAG_ROWS :, :LANES].astype(jnp.float32)
        place = 0
        for part_ref in part_refs:
            count = part_ref.shape[0] // LANES * LANES
            tags = []
            for at in range(place, place + count // LANES):
                span = slice(at * LANES, (at + 1) * LANES)
                if own_first:
                    tag = jnp.broadcast_to(row_tags[at : at + 1, :], (LANES, LANES)).T
                    row_tag_outs[block][span, :] = tag
                else:
                    tag = row_tag_refs[block][span, :]
                tags.append(tag)
            across = [None] * len(tags)
            for key, key_ref in enumerate(key_refs):
                key_tags = key_ref[row_count:, :LANES].astype(jnp.float32)
                scores = lax.dot_general(
                    part_ref[:count, :],
                    key_ref[:row_count, :],
                    (((1,), (1,)), ((), ())),
                    preferred_element_type=jnp.float32,
                )
                for tile, tag in enumerate(tags):
                    for at in range(tiles):
                        same = tag == key_tags[at : at + 1, :]
                        if own_first and block == 0 and at == place + tile:
                            same = same & (
                                lax.broadcasted_iota(jnp.int32, (LANES, LANES), 0)
                                != lax.broadcasted_iota(jnp.int32, (LANES, LANES), 1)
                            )
                        kept = scores[
                            tile * LANES : (tile + 1) * LANES, at * LANES : (at + 1) * LANES
                        ]
                        kept = jnp.where(same, kept, ABSENT)
                        if key < len(best):
                            best[key][at] = jnp.maximum(
                                best[key][at], jnp.max(kept.reshape(LANES // 8, 8, LANES), axis=0)
                            )
                        if not own_first:
                            across[tile] = (
                                kept if across[tile] is None else jnp.maximum(across[tile], kept)
                            )
            if not own_first:
                for tile in range(len(tags)):
                    at = block % group * tiles + place + tile
                    found = jnp.max(across[tile].T, axis=0, keepdims=True)
                    if block // group < known:
                        found = jnp.maximum(found, known_refs[block // group][at : at + 1, :])
                    row_outs[block // group][at : at + 1, :] = found
            place += len(tags)
    for key, found in enumerate(best):
        for at in range(tiles):
            highest = jnp.max(found[at], axis=0, keepdims=True)
            if own_first:
                row_outs[0][at : at + 1, :] = highest
            else:
                col_refs[key][at : at + 1, :] = highest
    if own_first:
        rest = row_outs[0].shape[0] - tiles
        row_outs[0][tiles:, :] = jnp.full((rest, LANES), ABSENT, jnp.float32)


def score(keys, rows, cols=0, known=(), row_tags=None):
    parts = [row if isinstance(row, tuple) else (row,) for row in rows]
    operands = [*keys, *(part for row in parts for part in row)]
    operands += known if row_tags is None else [*known, *row_tags]
    own_first = row_tags is None
    tiles = keys[0].shape[0] // LANES
    best = jax.ShapeDtypeStruct((tiles, LANES), jnp.float32)
    group = jax.ShapeDtypeStruct((len(rows) // 2 * tiles, LANES), jnp.float32)
    row_tag = jax.ShapeDtypeStruct((tiles * LANES, LANES), jnp.float32)
    out_shape = [best] * cols + ([group] + [row_tag] * len(rows) if own_first else [group] * 2)
    inside = pl.BlockSpec(memory_space=pltpu.VMEM)
    found = pl.pallas_call(
        functools.partial(
            score_kernel,
            len(keys),
            cols,
            [len(row) for row in parts],
            len(known),
            own_first,
        ),
        in_specs=[inside] * len(operands),
        out_specs=[inside] * len(out_shape),
        out_shape=out_shape,
        compiler_params=pltpu.CompilerParams(vmem_limit_bytes=VMEM_LIMIT),
        cost_estimate=pl.CostEstimate(flops=0, bytes_accessed=0, transcendentals=0),
    )(*operands)
    return list(found[:cols]), list(found[cols:])


def owner_steps(count):
    half = count // 2
    circle = [count - 1 - 2 * i for i in range(half)] + [count - 2 - 2 * i for i in range(half)]
    return [
        [(circle[i], circle[(i + step) % count]) for i in range(count)]
        for step in range(1, half + 1)
    ]


def per_device(embeddings, basis, owner_ids, sub_cluster):
    row_count = embeddings.shape[0]
    tiles = row_count // LANES
    split_count, owner_count = lax.axis_size("split"), lax.axis_size("owners")

    def swap(block, offset):
        return lax.ppermute(block, "split", [(s, s ^ offset) for s in range(split_count)])

    def halves(block):
        return block[: row_count // 2], block[row_count // 2 :]

    own = project(embeddings, basis, owner_ids, sub_cluster)
    *steps, last = owner_steps(owner_count)
    keys = [lax.ppermute(own, "owners", step) for step in steps]
    nearby = lax.ppermute(own, "owners", last)
    offsets = range(2, split_count, 2)
    one_turn = 1 + (lax.axis_index("groups") >> 16)
    besides = lax.fori_loop(
        0,
        one_turn,
        lambda _, blocks: [swap(block, offset) for block, offset in zip(blocks, offsets)],
        [own] * len(offsets),
    )
    rows = [own, *besides, swap(own, 1)]
    rows += [tuple(swap(part, 1) for part in halves(beside)) for beside in besides]
    _, (own_best, *row_tags) = score([own], rows)
    _, row_best = score([nearby], rows, known=[own_best], row_tags=row_tags)
    backs = []
    for key, step in zip(keys, steps):
        (found,), row_best = score([key], rows, cols=1, known=row_best, row_tags=row_tags)
        backs.append(lax.ppermute(found, "owners", [(b, a) for a, b in step]))
    local = jnp.maximum(row_best[0], swap(row_best[1], 1))
    best = local[:tiles]
    for at, offset in enumerate(offsets, start=1):
        best = jnp.maximum(best, swap(local[at * tiles : (at + 1) * tiles], offset))
    for back in backs:
        best = jnp.maximum(best, back)
    return jnp.maximum(best, -1.0).reshape(row_count)


def solution(mesh):
    placed = (
        P(("groups", "owners", "split"), None),
        P(),
        P(("groups", "owners", "split"), None),
        P(("groups", "owners", "split")),
    )
    return jax.shard_map(
        per_device,
        mesh=mesh,
        in_specs=placed,
        out_specs=P(("groups", "owners", "split")),
        check_vma=False,
    )
```

```python
import functools

import jax
import jax.numpy as jnp
from jax import lax
from jax.experimental import pallas as pl
from jax.experimental.pallas import tpu as pltpu
from jax.sharding import PartitionSpec as P

CPO = 8
LANES = 128
TAG_ROWS = 16
ABSENT = -2.0
STEPS = 8
ROW_PARTS = 4
VMEM_LIMIT = 48 * 1024 * 1024


def project_kernel(source_hbm, basis_hbm, owner_hbm, sub_hbm, packed_ref, *scratch):
    source, basis, owner, sub, sems, tag_sems = scratch
    row_count, depth = source.shape
    width = basis.shape[1]
    spans = cut(depth, STEPS)
    copies = [
        (
            pltpu.make_async_copy(basis_hbm.at[span, :], basis.at[span, :], sems.at[0, step]),
            pltpu.make_async_copy(source_hbm.at[:, span], source.at[:, span], sems.at[1, step]),
        )
        for step, span in enumerate(spans)
    ]
    tag_copies = [
        pltpu.make_async_copy(owner_hbm, owner, tag_sems.at[0]),
        pltpu.make_async_copy(sub_hbm, sub, tag_sems.at[1]),
    ]
    for copy in [copy for pair in copies for copy in pair] + tag_copies:
        copy.start()
    totals = [None] * ROW_PARTS
    for span, pair in zip(spans, copies):
        for copy in pair:
            copy.wait()
        for at, rows in enumerate(cut(row_count, ROW_PARTS)):
            part = jnp.dot(source[rows, span], basis[span, :], preferred_element_type=jnp.float32)
            totals[at] = part if totals[at] is None else totals[at] + part
    for projected, rows in zip(totals, cut(row_count, ROW_PARTS)):
        norms = jnp.sum(projected * projected, axis=1, keepdims=True)
        packed_ref[rows, :] = (projected * lax.rsqrt(norms + 1e-06)).astype(jnp.bfloat16)
    for copy in tag_copies:
        copy.wait()
    tags = (owner[...] * CPO + sub[...] + 1).astype(jnp.float32)
    tags = jnp.concatenate(
        [tags, jnp.zeros((TAG_ROWS - tags.shape[0], LANES), jnp.float32)], axis=0
    )
    tags = jnp.concatenate([tags, jnp.zeros((TAG_ROWS, width - LANES), jnp.float32)], axis=1)
    packed_ref[row_count:, :] = tags.astype(jnp.bfloat16)


def cut(size, steps):
    return [pl.ds(size // steps * step, size // steps) for step in range(steps)]


def project(embeddings, basis, owner_ids, sub_cluster):
    row_count, depth = embeddings.shape
    width = basis.shape[1]
    tag_shape = (row_count // LANES, LANES)
    return pl.pallas_call(
        project_kernel,
        in_specs=[pl.BlockSpec(memory_space=pltpu.HBM)] * 4,
        out_specs=pl.BlockSpec(memory_space=pltpu.VMEM),
        out_shape=jax.ShapeDtypeStruct((row_count + TAG_ROWS, width), jnp.bfloat16),
        scratch_shapes=[
            pltpu.VMEM((row_count, depth), jnp.bfloat16),
            pltpu.VMEM((depth, width), jnp.bfloat16),
            pltpu.VMEM(tag_shape, jnp.int32),
            pltpu.VMEM(tag_shape, jnp.int32),
            pltpu.SemaphoreType.DMA((2, STEPS)),
            pltpu.SemaphoreType.DMA((2,)),
        ],
        compiler_params=pltpu.CompilerParams(vmem_limit_bytes=VMEM_LIMIT),
        cost_estimate=pl.CostEstimate(
            flops=2 * row_count * depth * width,
            bytes_accessed=2 * depth * (row_count + width),
            transcendentals=0,
        ),
    )(
        *[
            pltpu.with_memory_space_constraint(array, pltpu.HBM)
            for array in (
                embeddings,
                basis,
                owner_ids.reshape(tag_shape),
                sub_cluster.reshape(tag_shape),
            )
        ]
    )


def score_kernel(key_count, cols, row_parts, known, own_first, *refs):
    refs = list(refs)
    group = len(row_parts) // 2
    key_refs = [refs.pop(0) for _ in range(key_count)]
    row_refs = [[refs.pop(0) for _ in range(parts)] for parts in row_parts]
    known_refs = [refs.pop(0) for _ in range(known)]
    col_refs = [refs.pop(0) for _ in range(cols)]
    row_outs = refs
    row_count = key_refs[0].shape[0] - TAG_ROWS
    tiles = row_count // LANES
    best = [
        [jnp.full((8, LANES), ABSENT, jnp.float32) for _ in range(tiles)]
        for _ in range(key_count if own_first else cols)
    ]
    for block, part_refs in enumerate(row_refs):
        tag_ref = part_refs[-1]
        row_tags = tag_ref[tag_ref.shape[0] - TAG_ROWS :, :LANES].astype(jnp.float32)
        place = 0
        for part_ref in part_refs:
            count = part_ref.shape[0] // LANES * LANES
            tags = [
                jnp.broadcast_to(row_tags[at : at + 1, :], (LANES, LANES)).T
                for at in range(place, place + count // LANES)
            ]
            across = [None] * len(tags)
            for key, key_ref in enumerate(key_refs):
                key_tags = key_ref[row_count:, :LANES].astype(jnp.float32)
                scores = lax.dot_general(
                    part_ref[:count, :],
                    key_ref[:row_count, :],
                    (((1,), (1,)), ((), ())),
                    preferred_element_type=jnp.float32,
                )
                for tile, tag in enumerate(tags):
                    for at in range(tiles):
                        same = tag == key_tags[at : at + 1, :]
                        if own_first and block == 0 and at == place + tile:
                            same = same & (
                                lax.broadcasted_iota(jnp.int32, (LANES, LANES), 0)
                                != lax.broadcasted_iota(jnp.int32, (LANES, LANES), 1)
                            )
                        kept = scores[
                            tile * LANES : (tile + 1) * LANES, at * LANES : (at + 1) * LANES
                        ]
                        kept = jnp.where(same, kept, ABSENT)
                        if key < len(best):
                            best[key][at] = jnp.maximum(
                                best[key][at], jnp.max(kept.reshape(LANES // 8, 8, LANES), axis=0)
                            )
                        if not own_first:
                            across[tile] = (
                                kept if across[tile] is None else jnp.maximum(across[tile], kept)
                            )
            if not own_first:
                for tile in range(len(tags)):
                    at = block % group * tiles + place + tile
                    found = jnp.max(across[tile].T, axis=0, keepdims=True)
                    if block // group < known:
                        found = jnp.maximum(found, known_refs[block // group][at : at + 1, :])
                    row_outs[block // group][at : at + 1, :] = found
            place += len(tags)
    for key, found in enumerate(best):
        for at in range(tiles):
            highest = jnp.max(found[at], axis=0, keepdims=True)
            if own_first:
                row_outs[0][at : at + 1, :] = highest
            else:
                col_refs[key][at : at + 1, :] = highest
    if own_first:
        rest = row_outs[0].shape[0] - tiles
        row_outs[0][tiles:, :] = jnp.full((rest, LANES), ABSENT, jnp.float32)


def score(keys, rows, cols=0, known=(), own_first=False):
    parts = [row if isinstance(row, tuple) else (row,) for row in rows]
    operands = [*keys, *(part for row in parts for part in row)]
    operands += known
    tiles = keys[0].shape[0] // LANES
    best = jax.ShapeDtypeStruct((tiles, LANES), jnp.float32)
    group = jax.ShapeDtypeStruct((len(rows) // 2 * tiles, LANES), jnp.float32)
    out_shape = [best] * cols + [group] * (1 if own_first else 2)
    inside = pl.BlockSpec(memory_space=pltpu.VMEM)
    found = pl.pallas_call(
        functools.partial(
            score_kernel,
            len(keys),
            cols,
            [len(row) for row in parts],
            len(known),
            own_first,
        ),
        in_specs=[inside] * len(operands),
        out_specs=[inside] * len(out_shape),
        out_shape=out_shape,
        compiler_params=pltpu.CompilerParams(vmem_limit_bytes=VMEM_LIMIT),
        cost_estimate=pl.CostEstimate(flops=0, bytes_accessed=0, transcendentals=0),
    )(*operands)
    return list(found[:cols]), list(found[cols:])


def owner_steps(count):
    half = count // 2
    circle = [count - 1 - 2 * i for i in range(half)] + [count - 2 - 2 * i for i in range(half)]
    return [
        [(circle[i], circle[(i + step) % count]) for i in range(count)]
        for step in range(1, half + 1)
    ]


def per_device(embeddings, basis, owner_ids, sub_cluster):
    row_count = embeddings.shape[0]
    tiles = row_count // LANES
    split_count, owner_count = lax.axis_size("split"), lax.axis_size("owners")

    def swap(block, offset):
        return lax.ppermute(block, "split", [(s, s ^ offset) for s in range(split_count)])

    def halves(block):
        return block[: row_count // 2], block[row_count // 2 :]

    own = project(embeddings, basis, owner_ids, sub_cluster)
    *steps, last = owner_steps(owner_count)
    keys = [lax.ppermute(own, "owners", step) for step in steps]
    nearby = lax.ppermute(own, "owners", last)
    offsets = range(2, split_count, 2)
    one_turn = 1 + (lax.axis_index("groups") >> 16)
    besides = lax.fori_loop(
        0,
        one_turn,
        lambda _, blocks: [swap(block, offset) for block, offset in zip(blocks, offsets)],
        [own] * len(offsets),
    )
    rows = [own, *besides, swap(own, 1)]
    rows += [tuple(swap(part, 1) for part in halves(beside)) for beside in besides]
    row_best, backs = [], []
    for key, step in zip(keys, steps):
        (found,), row_best = score([key], rows, cols=1, known=row_best)
        backs.append(lax.ppermute(found, "owners", [(b, a) for a, b in step]))
    _, row_best = score([nearby], rows, known=row_best)
    _, (own_best,) = score([own], rows, own_first=True)
    local = jnp.maximum(row_best[0], swap(row_best[1], 1))
    best = jnp.maximum(local[:tiles], own_best[:tiles])
    for at, offset in enumerate(offsets, start=1):
        best = jnp.maximum(best, swap(local[at * tiles : (at + 1) * tiles], offset))
    for back in backs:
        best = jnp.maximum(best, back)
    return jnp.maximum(best, -1.0).reshape(row_count)


def solution(mesh):
    placed = (
        P(("groups", "owners", "split"), None),
        P(),
        P(("groups", "owners", "split"), None),
        P(("groups", "owners", "split")),
    )
    return jax.shard_map(
        per_device,
        mesh=mesh,
        in_specs=placed,
        out_specs=P(("groups", "owners", "split")),
        check_vma=False,
    )
```

```python
import functools

import jax
import jax.numpy as jnp
from jax import lax
from jax.experimental import pallas as pl
from jax.experimental.pallas import tpu as pltpu
from jax.sharding import PartitionSpec as P

CPO = 8
LANES = 128
TAG_ROWS = 16
ABSENT = -2.0
STEPS = 16
ROW_PARTS = 2
VMEM_LIMIT = 48 * 1024 * 1024


def project_kernel(source_hbm, basis_hbm, owner_hbm, sub_hbm, packed_ref, *scratch):
    source, basis, owner, sub, sems, tag_sems = scratch
    row_count, depth = source.shape
    width = basis.shape[1]
    spans = cut(depth, STEPS)
    copies = [
        (
            pltpu.make_async_copy(basis_hbm.at[span, :], basis.at[span, :], sems.at[0, step]),
            pltpu.make_async_copy(source_hbm.at[:, span], source.at[:, span], sems.at[1, step]),
        )
        for step, span in enumerate(spans)
    ]
    tag_copies = [
        pltpu.make_async_copy(owner_hbm, owner, tag_sems.at[0]),
        pltpu.make_async_copy(sub_hbm, sub, tag_sems.at[1]),
    ]
    for copy in [copy for pair in copies for copy in pair] + tag_copies:
        copy.start()
    totals = [None] * ROW_PARTS
    for span, pair in zip(spans, copies):
        for copy in pair:
            copy.wait()
        for at, rows in enumerate(cut(row_count, ROW_PARTS)):
            part = jnp.dot(source[rows, span], basis[span, :], preferred_element_type=jnp.float32)
            totals[at] = part if totals[at] is None else totals[at] + part
    for projected, rows in zip(totals, cut(row_count, ROW_PARTS)):
        norms = jnp.sum(projected * projected, axis=1, keepdims=True)
        packed_ref[rows, :] = (projected * lax.rsqrt(norms + 1e-06)).astype(jnp.bfloat16)
    for copy in tag_copies:
        copy.wait()
    tags = (owner[...] * CPO + sub[...] + 1).astype(jnp.float32)
    tags = jnp.concatenate(
        [tags, jnp.zeros((TAG_ROWS - tags.shape[0], LANES), jnp.float32)], axis=0
    )
    tags = jnp.concatenate([tags, jnp.zeros((TAG_ROWS, width - LANES), jnp.float32)], axis=1)
    packed_ref[row_count:, :] = tags.astype(jnp.bfloat16)


def cut(size, steps):
    return [pl.ds(size // steps * step, size // steps) for step in range(steps)]


def project(embeddings, basis, owner_ids, sub_cluster):
    row_count, depth = embeddings.shape
    width = basis.shape[1]
    tag_shape = (row_count // LANES, LANES)
    return pl.pallas_call(
        project_kernel,
        in_specs=[pl.BlockSpec(memory_space=pltpu.HBM)] * 4,
        out_specs=pl.BlockSpec(memory_space=pltpu.VMEM),
        out_shape=jax.ShapeDtypeStruct((row_count + TAG_ROWS, width), jnp.bfloat16),
        scratch_shapes=[
            pltpu.VMEM((row_count, depth), jnp.bfloat16),
            pltpu.VMEM((depth, width), jnp.bfloat16),
            pltpu.VMEM(tag_shape, jnp.int32),
            pltpu.VMEM(tag_shape, jnp.int32),
            pltpu.SemaphoreType.DMA((2, STEPS)),
            pltpu.SemaphoreType.DMA((2,)),
        ],
        compiler_params=pltpu.CompilerParams(vmem_limit_bytes=VMEM_LIMIT),
        cost_estimate=pl.CostEstimate(
            flops=2 * row_count * depth * width,
            bytes_accessed=2 * depth * (row_count + width),
            transcendentals=0,
        ),
    )(
        *[
            pltpu.with_memory_space_constraint(array, pltpu.HBM)
            for array in (
                embeddings,
                basis,
                owner_ids.reshape(tag_shape),
                sub_cluster.reshape(tag_shape),
            )
        ]
    )


def score_kernel(key_count, cols, row_parts, known, own_first, *refs):
    refs = list(refs)
    group = len(row_parts) // 2
    key_refs = [refs.pop(0) for _ in range(key_count)]
    row_refs = [[refs.pop(0) for _ in range(parts)] for parts in row_parts]
    known_refs = [refs.pop(0) for _ in range(known)]
    col_refs = [refs.pop(0) for _ in range(cols)]
    row_outs = refs
    row_count = key_refs[0].shape[0] - TAG_ROWS
    tiles = row_count // LANES
    best = [
        [jnp.full((8, LANES), ABSENT, jnp.float32) for _ in range(tiles)]
        for _ in range(key_count if own_first else cols)
    ]
    for block, part_refs in enumerate(row_refs):
        tag_ref = part_refs[-1]
        row_tags = tag_ref[tag_ref.shape[0] - TAG_ROWS :, :LANES].astype(jnp.float32)
        place = 0
        for part_ref in part_refs:
            count = part_ref.shape[0] // LANES * LANES
            tags = [
                jnp.broadcast_to(row_tags[at : at + 1, :], (LANES, LANES)).T
                for at in range(place, place + count // LANES)
            ]
            across = [None] * len(tags)
            for key, key_ref in enumerate(key_refs):
                key_tags = key_ref[row_count:, :LANES].astype(jnp.float32)
                scores = lax.dot_general(
                    part_ref[:count, :],
                    key_ref[:row_count, :],
                    (((1,), (1,)), ((), ())),
                    preferred_element_type=jnp.float32,
                )
                for tile, tag in enumerate(tags):
                    for at in range(tiles):
                        same = tag == key_tags[at : at + 1, :]
                        if own_first and block == 0 and at == place + tile:
                            same = same & (
                                lax.broadcasted_iota(jnp.int32, (LANES, LANES), 0)
                                != lax.broadcasted_iota(jnp.int32, (LANES, LANES), 1)
                            )
                        kept = scores[
                            tile * LANES : (tile + 1) * LANES, at * LANES : (at + 1) * LANES
                        ]
                        kept = jnp.where(same, kept, ABSENT)
                        if key < len(best):
                            best[key][at] = jnp.maximum(
                                best[key][at], jnp.max(kept.reshape(LANES // 8, 8, LANES), axis=0)
                            )
                        if not own_first:
                            across[tile] = (
                                kept if across[tile] is None else jnp.maximum(across[tile], kept)
                            )
            if not own_first:
                for tile in range(len(tags)):
                    at = block % group * tiles + place + tile
                    found = jnp.max(across[tile].T, axis=0, keepdims=True)
                    if block // group < known:
                        found = jnp.maximum(found, known_refs[block // group][at : at + 1, :])
                    row_outs[block // group][at : at + 1, :] = found
            place += len(tags)
    for key, found in enumerate(best):
        for at in range(tiles):
            highest = jnp.max(found[at], axis=0, keepdims=True)
            if own_first:
                row_outs[0][at : at + 1, :] = highest
            else:
                col_refs[key][at : at + 1, :] = highest
    if own_first:
        rest = row_outs[0].shape[0] - tiles
        row_outs[0][tiles:, :] = jnp.full((rest, LANES), ABSENT, jnp.float32)


def score(keys, rows, cols=0, known=(), own_first=False):
    parts = [row if isinstance(row, tuple) else (row,) for row in rows]
    operands = [*keys, *(part for row in parts for part in row)]
    operands += known
    tiles = keys[0].shape[0] // LANES
    best = jax.ShapeDtypeStruct((tiles, LANES), jnp.float32)
    group = jax.ShapeDtypeStruct((len(rows) // 2 * tiles, LANES), jnp.float32)
    out_shape = [best] * cols + [group] * (1 if own_first else 2)
    inside = pl.BlockSpec(memory_space=pltpu.VMEM)
    found = pl.pallas_call(
        functools.partial(
            score_kernel,
            len(keys),
            cols,
            [len(row) for row in parts],
            len(known),
            own_first,
        ),
        in_specs=[inside] * len(operands),
        out_specs=[inside] * len(out_shape),
        out_shape=out_shape,
        compiler_params=pltpu.CompilerParams(vmem_limit_bytes=VMEM_LIMIT),
        cost_estimate=pl.CostEstimate(flops=0, bytes_accessed=0, transcendentals=0),
    )(*operands)
    return list(found[:cols]), list(found[cols:])


def owner_steps(count):
    half = count // 2
    circle = [count - 1 - 2 * i for i in range(half)] + [count - 2 - 2 * i for i in range(half)]
    return [
        [(circle[i], circle[(i + step) % count]) for i in range(count)]
        for step in range(1, half + 1)
    ]


def per_device(embeddings, basis, owner_ids, sub_cluster):
    row_count = embeddings.shape[0]
    tiles = row_count // LANES
    split_count, owner_count = lax.axis_size("split"), lax.axis_size("owners")

    def swap(block, offset):
        return lax.ppermute(block, "split", [(s, s ^ offset) for s in range(split_count)])

    def halves(block):
        return block[: row_count // 2], block[row_count // 2 :]

    own = project(embeddings, basis, owner_ids, sub_cluster)
    *steps, last = owner_steps(owner_count)
    keys = [lax.ppermute(own, "owners", step) for step in steps]
    nearby = lax.ppermute(own, "owners", last)
    offsets = range(2, split_count, 2)
    one_turn = 1 + (lax.axis_index("groups") >> 16)
    besides = lax.fori_loop(
        0,
        one_turn,
        lambda _, blocks: [swap(block, offset) for block, offset in zip(blocks, offsets)],
        [own] * len(offsets),
    )
    rows = [own, *besides, swap(own, 1)]
    rows += [tuple(swap(part, 1) for part in halves(beside)) for beside in besides]
    _, row_best = score([own], rows, own_first=True)
    backs = []
    for key, step in zip(keys, steps):
        (found,), row_best = score([key], rows, cols=1, known=row_best)
        backs.append(lax.ppermute(found, "owners", [(b, a) for a, b in step]))
    _, row_best = score([nearby], rows, known=row_best)

    def exchange_split(_, row_best):
        local = jnp.maximum(row_best[0], swap(row_best[1], 1))
        best = local[:tiles]
        for at, offset in enumerate(offsets, start=1):
            best = jnp.maximum(best, swap(local[at * tiles : (at + 1) * tiles], offset))
        return [jnp.concatenate([best, local[tiles:]]), local]

    best = lax.fori_loop(0, one_turn, exchange_split, row_best)[0][:tiles]
    for back in backs:
        best = jnp.maximum(best, back)
    return jnp.maximum(best, -1.0).reshape(row_count)


def solution(mesh):
    placed = (
        P(("groups", "owners", "split"), None),
        P(),
        P(("groups", "owners", "split"), None),
        P(("groups", "owners", "split")),
    )
    return jax.shard_map(
        per_device,
        mesh=mesh,
        in_specs=placed,
        out_specs=P(("groups", "owners", "split")),
        check_vma=False,
    )
```

```python
import functools

import jax
import jax.numpy as jnp
from jax import lax
from jax.experimental import pallas as pl
from jax.experimental.pallas import tpu as pltpu
from jax.sharding import PartitionSpec as P

CPO = 8
LANES = 128
TAG_ROWS = 16
ABSENT = -2.0
STEPS = 2
ROW_PARTS = 4
DEPTH_PARTS = 4
VMEM_LIMIT = 48 * 1024 * 1024


def project_kernel(source_hbm, basis_hbm, owner_hbm, sub_hbm, packed_ref, *scratch):
    source, basis, owner, sub, basis_sems, source_sems, tag_sems = scratch
    row_count, depth = source.shape
    width = basis.shape[1]
    spans, groups = cut(depth, STEPS), cut(row_count, ROW_PARTS)
    basis_copies = [
        pltpu.make_async_copy(basis_hbm.at[span, :], basis.at[span, :], basis_sems.at[step])
        for step, span in enumerate(spans)
    ]
    source_copies = [
        [
            pltpu.make_async_copy(
                source_hbm.at[rows, span], source.at[rows, span], source_sems.at[step, at]
            )
            for at, rows in enumerate(groups)
        ]
        for step, span in enumerate(spans)
    ]
    tag_copies = [
        pltpu.make_async_copy(owner_hbm, owner, tag_sems.at[0]),
        pltpu.make_async_copy(sub_hbm, sub, tag_sems.at[1]),
    ]
    for basis_copy, row_copies in zip(basis_copies, source_copies):
        basis_copy.start()
        for copy in row_copies:
            copy.start()
    for copy in tag_copies:
        copy.start()
    totals = [None] * ROW_PARTS
    for step, span in enumerate(spans):
        basis_copies[step].wait()
        for at, rows in enumerate(groups):
            source_copies[step][at].wait()
            chunk = depth // STEPS // DEPTH_PARTS
            for part in range(DEPTH_PARTS):
                here = pl.ds(span.start + part * chunk, chunk)
                found = jnp.dot(
                    source[rows, here], basis[here, :], preferred_element_type=jnp.float32
                )
                totals[at] = found if totals[at] is None else totals[at] + found
            if step == STEPS - 1:
                projected = totals[at]
                norms = jnp.sum(projected * projected, axis=1, keepdims=True)
                units = projected * lax.rsqrt(norms + 1e-06)
                packed_ref[rows, :] = units.astype(jnp.bfloat16)
    for copy in tag_copies:
        copy.wait()
    tags = (owner[...] * CPO + sub[...] + 1).astype(jnp.float32)
    tags = jnp.concatenate(
        [tags, jnp.zeros((TAG_ROWS - tags.shape[0], LANES), jnp.float32)], axis=0
    )
    tags = jnp.concatenate([tags, jnp.zeros((TAG_ROWS, width - LANES), jnp.float32)], axis=1)
    packed_ref[row_count:, :] = tags.astype(jnp.bfloat16)


def cut(size, steps):
    return [pl.ds(size // steps * step, size // steps) for step in range(steps)]


def project(embeddings, basis, owner_ids, sub_cluster):
    row_count, depth = embeddings.shape
    width = basis.shape[1]
    tag_shape = (row_count // LANES, LANES)
    return pl.pallas_call(
        project_kernel,
        in_specs=[pl.BlockSpec(memory_space=pltpu.HBM)] * 4,
        out_specs=pl.BlockSpec(memory_space=pltpu.VMEM),
        out_shape=jax.ShapeDtypeStruct((row_count + TAG_ROWS, width), jnp.bfloat16),
        scratch_shapes=[
            pltpu.VMEM((row_count, depth), jnp.bfloat16),
            pltpu.VMEM((depth, width), jnp.bfloat16),
            pltpu.VMEM(tag_shape, jnp.int32),
            pltpu.VMEM(tag_shape, jnp.int32),
            pltpu.SemaphoreType.DMA((STEPS,)),
            pltpu.SemaphoreType.DMA((STEPS, ROW_PARTS)),
            pltpu.SemaphoreType.DMA((2,)),
        ],
        compiler_params=pltpu.CompilerParams(vmem_limit_bytes=VMEM_LIMIT),
        cost_estimate=pl.CostEstimate(
            flops=2 * row_count * depth * width,
            bytes_accessed=2 * depth * (row_count + width),
            transcendentals=0,
        ),
    )(
        *[
            pltpu.with_memory_space_constraint(array, pltpu.HBM)
            for array in (
                embeddings,
                basis,
                owner_ids.reshape(tag_shape),
                sub_cluster.reshape(tag_shape),
            )
        ]
    )


def score_kernel(key_count, cols, row_parts, known, own_first, *refs):
    refs = list(refs)
    group = len(row_parts) // 2
    key_refs = [refs.pop(0) for _ in range(key_count)]
    row_refs = [[refs.pop(0) for _ in range(parts)] for parts in row_parts]
    known_refs = [refs.pop(0) for _ in range(known)]
    col_refs = [refs.pop(0) for _ in range(cols)]
    row_outs = refs
    row_count = key_refs[0].shape[0] - TAG_ROWS
    tiles = row_count // LANES
    best = [
        [jnp.full((8, LANES), ABSENT, jnp.float32) for _ in range(tiles)]
        for _ in range(key_count if own_first else cols)
    ]
    for block, part_refs in enumerate(row_refs):
        tag_ref = part_refs[-1]
        row_tags = tag_ref[tag_ref.shape[0] - TAG_ROWS :, :LANES].astype(jnp.float32)
        place = 0
        for part_ref in part_refs:
            count = part_ref.shape[0] // LANES * LANES
            tags = [
                jnp.broadcast_to(row_tags[at : at + 1, :], (LANES, LANES)).T
                for at in range(place, place + count // LANES)
            ]
            across = [None] * len(tags)
            for key, key_ref in enumerate(key_refs):
                key_tags = key_ref[row_count:, :LANES].astype(jnp.float32)
                scores = lax.dot_general(
                    part_ref[:count, :],
                    key_ref[:row_count, :],
                    (((1,), (1,)), ((), ())),
                    preferred_element_type=jnp.float32,
                )
                for tile, tag in enumerate(tags):
                    for at in range(tiles):
                        same = tag == key_tags[at : at + 1, :]
                        if own_first and block == 0 and at == place + tile:
                            same = same & (
                                lax.broadcasted_iota(jnp.int32, (LANES, LANES), 0)
                                != lax.broadcasted_iota(jnp.int32, (LANES, LANES), 1)
                            )
                        kept = scores[
                            tile * LANES : (tile + 1) * LANES, at * LANES : (at + 1) * LANES
                        ]
                        kept = jnp.where(same, kept, ABSENT)
                        if key < len(best):
                            best[key][at] = jnp.maximum(
                                best[key][at], jnp.max(kept.reshape(LANES // 8, 8, LANES), axis=0)
                            )
                        if not own_first:
                            across[tile] = (
                                kept if across[tile] is None else jnp.maximum(across[tile], kept)
                            )
            if not own_first:
                for tile in range(len(tags)):
                    at = block % group * tiles + place + tile
                    found = jnp.max(across[tile].T, axis=0, keepdims=True)
                    if block // group < known:
                        found = jnp.maximum(found, known_refs[block // group][at : at + 1, :])
                    row_outs[block // group][at : at + 1, :] = found
            place += len(tags)
    for key, found in enumerate(best):
        for at in range(tiles):
            highest = jnp.max(found[at], axis=0, keepdims=True)
            if own_first:
                row_outs[0][at : at + 1, :] = highest
            else:
                col_refs[key][at : at + 1, :] = highest
    if own_first:
        rest = row_outs[0].shape[0] - tiles
        row_outs[0][tiles:, :] = jnp.full((rest, LANES), ABSENT, jnp.float32)


def score(keys, rows, cols=0, known=(), own_first=False):
    parts = [row if isinstance(row, tuple) else (row,) for row in rows]
    operands = [*keys, *(part for row in parts for part in row)]
    operands += known
    tiles = keys[0].shape[0] // LANES
    best = jax.ShapeDtypeStruct((tiles, LANES), jnp.float32)
    group = jax.ShapeDtypeStruct((len(rows) // 2 * tiles, LANES), jnp.float32)
    out_shape = [best] * cols + [group] * (1 if own_first else 2)
    inside = pl.BlockSpec(memory_space=pltpu.VMEM)
    found = pl.pallas_call(
        functools.partial(
            score_kernel,
            len(keys),
            cols,
            [len(row) for row in parts],
            len(known),
            own_first,
        ),
        in_specs=[inside] * len(operands),
        out_specs=[inside] * len(out_shape),
        out_shape=out_shape,
        compiler_params=pltpu.CompilerParams(vmem_limit_bytes=VMEM_LIMIT),
        cost_estimate=pl.CostEstimate(flops=0, bytes_accessed=0, transcendentals=0),
    )(*operands)
    return list(found[:cols]), list(found[cols:])


def owner_steps(count):
    half = count // 2
    circle = [count - 1 - 2 * i for i in range(half)] + [count - 2 - 2 * i for i in range(half)]
    return [
        [(circle[i], circle[(i + step) % count]) for i in range(count)]
        for step in range(1, half + 1)
    ]


def per_device(embeddings, basis, owner_ids, sub_cluster):
    row_count = embeddings.shape[0]
    tiles = row_count // LANES
    split_count, owner_count = lax.axis_size("split"), lax.axis_size("owners")

    def swap(block, offset):
        return lax.ppermute(block, "split", [(s, s ^ offset) for s in range(split_count)])

    def halves(block):
        return block[: row_count // 2], block[row_count // 2 :]

    own = project(embeddings, basis, owner_ids, sub_cluster)
    *steps, last = owner_steps(owner_count)
    keys = [lax.ppermute(own, "owners", step) for step in steps]
    nearby = lax.ppermute(own, "owners", last)
    offsets = range(2, split_count, 2)
    one_turn = 1 + (lax.axis_index("groups") >> 16)
    besides = lax.fori_loop(
        0,
        one_turn,
        lambda _, blocks: [swap(block, offset) for block, offset in zip(blocks, offsets)],
        [own] * len(offsets),
    )
    rows = [own, *besides, swap(own, 1)]
    rows += [tuple(swap(part, 1) for part in halves(beside)) for beside in besides]
    row_best, backs = [], []
    for key, step in zip(keys, steps):
        (found,), row_best = score([key], rows, cols=1, known=row_best)
        backs.append(lax.ppermute(found, "owners", [(b, a) for a, b in step]))
    _, row_best = score([nearby], rows, known=row_best)
    _, (own_best,) = score([own], rows, own_first=True)
    local = jnp.maximum(row_best[0], swap(row_best[1], 1))
    best = jnp.maximum(local[:tiles], own_best[:tiles])
    for at, offset in enumerate(offsets, start=1):
        best = jnp.maximum(best, swap(local[at * tiles : (at + 1) * tiles], offset))
    for back in backs:
        best = jnp.maximum(best, back)
    return jnp.maximum(best, -1.0).reshape(row_count)


def solution(mesh):
    placed = (
        P(("groups", "owners", "split"), None),
        P(),
        P(("groups", "owners", "split"), None),
        P(("groups", "owners", "split")),
    )
    return jax.shard_map(
        per_device,
        mesh=mesh,
        in_specs=placed,
        out_specs=P(("groups", "owners", "split")),
        check_vma=False,
    )
```

```python
import functools

import jax
import jax.numpy as jnp
from jax import lax
from jax.experimental import pallas as pl
from jax.experimental.pallas import tpu as pltpu
from jax.sharding import PartitionSpec as P

CPO = 8
LANES = 128
TAG_ROWS = 16
ABSENT = -2.0
STEPS = 8
ROW_PARTS = 4
VMEM_LIMIT = 48 * 1024 * 1024


def project_kernel(source_hbm, basis_hbm, owner_hbm, sub_hbm, packed_ref, *scratch):
    source, basis, owner, sub, sems, tag_sems = scratch
    row_count, depth = source.shape
    width = basis.shape[1]
    spans = cut(depth, STEPS)
    copies = [
        (
            pltpu.make_async_copy(basis_hbm.at[span, :], basis.at[span, :], sems.at[0, step]),
            pltpu.make_async_copy(source_hbm.at[:, span], source.at[:, span], sems.at[1, step]),
        )
        for step, span in enumerate(spans)
    ]
    tag_copies = [
        pltpu.make_async_copy(owner_hbm, owner, tag_sems.at[0]),
        pltpu.make_async_copy(sub_hbm, sub, tag_sems.at[1]),
    ]
    for copy in [copy for pair in copies for copy in pair] + tag_copies:
        copy.start()
    totals = [None] * ROW_PARTS
    for span, pair in zip(spans, copies):
        for copy in pair:
            copy.wait()
        for at, rows in enumerate(cut(row_count, ROW_PARTS)):
            part = jnp.dot(source[rows, span], basis[span, :], preferred_element_type=jnp.float32)
            totals[at] = part if totals[at] is None else totals[at] + part
    for projected, rows in zip(totals, cut(row_count, ROW_PARTS)):
        norms = jnp.sum(projected * projected, axis=1, keepdims=True)
        packed_ref[rows, :] = (projected * lax.rsqrt(norms + 1e-06)).astype(jnp.bfloat16)
    for copy in tag_copies:
        copy.wait()
    tags = (owner[...] * CPO + sub[...] + 1).astype(jnp.float32)
    tags = jnp.concatenate(
        [tags, jnp.zeros((TAG_ROWS - tags.shape[0], LANES), jnp.float32)], axis=0
    )
    tags = jnp.concatenate([tags, jnp.zeros((TAG_ROWS, width - LANES), jnp.float32)], axis=1)
    packed_ref[row_count:, :] = tags.astype(jnp.bfloat16)


def cut(size, steps):
    return [pl.ds(size // steps * step, size // steps) for step in range(steps)]


def project(embeddings, basis, owner_ids, sub_cluster):
    row_count, depth = embeddings.shape
    width = basis.shape[1]
    tag_shape = (row_count // LANES, LANES)
    return pl.pallas_call(
        project_kernel,
        in_specs=[pl.BlockSpec(memory_space=pltpu.HBM)] * 4,
        out_specs=pl.BlockSpec(memory_space=pltpu.VMEM),
        out_shape=jax.ShapeDtypeStruct((row_count + TAG_ROWS, width), jnp.bfloat16),
        scratch_shapes=[
            pltpu.VMEM((row_count, depth), jnp.bfloat16),
            pltpu.VMEM((depth, width), jnp.bfloat16),
            pltpu.VMEM(tag_shape, jnp.int32),
            pltpu.VMEM(tag_shape, jnp.int32),
            pltpu.SemaphoreType.DMA((2, STEPS)),
            pltpu.SemaphoreType.DMA((2,)),
        ],
        compiler_params=pltpu.CompilerParams(vmem_limit_bytes=VMEM_LIMIT),
        cost_estimate=pl.CostEstimate(
            flops=2 * row_count * depth * width,
            bytes_accessed=2 * depth * (row_count + width),
            transcendentals=0,
        ),
    )(
        *[
            pltpu.with_memory_space_constraint(array, pltpu.HBM)
            for array in (
                embeddings,
                basis,
                owner_ids.reshape(tag_shape),
                sub_cluster.reshape(tag_shape),
            )
        ]
    )


def score_kernel(key_count, cols, row_parts, known, own_first, *refs):
    refs = list(refs)
    group = len(row_parts) // 2
    key_refs = [refs.pop(0) for _ in range(key_count)]
    row_refs = [[refs.pop(0) for _ in range(parts)] for parts in row_parts]
    known_refs = [refs.pop(0) for _ in range(known)]
    col_refs = [refs.pop(0) for _ in range(cols)]
    row_outs = refs
    row_count = key_refs[0].shape[0] - TAG_ROWS
    tiles = row_count // LANES
    best = [
        [jnp.full((8, LANES), ABSENT, jnp.float32) for _ in range(tiles)]
        for _ in range(key_count if own_first else cols)
    ]
    for block, part_refs in enumerate(row_refs):
        tag_ref = part_refs[-1]
        row_tags = tag_ref[tag_ref.shape[0] - TAG_ROWS :, :LANES].astype(jnp.float32)
        place = 0
        for part_ref in part_refs:
            count = part_ref.shape[0] // LANES * LANES
            tags = [
                jnp.broadcast_to(row_tags[at : at + 1, :], (LANES, LANES)).T
                for at in range(place, place + count // LANES)
            ]
            across = [None] * len(tags)
            for key, key_ref in enumerate(key_refs):
                key_tags = key_ref[row_count:, :LANES].astype(jnp.float32)
                scores = lax.dot_general(
                    part_ref[:count, :],
                    key_ref[:row_count, :],
                    (((1,), (1,)), ((), ())),
                    preferred_element_type=jnp.float32,
                )
                for tile, tag in enumerate(tags):
                    for at in range(tiles):
                        same = tag == key_tags[at : at + 1, :]
                        if own_first and block == 0 and at == place + tile:
                            same = same & (
                                lax.broadcasted_iota(jnp.int32, (LANES, LANES), 0)
                                != lax.broadcasted_iota(jnp.int32, (LANES, LANES), 1)
                            )
                        kept = scores[
                            tile * LANES : (tile + 1) * LANES, at * LANES : (at + 1) * LANES
                        ]
                        kept = jnp.where(same, kept, ABSENT)
                        if key < len(best):
                            best[key][at] = jnp.maximum(
                                best[key][at], jnp.max(kept.reshape(LANES // 8, 8, LANES), axis=0)
                            )
                        if not own_first:
                            across[tile] = (
                                kept if across[tile] is None else jnp.maximum(across[tile], kept)
                            )
            if not own_first:
                for tile in range(len(tags)):
                    at = block % group * tiles + place + tile
                    found = jnp.max(across[tile].T, axis=0, keepdims=True)
                    if block // group < known:
                        found = jnp.maximum(found, known_refs[block // group][at : at + 1, :])
                    row_outs[block // group][at : at + 1, :] = found
            place += len(tags)
    for key, found in enumerate(best):
        for at in range(tiles):
            highest = jnp.max(found[at], axis=0, keepdims=True)
            if own_first:
                row_outs[0][at : at + 1, :] = highest
            else:
                col_refs[key][at : at + 1, :] = highest
    if own_first:
        rest = row_outs[0].shape[0] - tiles
        row_outs[0][tiles:, :] = jnp.full((rest, LANES), ABSENT, jnp.float32)


def score(keys, rows, cols=0, known=(), own_first=False):
    parts = [row if isinstance(row, tuple) else (row,) for row in rows]
    operands = [*keys, *(part for row in parts for part in row)]
    operands += known
    tiles = keys[0].shape[0] // LANES
    best = jax.ShapeDtypeStruct((tiles, LANES), jnp.float32)
    group = jax.ShapeDtypeStruct((len(rows) // 2 * tiles, LANES), jnp.float32)
    out_shape = [best] * cols + [group] * (1 if own_first else 2)
    inside = pl.BlockSpec(memory_space=pltpu.VMEM)
    found = pl.pallas_call(
        functools.partial(
            score_kernel,
            len(keys),
            cols,
            [len(row) for row in parts],
            len(known),
            own_first,
        ),
        in_specs=[inside] * len(operands),
        out_specs=[inside] * len(out_shape),
        out_shape=out_shape,
        compiler_params=pltpu.CompilerParams(vmem_limit_bytes=VMEM_LIMIT),
        cost_estimate=pl.CostEstimate(flops=0, bytes_accessed=0, transcendentals=0),
    )(*operands)
    return list(found[:cols]), list(found[cols:])


def owner_steps(count):
    half = count // 2
    circle = [count - 1 - 2 * i for i in range(half)] + [count - 2 - 2 * i for i in range(half)]
    return [
        [(circle[i], circle[(i + step) % count]) for i in range(count)]
        for step in range(1, half + 1)
    ]


def per_device(embeddings, basis, owner_ids, sub_cluster):
    row_count = embeddings.shape[0]
    tiles = row_count // LANES
    split_count, owner_count = lax.axis_size("split"), lax.axis_size("owners")

    def swap(block, offset):
        return lax.ppermute(block, "split", [(s, s ^ offset) for s in range(split_count)])

    def halves(block):
        return block[: row_count // 2], block[row_count // 2 :]

    own = project(embeddings, basis, owner_ids, sub_cluster)
    *steps, last = owner_steps(owner_count)
    steps = [
        [(a * split_count + s, b * split_count + (s ^ 1)) for a, b in step for s in range(split_count)]
        for step in steps
    ]
    both = ("owners", "split")
    keys = [lax.ppermute(own, both, step) for step in steps]
    nearby = lax.ppermute(own, "owners", last)
    offsets = range(2, split_count, 2)
    one_turn = 1 + (lax.axis_index("groups") >> 16)
    besides = lax.fori_loop(
        0,
        one_turn,
        lambda _, blocks: [swap(block, offset) for block, offset in zip(blocks, offsets)],
        [own] * len(offsets),
    )
    rows = [own, *besides, swap(own, 1)]
    rows += [tuple(swap(part, 1) for part in halves(beside)) for beside in besides]
    row_best, backs = [], []
    for key, step in zip(keys, steps):
        (found,), row_best = score([key], rows, cols=1, known=row_best)
        backs.append(lax.ppermute(found, both, [(b, a) for a, b in step]))
    _, row_best = score([nearby], rows, known=row_best)
    _, (own_best,) = score([own], rows, own_first=True)
    local = jnp.maximum(row_best[0], swap(row_best[1], 1))
    best = jnp.maximum(local[:tiles], own_best[:tiles])
    for at, offset in enumerate(offsets, start=1):
        best = jnp.maximum(best, swap(local[at * tiles : (at + 1) * tiles], offset))
    for back in backs:
        best = jnp.maximum(best, back)
    return jnp.maximum(best, -1.0).reshape(row_count)


def solution(mesh):
    placed = (
        P(("groups", "owners", "split"), None),
        P(),
        P(("groups", "owners", "split"), None),
        P(("groups", "owners", "split")),
    )
    return jax.shard_map(
        per_device,
        mesh=mesh,
        in_specs=placed,
        out_specs=P(("groups", "owners", "split")),
        check_vma=False,
    )
```

```python
import functools

import jax
import jax.numpy as jnp
from jax import lax
from jax.experimental import pallas as pl
from jax.experimental.pallas import tpu as pltpu
from jax.sharding import PartitionSpec as P

CPO = 8
LANES = 128
TAG_ROWS = 16
ABSENT = -2.0
STEPS = 8
ROW_PARTS = 4
VMEM_LIMIT = 48 * 1024 * 1024


def project_kernel(source_hbm, basis_hbm, owner_hbm, sub_hbm, packed_ref, *scratch):
    source, basis, owner, sub, sems, tag_sems = scratch
    row_count, depth = source.shape
    width = basis.shape[1]
    spans = cut(depth, STEPS)
    copies = [
        (
            pltpu.make_async_copy(basis_hbm.at[span, :], basis.at[span, :], sems.at[0, step]),
            pltpu.make_async_copy(source_hbm.at[:, span], source.at[:, span], sems.at[1, step]),
        )
        for step, span in enumerate(spans)
    ]
    tag_copies = [
        pltpu.make_async_copy(owner_hbm, owner, tag_sems.at[0]),
        pltpu.make_async_copy(sub_hbm, sub, tag_sems.at[1]),
    ]
    for copy in [copy for pair in copies for copy in pair] + tag_copies:
        copy.start()
    totals = [None] * ROW_PARTS
    for span, pair in zip(spans, copies):
        for copy in pair:
            copy.wait()
        for at, rows in enumerate(cut(row_count, ROW_PARTS)):
            part = jnp.dot(source[rows, span], basis[span, :], preferred_element_type=jnp.float32)
            totals[at] = part if totals[at] is None else totals[at] + part
    for projected, rows in zip(totals, cut(row_count, ROW_PARTS)):
        norms = jnp.sum(projected * projected, axis=1, keepdims=True)
        packed_ref[rows, :] = (projected * lax.rsqrt(norms + 1e-06)).astype(jnp.bfloat16)
    for copy in tag_copies:
        copy.wait()
    tags = (owner[...] * CPO + sub[...] + 1).astype(jnp.float32)
    tags = jnp.concatenate(
        [tags, jnp.zeros((TAG_ROWS - tags.shape[0], LANES), jnp.float32)], axis=0
    )
    tags = jnp.concatenate([tags, jnp.zeros((TAG_ROWS, width - LANES), jnp.float32)], axis=1)
    packed_ref[row_count:, :] = tags.astype(jnp.bfloat16)


def cut(size, steps):
    return [pl.ds(size // steps * step, size // steps) for step in range(steps)]


def project(embeddings, basis, owner_ids, sub_cluster):
    row_count, depth = embeddings.shape
    width = basis.shape[1]
    tag_shape = (row_count // LANES, LANES)
    return pl.pallas_call(
        project_kernel,
        in_specs=[pl.BlockSpec(memory_space=pltpu.HBM)] * 4,
        out_specs=pl.BlockSpec(memory_space=pltpu.VMEM),
        out_shape=jax.ShapeDtypeStruct((row_count + TAG_ROWS, width), jnp.bfloat16),
        scratch_shapes=[
            pltpu.VMEM((row_count, depth), jnp.bfloat16),
            pltpu.VMEM((depth, width), jnp.bfloat16),
            pltpu.VMEM(tag_shape, jnp.int32),
            pltpu.VMEM(tag_shape, jnp.int32),
            pltpu.SemaphoreType.DMA((2, STEPS)),
            pltpu.SemaphoreType.DMA((2,)),
        ],
        compiler_params=pltpu.CompilerParams(vmem_limit_bytes=VMEM_LIMIT),
        cost_estimate=pl.CostEstimate(
            flops=2 * row_count * depth * width,
            bytes_accessed=2 * depth * (row_count + width),
            transcendentals=0,
        ),
    )(
        *[
            pltpu.with_memory_space_constraint(array, pltpu.HBM)
            for array in (
                embeddings,
                basis,
                owner_ids.reshape(tag_shape),
                sub_cluster.reshape(tag_shape),
            )
        ]
    )


def score_kernel(key_count, cols, row_parts, known, own_first, *refs):
    refs = list(refs)
    group = len(row_parts) // 2
    key_refs = [refs.pop(0) for _ in range(key_count)]
    row_refs = [[refs.pop(0) for _ in range(parts)] for parts in row_parts]
    known_refs = [refs.pop(0) for _ in range(known)]
    col_refs = [refs.pop(0) for _ in range(cols)]
    row_outs = refs
    row_count = key_refs[0].shape[0] - TAG_ROWS
    tiles = row_count // LANES
    best = [
        [jnp.full((8, LANES), ABSENT, jnp.float32) for _ in range(tiles)]
        for _ in range(key_count if own_first else cols)
    ]
    for block, part_refs in enumerate(row_refs):
        tag_ref = part_refs[-1]
        row_tags = tag_ref[tag_ref.shape[0] - TAG_ROWS :, :LANES].astype(jnp.float32)
        place = 0
        for part_ref in part_refs:
            count = part_ref.shape[0] // LANES * LANES
            tags = [
                jnp.broadcast_to(row_tags[at : at + 1, :], (LANES, LANES)).T
                for at in range(place, place + count // LANES)
            ]
            across = [None] * len(tags)
            for key, key_ref in enumerate(key_refs):
                key_tags = key_ref[row_count:, :LANES].astype(jnp.float32)
                scores = lax.dot_general(
                    part_ref[:count, :],
                    key_ref[:row_count, :],
                    (((1,), (1,)), ((), ())),
                    preferred_element_type=jnp.float32,
                )
                for tile, tag in enumerate(tags):
                    for at in range(tiles):
                        same = tag == key_tags[at : at + 1, :]
                        if own_first and block == 0 and at == place + tile:
                            same = same & (
                                lax.broadcasted_iota(jnp.int32, (LANES, LANES), 0)
                                != lax.broadcasted_iota(jnp.int32, (LANES, LANES), 1)
                            )
                        kept = scores[
                            tile * LANES : (tile + 1) * LANES, at * LANES : (at + 1) * LANES
                        ]
                        kept = jnp.where(same, kept, ABSENT)
                        if key < len(best):
                            best[key][at] = jnp.maximum(
                                best[key][at], jnp.max(kept.reshape(LANES // 8, 8, LANES), axis=0)
                            )
                        if not own_first:
                            across[tile] = (
                                kept if across[tile] is None else jnp.maximum(across[tile], kept)
                            )
            if not own_first:
                for tile in range(len(tags)):
                    at = block % group * tiles + place + tile
                    found = jnp.max(across[tile].T, axis=0, keepdims=True)
                    if block // group < known:
                        found = jnp.maximum(found, known_refs[block // group][at : at + 1, :])
                    row_outs[block // group][at : at + 1, :] = found
            place += len(tags)
    for key, found in enumerate(best):
        for at in range(tiles):
            highest = jnp.max(found[at], axis=0, keepdims=True)
            if own_first:
                row_outs[0][at : at + 1, :] = highest
            else:
                col_refs[key][at : at + 1, :] = highest
    if own_first:
        rest = row_outs[0].shape[0] - tiles
        row_outs[0][tiles:, :] = jnp.full((rest, LANES), ABSENT, jnp.float32)


def score(keys, rows, cols=0, known=(), own_first=False):
    parts = [row if isinstance(row, tuple) else (row,) for row in rows]
    operands = [*keys, *(part for row in parts for part in row)]
    operands += known
    tiles = keys[0].shape[0] // LANES
    best = jax.ShapeDtypeStruct((tiles, LANES), jnp.float32)
    group = jax.ShapeDtypeStruct((len(rows) // 2 * tiles, LANES), jnp.float32)
    out_shape = [best] * cols + [group] * (1 if own_first else 2)
    inside = pl.BlockSpec(memory_space=pltpu.VMEM)
    found = pl.pallas_call(
        functools.partial(
            score_kernel,
            len(keys),
            cols,
            [len(row) for row in parts],
            len(known),
            own_first,
        ),
        in_specs=[inside] * len(operands),
        out_specs=[inside] * len(out_shape),
        out_shape=out_shape,
        compiler_params=pltpu.CompilerParams(vmem_limit_bytes=VMEM_LIMIT),
        cost_estimate=pl.CostEstimate(flops=0, bytes_accessed=0, transcendentals=0),
    )(*operands)
    return list(found[:cols]), list(found[cols:])


def owner_steps(count):
    half = count // 2
    circle = [count - 1 - 2 * i for i in range(half)] + [count - 2 - 2 * i for i in range(half)]
    return [
        [(circle[i], circle[(i + step) % count]) for i in range(count)]
        for step in range(1, half + 1)
    ]


def per_device(embeddings, basis, owner_ids, sub_cluster):
    row_count = embeddings.shape[0]
    tiles = row_count // LANES
    split_count, owner_count = lax.axis_size("split"), lax.axis_size("owners")

    def swap(block, offset):
        return lax.ppermute(block, "split", [(s, s ^ offset) for s in range(split_count)])

    def halves(block):
        return block[: row_count // 2], block[row_count // 2 :]

    own = project(embeddings, basis, owner_ids, sub_cluster)
    both = ("owners", "split")
    *steps, last = [
        [(a * split_count + s, b * split_count + (s ^ 1)) for a, b in step for s in range(split_count)]
        for step in owner_steps(owner_count)
    ]
    keys = [lax.ppermute(own, both, step) for step in steps]
    nearby = lax.ppermute(own, both, last)
    offsets = range(2, split_count, 2)
    one_turn = 1 + (lax.axis_index("groups") >> 16)
    besides = lax.fori_loop(
        0,
        one_turn,
        lambda _, blocks: [swap(block, offset) for block, offset in zip(blocks, offsets)],
        [own] * len(offsets),
    )
    rows = [own, *besides, swap(own, 1)]
    rows += [tuple(swap(part, 1) for part in halves(beside)) for beside in besides]
    row_best, backs = [], []
    for key, step in zip(keys, steps):
        (found,), row_best = score([key], rows, cols=1, known=row_best)
        backs.append(lax.ppermute(found, both, [(b, a) for a, b in step]))
    _, row_best = score([nearby], rows, known=row_best)
    _, (own_best,) = score([own], rows, own_first=True)
    local = jnp.maximum(row_best[0], swap(row_best[1], 1))
    best = jnp.maximum(local[:tiles], own_best[:tiles])
    for at, offset in enumerate(offsets, start=1):
        best = jnp.maximum(best, swap(local[at * tiles : (at + 1) * tiles], offset))
    for back in backs:
        best = jnp.maximum(best, back)
    return jnp.maximum(best, -1.0).reshape(row_count)


def solution(mesh):
    placed = (
        P(("groups", "owners", "split"), None),
        P(),
        P(("groups", "owners", "split"), None),
        P(("groups", "owners", "split")),
    )
    return jax.shard_map(
        per_device,
        mesh=mesh,
        in_specs=placed,
        out_specs=P(("groups", "owners", "split")),
        check_vma=False,
    )
```

```python
import functools

import jax
import jax.numpy as jnp
from jax import lax
from jax.experimental import pallas as pl
from jax.experimental.pallas import tpu as pltpu
from jax.sharding import PartitionSpec as P

CPO = 8
LANES = 128
TAG_ROWS = 16
ABSENT = -2.0
STEPS = 8
ROW_PARTS = 4
VMEM_LIMIT = 48 * 1024 * 1024


def project_kernel(source_hbm, basis_hbm, owner_hbm, sub_hbm, packed_ref, *scratch):
    source, basis, owner, sub, sems, tag_sems = scratch
    row_count, depth = source.shape
    width = basis.shape[1]
    spans = cut(depth, STEPS)
    copies = [
        (
            pltpu.make_async_copy(basis_hbm.at[span, :], basis.at[span, :], sems.at[0, step]),
            pltpu.make_async_copy(source_hbm.at[:, span], source.at[:, span], sems.at[1, step]),
        )
        for step, span in enumerate(spans)
    ]
    tag_copies = [
        pltpu.make_async_copy(owner_hbm, owner, tag_sems.at[0]),
        pltpu.make_async_copy(sub_hbm, sub, tag_sems.at[1]),
    ]
    for copy in [copy for pair in copies for copy in pair] + tag_copies:
        copy.start()
    totals = [None] * ROW_PARTS
    for span, pair in zip(spans, copies):
        for copy in pair:
            copy.wait()
        for at, rows in enumerate(cut(row_count, ROW_PARTS)):
            part = jnp.dot(source[rows, span], basis[span, :], preferred_element_type=jnp.float32)
            totals[at] = part if totals[at] is None else totals[at] + part
    for projected, rows in zip(totals, cut(row_count, ROW_PARTS)):
        norms = jnp.sum(projected * projected, axis=1, keepdims=True)
        packed_ref[rows, :] = (projected * lax.rsqrt(norms + 1e-06)).astype(jnp.bfloat16)
    for copy in tag_copies:
        copy.wait()
    tags = (owner[...] * CPO + sub[...] + 1).astype(jnp.float32)
    tags = jnp.concatenate(
        [tags, jnp.zeros((TAG_ROWS - tags.shape[0], LANES), jnp.float32)], axis=0
    )
    tags = jnp.concatenate([tags, jnp.zeros((TAG_ROWS, width - LANES), jnp.float32)], axis=1)
    packed_ref[row_count:, :] = tags.astype(jnp.bfloat16)


def cut(size, steps):
    return [pl.ds(size // steps * step, size // steps) for step in range(steps)]


def project(embeddings, basis, owner_ids, sub_cluster):
    row_count, depth = embeddings.shape
    width = basis.shape[1]
    tag_shape = (row_count // LANES, LANES)
    return pl.pallas_call(
        project_kernel,
        in_specs=[pl.BlockSpec(memory_space=pltpu.HBM)] * 4,
        out_specs=pl.BlockSpec(memory_space=pltpu.VMEM),
        out_shape=jax.ShapeDtypeStruct((row_count + TAG_ROWS, width), jnp.bfloat16),
        scratch_shapes=[
            pltpu.VMEM((row_count, depth), jnp.bfloat16),
            pltpu.VMEM((depth, width), jnp.bfloat16),
            pltpu.VMEM(tag_shape, jnp.int32),
            pltpu.VMEM(tag_shape, jnp.int32),
            pltpu.SemaphoreType.DMA((2, STEPS)),
            pltpu.SemaphoreType.DMA((2,)),
        ],
        compiler_params=pltpu.CompilerParams(vmem_limit_bytes=VMEM_LIMIT),
        cost_estimate=pl.CostEstimate(
            flops=2 * row_count * depth * width,
            bytes_accessed=2 * depth * (row_count + width),
            transcendentals=0,
        ),
    )(
        *[
            pltpu.with_memory_space_constraint(array, pltpu.HBM)
            for array in (
                embeddings,
                basis,
                owner_ids.reshape(tag_shape),
                sub_cluster.reshape(tag_shape),
            )
        ]
    )


def score_kernel(key_count, cols, row_parts, known, own_first, *refs):
    refs = list(refs)
    group = len(row_parts) // 2
    key_refs = [refs.pop(0) for _ in range(key_count)]
    row_refs = [[refs.pop(0) for _ in range(parts)] for parts in row_parts]
    known_refs = [refs.pop(0) for _ in range(known)]
    col_refs = [refs.pop(0) for _ in range(cols)]
    row_outs = refs
    row_count = key_refs[0].shape[0] - TAG_ROWS
    tiles = row_count // LANES
    best = [
        [jnp.full((8, LANES), ABSENT, jnp.float32) for _ in range(tiles)]
        for _ in range(key_count if own_first else cols)
    ]
    for block, part_refs in enumerate(row_refs):
        tag_ref = part_refs[-1]
        row_tags = tag_ref[tag_ref.shape[0] - TAG_ROWS :, :LANES].astype(jnp.float32)
        place = 0
        for part_ref in part_refs:
            count = part_ref.shape[0] // LANES * LANES
            tags = [
                jnp.broadcast_to(row_tags[at : at + 1, :], (LANES, LANES)).T
                for at in range(place, place + count // LANES)
            ]
            across = [None] * len(tags)
            for key, key_ref in enumerate(key_refs):
                key_tags = key_ref[row_count:, :LANES].astype(jnp.float32)
                scores = lax.dot_general(
                    part_ref[:count, :],
                    key_ref[:row_count, :],
                    (((1,), (1,)), ((), ())),
                    preferred_element_type=jnp.float32,
                )
                for tile, tag in enumerate(tags):
                    for at in range(tiles):
                        same = tag == key_tags[at : at + 1, :]
                        if own_first and block == 0 and at == place + tile:
                            same = same & (
                                lax.broadcasted_iota(jnp.int32, (LANES, LANES), 0)
                                != lax.broadcasted_iota(jnp.int32, (LANES, LANES), 1)
                            )
                        kept = scores[
                            tile * LANES : (tile + 1) * LANES, at * LANES : (at + 1) * LANES
                        ]
                        kept = jnp.where(same, kept, ABSENT)
                        if key < len(best):
                            best[key][at] = jnp.maximum(
                                best[key][at], jnp.max(kept.reshape(LANES // 8, 8, LANES), axis=0)
                            )
                        if not own_first:
                            across[tile] = (
                                kept if across[tile] is None else jnp.maximum(across[tile], kept)
                            )
            if not own_first:
                for tile in range(len(tags)):
                    at = block % group * tiles + place + tile
                    found = jnp.max(across[tile].T, axis=0, keepdims=True)
                    if block // group < known:
                        found = jnp.maximum(found, known_refs[block // group][at : at + 1, :])
                    row_outs[block // group][at : at + 1, :] = found
            place += len(tags)
    for key, found in enumerate(best):
        for at in range(tiles):
            highest = jnp.max(found[at], axis=0, keepdims=True)
            if own_first:
                row_outs[0][at : at + 1, :] = highest
            else:
                col_refs[key][at : at + 1, :] = highest
    if own_first:
        rest = row_outs[0].shape[0] - tiles
        row_outs[0][tiles:, :] = jnp.full((rest, LANES), ABSENT, jnp.float32)


def score(keys, rows, cols=0, known=(), own_first=False):
    parts = [row if isinstance(row, tuple) else (row,) for row in rows]
    operands = [*keys, *(part for row in parts for part in row)]
    operands += known
    tiles = keys[0].shape[0] // LANES
    best = jax.ShapeDtypeStruct((tiles, LANES), jnp.float32)
    group = jax.ShapeDtypeStruct((len(rows) // 2 * tiles, LANES), jnp.float32)
    out_shape = [best] * cols + [group] * (1 if own_first else 2)
    inside = pl.BlockSpec(memory_space=pltpu.VMEM)
    found = pl.pallas_call(
        functools.partial(
            score_kernel,
            len(keys),
            cols,
            [len(row) for row in parts],
            len(known),
            own_first,
        ),
        in_specs=[inside] * len(operands),
        out_specs=[inside] * len(out_shape),
        out_shape=out_shape,
        compiler_params=pltpu.CompilerParams(vmem_limit_bytes=VMEM_LIMIT),
        cost_estimate=pl.CostEstimate(flops=0, bytes_accessed=0, transcendentals=0),
    )(*operands)
    return list(found[:cols]), list(found[cols:])


def owner_steps(count):
    half = count // 2
    circle = [count - 1 - 2 * i for i in range(half)] + [count - 2 - 2 * i for i in range(half)]
    return [
        [(circle[i], circle[(i + step) % count]) for i in range(count)]
        for step in range(1, half + 1)
    ]


def per_device(embeddings, basis, owner_ids, sub_cluster):
    row_count = embeddings.shape[0]
    tiles = row_count // LANES
    split_count, owner_count = lax.axis_size("split"), lax.axis_size("owners")

    def swap(block, offset):
        return lax.ppermute(block, "split", [(s, s ^ offset) for s in range(split_count)])

    def halves(block):
        return block[: row_count // 2], block[row_count // 2 :]

    own = project(embeddings, basis, owner_ids, sub_cluster)
    both = ("owners", "split")
    *steps, last = [
        [(a * split_count + s, b * split_count + (s ^ 1)) for a, b in step for s in range(split_count)]
        for step in owner_steps(owner_count)
    ]
    keys = [lax.ppermute(own, both, step) for step in steps]
    nearby = lax.ppermute(own, both, last)
    offsets = range(2, split_count, 2)
    one_turn = 1 + (lax.axis_index("groups") >> 16)
    besides = lax.fori_loop(
        0,
        one_turn,
        lambda _, blocks: [swap(block, offset) for block, offset in zip(blocks, offsets)],
        [own] * len(offsets),
    )
    rows = [own, *besides, swap(own, 1)]
    rows += [tuple(swap(part, 1) for part in halves(beside)) for beside in besides]
    _, row_best = score([nearby], rows)
    backs = []
    for key, step in zip(keys, steps):
        (found,), row_best = score([key], rows, cols=1, known=row_best)
        backs.append(lax.ppermute(found, both, [(b, a) for a, b in step]))
    _, (own_best,) = score([own], rows, own_first=True)
    local = jnp.maximum(row_best[0], swap(row_best[1], 1))
    best = jnp.maximum(local[:tiles], own_best[:tiles])
    for at, offset in enumerate(offsets, start=1):
        best = jnp.maximum(best, swap(local[at * tiles : (at + 1) * tiles], offset))
    for back in backs:
        best = jnp.maximum(best, back)
    return jnp.maximum(best, -1.0).reshape(row_count)


def solution(mesh):
    placed = (
        P(("groups", "owners", "split"), None),
        P(),
        P(("groups", "owners", "split"), None),
        P(("groups", "owners", "split")),
    )
    return jax.shard_map(
        per_device,
        mesh=mesh,
        in_specs=placed,
        out_specs=P(("groups", "owners", "split")),
        check_vma=False,
    )
```

```python
import functools

import jax
import jax.numpy as jnp
from jax import lax
from jax.experimental import pallas as pl
from jax.experimental.pallas import tpu as pltpu
from jax.sharding import PartitionSpec as P

CPO = 8
LANES = 128
TAG_ROWS = 16
ABSENT = -2.0
STEPS = 8
ROW_PARTS = 4
VMEM_LIMIT = 48 * 1024 * 1024


def project_kernel(source_hbm, basis_hbm, owner_hbm, sub_hbm, packed_ref, *scratch):
    source, basis, owner, sub, sems, tag_sems = scratch
    row_count, depth = source.shape
    width = basis.shape[1]
    spans = cut(depth, STEPS)
    copies = [
        (
            pltpu.make_async_copy(basis_hbm.at[span, :], basis.at[span, :], sems.at[0, step]),
            pltpu.make_async_copy(source_hbm.at[:, span], source.at[:, span], sems.at[1, step]),
        )
        for step, span in enumerate(spans)
    ]
    tag_copies = [
        pltpu.make_async_copy(owner_hbm, owner, tag_sems.at[0]),
        pltpu.make_async_copy(sub_hbm, sub, tag_sems.at[1]),
    ]
    for copy in [copy for pair in copies for copy in pair] + tag_copies:
        copy.start()
    totals = [None] * ROW_PARTS
    for span, pair in zip(spans, copies):
        for copy in pair:
            copy.wait()
        for at, rows in enumerate(cut(row_count, ROW_PARTS)):
            part = jnp.dot(source[rows, span], basis[span, :], preferred_element_type=jnp.float32)
            totals[at] = part if totals[at] is None else totals[at] + part
    for projected, rows in zip(totals, cut(row_count, ROW_PARTS)):
        norms = jnp.sum(projected * projected, axis=1, keepdims=True)
        packed_ref[rows, :] = (projected * lax.rsqrt(norms + 1e-06)).astype(jnp.bfloat16)
    for copy in tag_copies:
        copy.wait()
    tags = (owner[...] * CPO + sub[...] + 1).astype(jnp.float32)
    tags = jnp.concatenate(
        [tags, jnp.zeros((TAG_ROWS - tags.shape[0], LANES), jnp.float32)], axis=0
    )
    tags = jnp.concatenate([tags, jnp.zeros((TAG_ROWS, width - LANES), jnp.float32)], axis=1)
    packed_ref[row_count:, :] = tags.astype(jnp.bfloat16)


def cut(size, steps):
    return [pl.ds(size // steps * step, size // steps) for step in range(steps)]


def project(embeddings, basis, owner_ids, sub_cluster):
    row_count, depth = embeddings.shape
    width = basis.shape[1]
    tag_shape = (row_count // LANES, LANES)
    return pl.pallas_call(
        project_kernel,
        in_specs=[pl.BlockSpec(memory_space=pltpu.HBM)] * 4,
        out_specs=pl.BlockSpec(memory_space=pltpu.VMEM),
        out_shape=jax.ShapeDtypeStruct((row_count + TAG_ROWS, width), jnp.bfloat16),
        scratch_shapes=[
            pltpu.VMEM((row_count, depth), jnp.bfloat16),
            pltpu.VMEM((depth, width), jnp.bfloat16),
            pltpu.VMEM(tag_shape, jnp.int32),
            pltpu.VMEM(tag_shape, jnp.int32),
            pltpu.SemaphoreType.DMA((2, STEPS)),
            pltpu.SemaphoreType.DMA((2,)),
        ],
        compiler_params=pltpu.CompilerParams(vmem_limit_bytes=VMEM_LIMIT),
        cost_estimate=pl.CostEstimate(
            flops=2 * row_count * depth * width,
            bytes_accessed=2 * depth * (row_count + width),
            transcendentals=0,
        ),
    )(
        *[
            pltpu.with_memory_space_constraint(array, pltpu.HBM)
            for array in (
                embeddings,
                basis,
                owner_ids.reshape(tag_shape),
                sub_cluster.reshape(tag_shape),
            )
        ]
    )


def score_kernel(key_count, cols, row_parts, known, own_first, *refs):
    refs = list(refs)
    group = len(row_parts) // 2
    key_refs = [refs.pop(0) for _ in range(key_count)]
    row_refs = [[refs.pop(0) for _ in range(parts)] for parts in row_parts]
    known_refs = [refs.pop(0) for _ in range(known)]
    col_refs = [refs.pop(0) for _ in range(cols)]
    row_outs = refs
    row_count = key_refs[0].shape[0] - TAG_ROWS
    tiles = row_count // LANES
    best = [
        [jnp.full((8, LANES), ABSENT, jnp.float32) for _ in range(tiles)]
        for _ in range(key_count if own_first else cols)
    ]
    for block, part_refs in enumerate(row_refs):
        tag_ref = part_refs[-1]
        row_tags = tag_ref[tag_ref.shape[0] - TAG_ROWS :, :LANES].astype(jnp.float32)
        place = 0
        for part_ref in part_refs:
            count = part_ref.shape[0] // LANES * LANES
            tags = [
                jnp.broadcast_to(row_tags[at : at + 1, :], (LANES, LANES)).T
                for at in range(place, place + count // LANES)
            ]
            across = [None] * len(tags)
            for key, key_ref in enumerate(key_refs):
                key_tags = key_ref[row_count:, :LANES].astype(jnp.float32)
                scores = lax.dot_general(
                    part_ref[:count, :],
                    key_ref[:row_count, :],
                    (((1,), (1,)), ((), ())),
                    preferred_element_type=jnp.float32,
                )
                for tile, tag in enumerate(tags):
                    for at in range(tiles):
                        same = tag == key_tags[at : at + 1, :]
                        if own_first and block == 0 and at == place + tile:
                            same = same & (
                                lax.broadcasted_iota(jnp.int32, (LANES, LANES), 0)
                                != lax.broadcasted_iota(jnp.int32, (LANES, LANES), 1)
                            )
                        kept = scores[
                            tile * LANES : (tile + 1) * LANES, at * LANES : (at + 1) * LANES
                        ]
                        kept = jnp.where(same, kept, ABSENT)
                        if key < len(best):
                            best[key][at] = jnp.maximum(
                                best[key][at], jnp.max(kept.reshape(LANES // 8, 8, LANES), axis=0)
                            )
                        if not own_first:
                            across[tile] = (
                                kept if across[tile] is None else jnp.maximum(across[tile], kept)
                            )
            if not own_first:
                for tile in range(len(tags)):
                    at = block % group * tiles + place + tile
                    found = jnp.max(across[tile].T, axis=0, keepdims=True)
                    if block // group < known:
                        found = jnp.maximum(found, known_refs[block // group][at : at + 1, :])
                    row_outs[block // group][at : at + 1, :] = found
            place += len(tags)
    for key, found in enumerate(best):
        for at in range(tiles):
            highest = jnp.max(found[at], axis=0, keepdims=True)
            if own_first:
                row_outs[0][at : at + 1, :] = highest
            else:
                col_refs[key][at : at + 1, :] = highest
    if own_first:
        rest = row_outs[0].shape[0] - tiles
        row_outs[0][tiles:, :] = jnp.full((rest, LANES), ABSENT, jnp.float32)


def score(keys, rows, cols=0, known=(), own_first=False):
    parts = [row if isinstance(row, tuple) else (row,) for row in rows]
    operands = [*keys, *(part for row in parts for part in row)]
    operands += known
    tiles = keys[0].shape[0] // LANES
    best = jax.ShapeDtypeStruct((tiles, LANES), jnp.float32)
    group = jax.ShapeDtypeStruct((len(rows) // 2 * tiles, LANES), jnp.float32)
    out_shape = [best] * cols + [group] * (1 if own_first else 2)
    inside = pl.BlockSpec(memory_space=pltpu.VMEM)
    found = pl.pallas_call(
        functools.partial(
            score_kernel,
            len(keys),
            cols,
            [len(row) for row in parts],
            len(known),
            own_first,
        ),
        in_specs=[inside] * len(operands),
        out_specs=[inside] * len(out_shape),
        out_shape=out_shape,
        compiler_params=pltpu.CompilerParams(vmem_limit_bytes=VMEM_LIMIT),
        cost_estimate=pl.CostEstimate(flops=0, bytes_accessed=0, transcendentals=0),
    )(*operands)
    return list(found[:cols]), list(found[cols:])


def owner_steps(count):
    half = count // 2
    circle = [count - 1 - 2 * i for i in range(half)] + [count - 2 - 2 * i for i in range(half)]
    return [
        [(circle[i], circle[(i + step) % count]) for i in range(count)]
        for step in range(1, half + 1)
    ]


def per_device(embeddings, basis, owner_ids, sub_cluster):
    row_count = embeddings.shape[0]
    tiles = row_count // LANES
    split_count, owner_count = lax.axis_size("split"), lax.axis_size("owners")

    def swap(block, offset):
        return lax.ppermute(block, "split", [(s, s ^ offset) for s in range(split_count)])

    def halves(block):
        return block[: row_count // 2], block[row_count // 2 :]

    own = project(embeddings, basis, owner_ids, sub_cluster)
    both = ("owners", "split")
    *steps, last = [
        [(a * split_count + s, b * split_count + (s ^ 1)) for a, b in step for s in range(split_count)]
        for step in owner_steps(owner_count)
    ]
    keys = [lax.ppermute(own, both, step) for step in steps]
    nearby = lax.ppermute(own, both, last)
    offsets = range(2, split_count, 2)
    one_turn = 1 + (lax.axis_index("groups") >> 16)
    besides = lax.fori_loop(
        0,
        one_turn,
        lambda _, blocks: [swap(block, offset) for block, offset in zip(blocks, offsets)],
        [own] * len(offsets),
    )
    across = [tuple(swap(part, 1) for part in halves(beside)) for beside in besides]
    rows = [own, *across, swap(own, 1), *besides]
    row_best, backs = [], []
    for key, step in zip(keys, steps):
        (found,), row_best = score([key], rows, cols=1, known=row_best)
        backs.append(lax.ppermute(found, both, [(b, a) for a, b in step]))
    _, row_best = score([nearby], rows, known=row_best)
    _, (own_best,) = score([own], rows, own_first=True)
    local = jnp.maximum(row_best[0], swap(row_best[1], 1))
    best = jnp.maximum(local[:tiles], own_best[:tiles])
    for at, offset in enumerate(offsets, start=1):
        best = jnp.maximum(best, swap(local[at * tiles : (at + 1) * tiles], offset + 1))
    for back in backs:
        best = jnp.maximum(best, back)
    return jnp.maximum(best, -1.0).reshape(row_count)


def solution(mesh):
    placed = (
        P(("groups", "owners", "split"), None),
        P(),
        P(("groups", "owners", "split"), None),
        P(("groups", "owners", "split")),
    )
    return jax.shard_map(
        per_device,
        mesh=mesh,
        in_specs=placed,
        out_specs=P(("groups", "owners", "split")),
        check_vma=False,
    )
```

```python
import functools

import jax
import jax.numpy as jnp
from jax import lax
from jax.experimental import pallas as pl
from jax.experimental.pallas import tpu as pltpu
from jax.sharding import PartitionSpec as P

CPO = 8
LANES = 128
TAG_ROWS = 16
ABSENT = -2.0
STEPS = 8
ROW_PARTS = 4
VMEM_LIMIT = 48 * 1024 * 1024


def project_kernel(source_hbm, basis_hbm, owner_hbm, sub_hbm, packed_ref, *scratch):
    source, basis, owner, sub, sems, tag_sems = scratch
    row_count, depth = source.shape
    width = basis.shape[1]
    spans = cut(depth, STEPS)
    copies = [
        (
            pltpu.make_async_copy(basis_hbm.at[span, :], basis.at[span, :], sems.at[0, step]),
            pltpu.make_async_copy(source_hbm.at[:, span], source.at[:, span], sems.at[1, step]),
        )
        for step, span in enumerate(spans)
    ]
    tag_copies = [
        pltpu.make_async_copy(owner_hbm, owner, tag_sems.at[0]),
        pltpu.make_async_copy(sub_hbm, sub, tag_sems.at[1]),
    ]
    for copy in [copy for pair in copies for copy in pair] + tag_copies:
        copy.start()
    totals = [None] * ROW_PARTS
    for span, pair in zip(spans, copies):
        for copy in pair:
            copy.wait()
        for at, rows in enumerate(cut(row_count, ROW_PARTS)):
            part = jnp.dot(source[rows, span], basis[span, :], preferred_element_type=jnp.float32)
            totals[at] = part if totals[at] is None else totals[at] + part
    for projected, rows in zip(totals, cut(row_count, ROW_PARTS)):
        norms = jnp.sum(projected * projected, axis=1, keepdims=True)
        packed_ref[rows, :] = (projected * lax.rsqrt(norms + 1e-06)).astype(jnp.bfloat16)
    for copy in tag_copies:
        copy.wait()
    tags = (owner[...] * CPO + sub[...] + 1).astype(jnp.float32)
    tags = jnp.concatenate(
        [tags, jnp.zeros((TAG_ROWS - tags.shape[0], LANES), jnp.float32)], axis=0
    )
    tags = jnp.concatenate([tags, jnp.zeros((TAG_ROWS, width - LANES), jnp.float32)], axis=1)
    packed_ref[row_count:, :] = tags.astype(jnp.bfloat16)


def cut(size, steps):
    return [pl.ds(size // steps * step, size // steps) for step in range(steps)]


def project(embeddings, basis, owner_ids, sub_cluster):
    row_count, depth = embeddings.shape
    width = basis.shape[1]
    tag_shape = (row_count // LANES, LANES)
    return pl.pallas_call(
        project_kernel,
        in_specs=[pl.BlockSpec(memory_space=pltpu.HBM)] * 4,
        out_specs=pl.BlockSpec(memory_space=pltpu.VMEM),
        out_shape=jax.ShapeDtypeStruct((row_count + TAG_ROWS, width), jnp.bfloat16),
        scratch_shapes=[
            pltpu.VMEM((row_count, depth), jnp.bfloat16),
            pltpu.VMEM((depth, width), jnp.bfloat16),
            pltpu.VMEM(tag_shape, jnp.int32),
            pltpu.VMEM(tag_shape, jnp.int32),
            pltpu.SemaphoreType.DMA((2, STEPS)),
            pltpu.SemaphoreType.DMA((2,)),
        ],
        compiler_params=pltpu.CompilerParams(vmem_limit_bytes=VMEM_LIMIT),
        cost_estimate=pl.CostEstimate(
            flops=2 * row_count * depth * width,
            bytes_accessed=2 * depth * (row_count + width),
            transcendentals=0,
        ),
    )(
        *[
            pltpu.with_memory_space_constraint(array, pltpu.HBM)
            for array in (
                embeddings,
                basis,
                owner_ids.reshape(tag_shape),
                sub_cluster.reshape(tag_shape),
            )
        ]
    )


def score_kernel(key_count, cols, row_parts, known, own_first, *refs):
    refs = list(refs)
    group = len(row_parts) // 2
    key_refs = [refs.pop(0) for _ in range(key_count)]
    row_refs = [[refs.pop(0) for _ in range(parts)] for parts in row_parts]
    known_refs = [refs.pop(0) for _ in range(known)]
    col_refs = [refs.pop(0) for _ in range(cols)]
    row_outs = refs
    row_count = key_refs[0].shape[0] - TAG_ROWS
    tiles = row_count // LANES
    best = [
        [jnp.full((8, LANES), ABSENT, jnp.float32) for _ in range(tiles)]
        for _ in range(key_count if own_first else cols)
    ]
    for block, part_refs in enumerate(row_refs):
        tag_ref = part_refs[-1]
        row_tags = tag_ref[tag_ref.shape[0] - TAG_ROWS :, :LANES].astype(jnp.float32)
        place = 0
        for part_ref in part_refs:
            count = part_ref.shape[0] // LANES * LANES
            tags = [
                jnp.broadcast_to(row_tags[at : at + 1, :], (LANES, LANES)).T
                for at in range(place, place + count // LANES)
            ]
            across = [None] * len(tags)
            for key, key_ref in enumerate(key_refs):
                key_tags = key_ref[row_count:, :LANES].astype(jnp.float32)
                scores = lax.dot_general(
                    part_ref[:count, :],
                    key_ref[:row_count, :],
                    (((1,), (1,)), ((), ())),
                    preferred_element_type=jnp.float32,
                )
                for tile, tag in enumerate(tags):
                    for at in range(tiles):
                        same = tag == key_tags[at : at + 1, :]
                        if own_first and block == 0 and at == place + tile:
                            same = same & (
                                lax.broadcasted_iota(jnp.int32, (LANES, LANES), 0)
                                != lax.broadcasted_iota(jnp.int32, (LANES, LANES), 1)
                            )
                        kept = scores[
                            tile * LANES : (tile + 1) * LANES, at * LANES : (at + 1) * LANES
                        ]
                        kept = jnp.where(same, kept, ABSENT)
                        if key < len(best):
                            best[key][at] = jnp.maximum(
                                best[key][at], jnp.max(kept.reshape(LANES // 8, 8, LANES), axis=0)
                            )
                        if not own_first:
                            across[tile] = (
                                kept if across[tile] is None else jnp.maximum(across[tile], kept)
                            )
            if not own_first:
                for tile in range(len(tags)):
                    at = block % group * tiles + place + tile
                    found = jnp.max(across[tile].T, axis=0, keepdims=True)
                    if block // group < known:
                        found = jnp.maximum(found, known_refs[block // group][at : at + 1, :])
                    row_outs[block // group][at : at + 1, :] = found
            place += len(tags)
    for key, found in enumerate(best):
        for at in range(tiles):
            highest = jnp.max(found[at], axis=0, keepdims=True)
            if own_first:
                row_outs[0][at : at + 1, :] = highest
            else:
                col_refs[key][at : at + 1, :] = highest
    if own_first:
        rest = row_outs[0].shape[0] - tiles
        row_outs[0][tiles:, :] = jnp.full((rest, LANES), ABSENT, jnp.float32)


def score(keys, rows, cols=0, known=(), own_first=False):
    parts = [row if isinstance(row, tuple) else (row,) for row in rows]
    operands = [*keys, *(part for row in parts for part in row)]
    operands += known
    tiles = keys[0].shape[0] // LANES
    best = jax.ShapeDtypeStruct((tiles, LANES), jnp.float32)
    group = jax.ShapeDtypeStruct((len(rows) // 2 * tiles, LANES), jnp.float32)
    out_shape = [best] * cols + [group] * (1 if own_first else 2)
    inside = pl.BlockSpec(memory_space=pltpu.VMEM)
    found = pl.pallas_call(
        functools.partial(
            score_kernel,
            len(keys),
            cols,
            [len(row) for row in parts],
            len(known),
            own_first,
        ),
        in_specs=[inside] * len(operands),
        out_specs=[inside] * len(out_shape),
        out_shape=out_shape,
        compiler_params=pltpu.CompilerParams(vmem_limit_bytes=VMEM_LIMIT),
        cost_estimate=pl.CostEstimate(flops=0, bytes_accessed=0, transcendentals=0),
    )(*operands)
    return list(found[:cols]), list(found[cols:])


def owner_steps(count):
    half = count // 2
    circle = [count - 1 - 2 * i for i in range(half)] + [count - 2 - 2 * i for i in range(half)]
    return [
        [(circle[i], circle[(i + step) % count]) for i in range(count)]
        for step in range(1, half + 1)
    ]


def per_device(embeddings, basis, owner_ids, sub_cluster):
    row_count = embeddings.shape[0]
    tiles = row_count // LANES
    split_count, owner_count = lax.axis_size("split"), lax.axis_size("owners")

    def swap(block, offset):
        return lax.ppermute(block, "split", [(s, s ^ offset) for s in range(split_count)])

    def halves(block):
        return block[: row_count // 2], block[row_count // 2 :]

    own = project(embeddings, basis, owner_ids, sub_cluster)
    both = ("owners", "split")
    *steps, last = [
        [(a * split_count + s, b * split_count + (s ^ 1)) for a, b in step for s in range(split_count)]
        for step in owner_steps(owner_count)
    ]
    keys = [lax.ppermute(own, both, step) for step in steps]
    nearby = lax.ppermute(own, both, last)
    offsets = range(2, split_count, 2)
    one_turn = 1 + (lax.axis_index("groups") >> 16)
    besides = lax.fori_loop(
        0,
        one_turn,
        lambda _, blocks: [swap(block, offset) for block, offset in zip(blocks, offsets)],
        [own] * len(offsets),
    )
    core, *across = [tuple(swap(part, 1) for part in halves(block)) for block in [own, *besides]]
    rows = [own, *across, core, *besides]
    row_best, backs = [], []
    for key, step in zip(keys, steps):
        (found,), row_best = score([key], rows, cols=1, known=row_best)
        backs.append(lax.ppermute(found, both, [(b, a) for a, b in step]))
    _, row_best = score([nearby], rows, known=row_best)
    _, (own_best,) = score([own], rows, own_first=True)
    local = jnp.maximum(row_best[0], swap(row_best[1], 1))
    best = jnp.maximum(local[:tiles], own_best[:tiles])
    for at, offset in enumerate(offsets, start=1):
        best = jnp.maximum(best, swap(local[at * tiles : (at + 1) * tiles], offset + 1))
    for back in backs:
        best = jnp.maximum(best, back)
    return jnp.maximum(best, -1.0).reshape(row_count)


def solution(mesh):
    placed = (
        P(("groups", "owners", "split"), None),
        P(),
        P(("groups", "owners", "split"), None),
        P(("groups", "owners", "split")),
    )
    return jax.shard_map(
        per_device,
        mesh=mesh,
        in_specs=placed,
        out_specs=P(("groups", "owners", "split")),
        check_vma=False,
    )
```

```python
import functools

import jax
import jax.numpy as jnp
from jax import lax
from jax.experimental import pallas as pl
from jax.experimental.pallas import tpu as pltpu
from jax.sharding import PartitionSpec as P

CPO = 8
LANES = 128
TAG_ROWS = 16
ABSENT = -2.0
STEPS = 8
ROW_PARTS = 4
VMEM_LIMIT = 48 * 1024 * 1024


def project_kernel(source_hbm, basis_hbm, owner_hbm, sub_hbm, packed_ref, *scratch):
    source, basis, owner, sub, sems, tag_sems = scratch
    row_count, depth = source.shape
    width = basis.shape[1]
    spans = cut(depth, STEPS)
    copies = [
        (
            pltpu.make_async_copy(basis_hbm.at[span, :], basis.at[span, :], sems.at[0, step]),
            pltpu.make_async_copy(source_hbm.at[:, span], source.at[:, span], sems.at[1, step]),
        )
        for step, span in enumerate(spans)
    ]
    tag_copies = [
        pltpu.make_async_copy(owner_hbm, owner, tag_sems.at[0]),
        pltpu.make_async_copy(sub_hbm, sub, tag_sems.at[1]),
    ]
    for copy in [copy for pair in copies for copy in pair] + tag_copies:
        copy.start()
    totals = [None] * ROW_PARTS
    for span, pair in zip(spans, copies):
        for copy in pair:
            copy.wait()
        for at, rows in enumerate(cut(row_count, ROW_PARTS)):
            part = jnp.dot(source[rows, span], basis[span, :], preferred_element_type=jnp.float32)
            totals[at] = part if totals[at] is None else totals[at] + part
    for projected, rows in zip(totals, cut(row_count, ROW_PARTS)):
        norms = jnp.sum(projected * projected, axis=1, keepdims=True)
        packed_ref[rows, :] = (projected * lax.rsqrt(norms + 1e-06)).astype(jnp.bfloat16)
    for copy in tag_copies:
        copy.wait()
    tags = (owner[...] * CPO + sub[...] + 1).astype(jnp.float32)
    tags = jnp.concatenate(
        [tags, jnp.zeros((TAG_ROWS - tags.shape[0], LANES), jnp.float32)], axis=0
    )
    tags = jnp.concatenate([tags, jnp.zeros((TAG_ROWS, width - LANES), jnp.float32)], axis=1)
    packed_ref[row_count:, :] = tags.astype(jnp.bfloat16)


def cut(size, steps):
    return [pl.ds(size // steps * step, size // steps) for step in range(steps)]


def project(embeddings, basis, owner_ids, sub_cluster):
    row_count, depth = embeddings.shape
    width = basis.shape[1]
    tag_shape = (row_count // LANES, LANES)
    return pl.pallas_call(
        project_kernel,
        in_specs=[pl.BlockSpec(memory_space=pltpu.HBM)] * 4,
        out_specs=pl.BlockSpec(memory_space=pltpu.VMEM),
        out_shape=jax.ShapeDtypeStruct((row_count + TAG_ROWS, width), jnp.bfloat16),
        scratch_shapes=[
            pltpu.VMEM((row_count, depth), jnp.bfloat16),
            pltpu.VMEM((depth, width), jnp.bfloat16),
            pltpu.VMEM(tag_shape, jnp.int32),
            pltpu.VMEM(tag_shape, jnp.int32),
            pltpu.SemaphoreType.DMA((2, STEPS)),
            pltpu.SemaphoreType.DMA((2,)),
        ],
        compiler_params=pltpu.CompilerParams(vmem_limit_bytes=VMEM_LIMIT),
        cost_estimate=pl.CostEstimate(
            flops=2 * row_count * depth * width,
            bytes_accessed=2 * depth * (row_count + width),
            transcendentals=0,
        ),
    )(
        *[
            pltpu.with_memory_space_constraint(array, pltpu.HBM)
            for array in (
                embeddings,
                basis,
                owner_ids.reshape(tag_shape),
                sub_cluster.reshape(tag_shape),
            )
        ]
    )


def score_kernel(key_count, cols, row_parts, known, own_first, *refs):
    refs = list(refs)
    group = len(row_parts) // 2
    key_refs = [refs.pop(0) for _ in range(key_count)]
    row_refs = [[refs.pop(0) for _ in range(parts)] for parts in row_parts]
    known_refs = [refs.pop(0) for _ in range(known)]
    col_refs = [refs.pop(0) for _ in range(cols)]
    row_outs = refs
    row_count = key_refs[0].shape[0] - TAG_ROWS
    tiles = row_count // LANES
    best = [
        [jnp.full((8, LANES), ABSENT, jnp.float32) for _ in range(tiles)]
        for _ in range(key_count if own_first else cols)
    ]
    for block, part_refs in enumerate(row_refs):
        tag_ref = part_refs[-1]
        row_tags = tag_ref[tag_ref.shape[0] - TAG_ROWS :, :LANES].astype(jnp.float32)
        place = 0
        for part_ref in part_refs:
            count = part_ref.shape[0] // LANES * LANES
            tags = [
                jnp.broadcast_to(row_tags[at : at + 1, :], (LANES, LANES)).T
                for at in range(place, place + count // LANES)
            ]
            across = [None] * len(tags)
            for key, key_ref in enumerate(key_refs):
                key_tags = key_ref[row_count:, :LANES].astype(jnp.float32)
                scores = lax.dot_general(
                    part_ref[:count, :],
                    key_ref[:row_count, :],
                    (((1,), (1,)), ((), ())),
                    preferred_element_type=jnp.float32,
                )
                for tile, tag in enumerate(tags):
                    for at in range(tiles):
                        same = tag == key_tags[at : at + 1, :]
                        if own_first and block == 0 and at == place + tile:
                            same = same & (
                                lax.broadcasted_iota(jnp.int32, (LANES, LANES), 0)
                                != lax.broadcasted_iota(jnp.int32, (LANES, LANES), 1)
                            )
                        kept = scores[
                            tile * LANES : (tile + 1) * LANES, at * LANES : (at + 1) * LANES
                        ]
                        kept = jnp.where(same, kept, ABSENT)
                        if key < len(best):
                            best[key][at] = jnp.maximum(
                                best[key][at], jnp.max(kept.reshape(LANES // 8, 8, LANES), axis=0)
                            )
                        if not own_first:
                            across[tile] = (
                                kept if across[tile] is None else jnp.maximum(across[tile], kept)
                            )
            if not own_first:
                for tile in range(len(tags)):
                    at = block % group * tiles + place + tile
                    found = jnp.max(across[tile].T, axis=0, keepdims=True)
                    if block // group < known:
                        found = jnp.maximum(found, known_refs[block // group][at : at + 1, :])
                    row_outs[block // group][at : at + 1, :] = found
            place += len(tags)
    for key, found in enumerate(best):
        for at in range(tiles):
            highest = jnp.max(found[at], axis=0, keepdims=True)
            if own_first:
                row_outs[0][at : at + 1, :] = highest
            else:
                col_refs[key][at : at + 1, :] = highest
    if own_first:
        rest = row_outs[0].shape[0] - tiles
        row_outs[0][tiles:, :] = jnp.full((rest, LANES), ABSENT, jnp.float32)


def score(keys, rows, cols=0, known=(), own_first=False):
    parts = [row if isinstance(row, tuple) else (row,) for row in rows]
    operands = [*keys, *(part for row in parts for part in row)]
    operands += known
    tiles = keys[0].shape[0] // LANES
    best = jax.ShapeDtypeStruct((tiles, LANES), jnp.float32)
    group = jax.ShapeDtypeStruct((len(rows) // 2 * tiles, LANES), jnp.float32)
    out_shape = [best] * cols + [group] * (1 if own_first else 2)
    inside = pl.BlockSpec(memory_space=pltpu.VMEM)
    found = pl.pallas_call(
        functools.partial(
            score_kernel,
            len(keys),
            cols,
            [len(row) for row in parts],
            len(known),
            own_first,
        ),
        in_specs=[inside] * len(operands),
        out_specs=[inside] * len(out_shape),
        out_shape=out_shape,
        compiler_params=pltpu.CompilerParams(vmem_limit_bytes=VMEM_LIMIT),
        cost_estimate=pl.CostEstimate(flops=0, bytes_accessed=0, transcendentals=0),
    )(*operands)
    return list(found[:cols]), list(found[cols:])


def owner_steps(count):
    half = count // 2
    circle = [count - 1 - 2 * i for i in range(half)] + [count - 2 - 2 * i for i in range(half)]
    return [
        [(circle[i], circle[(i + step) % count]) for i in range(count)]
        for step in range(1, half + 1)
    ]


def per_device(embeddings, basis, owner_ids, sub_cluster):
    row_count = embeddings.shape[0]
    tiles = row_count // LANES
    split_count, owner_count = lax.axis_size("split"), lax.axis_size("owners")

    def swap(block, offset):
        return lax.ppermute(block, "split", [(s, s ^ offset) for s in range(split_count)])

    def halves(block):
        return block[: row_count // 2], block[row_count // 2 :]

    own = project(embeddings, basis, owner_ids, sub_cluster)
    both = ("owners", "split")
    *steps, last = [
        [(a * split_count + s, b * split_count + (s ^ 1)) for a, b in step for s in range(split_count)]
        for step in owner_steps(owner_count)
    ]
    keys = [lax.ppermute(own, both, step) for step in steps]
    nearby = lax.ppermute(own, both, last)
    offsets = range(2, split_count, 2)
    one_turn = 1 + (lax.axis_index("groups") >> 16)
    besides = lax.fori_loop(
        0,
        one_turn,
        lambda _, blocks: [swap(block, offset) for block, offset in zip(blocks, offsets)],
        [own] * len(offsets),
    )
    core, *across = [tuple(swap(part, 1) for part in halves(block)) for block in [own, *besides]]
    rows = [own, *across, core, *besides]
    col_best, row_best = score([*keys, nearby], rows, cols=len(keys))
    backs = [
        lax.ppermute(found, both, [(b, a) for a, b in step])
        for found, step in zip(col_best, steps)
    ]
    _, (own_best,) = score([own], rows, own_first=True)
    local = jnp.maximum(row_best[0], swap(row_best[1], 1))
    best = jnp.maximum(local[:tiles], own_best[:tiles])
    for at, offset in enumerate(offsets, start=1):
        best = jnp.maximum(best, swap(local[at * tiles : (at + 1) * tiles], offset + 1))
    for back in backs:
        best = jnp.maximum(best, back)
    return jnp.maximum(best, -1.0).reshape(row_count)


def solution(mesh):
    placed = (
        P(("groups", "owners", "split"), None),
        P(),
        P(("groups", "owners", "split"), None),
        P(("groups", "owners", "split")),
    )
    return jax.shard_map(
        per_device,
        mesh=mesh,
        in_specs=placed,
        out_specs=P(("groups", "owners", "split")),
        check_vma=False,
    )
```

```python
import functools

import jax
import jax.numpy as jnp
from jax import lax
from jax.experimental import pallas as pl
from jax.experimental.pallas import tpu as pltpu
from jax.sharding import PartitionSpec as P

CPO = 8
LANES = 128
TAG_ROWS = 16
ABSENT = -2.0
STEPS = 8
ROW_PARTS = 4
VMEM_LIMIT = 48 * 1024 * 1024


def project_kernel(source_hbm, basis_hbm, owner_hbm, sub_hbm, packed_ref, *scratch):
    source, basis, owner, sub, sems, tag_sems = scratch
    row_count, depth = source.shape
    width = basis.shape[1]
    spans = cut(depth, STEPS)
    copies = [
        (
            pltpu.make_async_copy(basis_hbm.at[span, :], basis.at[span, :], sems.at[0, step]),
            pltpu.make_async_copy(source_hbm.at[:, span], source.at[:, span], sems.at[1, step]),
        )
        for step, span in enumerate(spans)
    ]
    tag_copies = [
        pltpu.make_async_copy(owner_hbm, owner, tag_sems.at[0]),
        pltpu.make_async_copy(sub_hbm, sub, tag_sems.at[1]),
    ]
    for copy in [copy for pair in copies for copy in pair] + tag_copies:
        copy.start()
    totals = [None] * ROW_PARTS
    for span, pair in zip(spans, copies):
        for copy in pair:
            copy.wait()
        for at, rows in enumerate(cut(row_count, ROW_PARTS)):
            part = jnp.dot(source[rows, span], basis[span, :], preferred_element_type=jnp.float32)
            totals[at] = part if totals[at] is None else totals[at] + part
    for projected, rows in zip(totals, cut(row_count, ROW_PARTS)):
        norms = jnp.sum(projected * projected, axis=1, keepdims=True)
        packed_ref[rows, :] = (projected * lax.rsqrt(norms + 1e-06)).astype(jnp.bfloat16)
    for copy in tag_copies:
        copy.wait()
    tags = (owner[...] * CPO + sub[...] + 1).astype(jnp.float32)
    tags = jnp.concatenate(
        [tags, jnp.zeros((TAG_ROWS - tags.shape[0], LANES), jnp.float32)], axis=0
    )
    tags = jnp.concatenate([tags, jnp.zeros((TAG_ROWS, width - LANES), jnp.float32)], axis=1)
    packed_ref[row_count:, :] = tags.astype(jnp.bfloat16)


def cut(size, steps):
    return [pl.ds(size // steps * step, size // steps) for step in range(steps)]


def project(embeddings, basis, owner_ids, sub_cluster):
    row_count, depth = embeddings.shape
    width = basis.shape[1]
    tag_shape = (row_count // LANES, LANES)
    return pl.pallas_call(
        project_kernel,
        in_specs=[pl.BlockSpec(memory_space=pltpu.HBM)] * 4,
        out_specs=pl.BlockSpec(memory_space=pltpu.VMEM),
        out_shape=jax.ShapeDtypeStruct((row_count + TAG_ROWS, width), jnp.bfloat16),
        scratch_shapes=[
            pltpu.VMEM((row_count, depth), jnp.bfloat16),
            pltpu.VMEM((depth, width), jnp.bfloat16),
            pltpu.VMEM(tag_shape, jnp.int32),
            pltpu.VMEM(tag_shape, jnp.int32),
            pltpu.SemaphoreType.DMA((2, STEPS)),
            pltpu.SemaphoreType.DMA((2,)),
        ],
        compiler_params=pltpu.CompilerParams(vmem_limit_bytes=VMEM_LIMIT),
        cost_estimate=pl.CostEstimate(
            flops=2 * row_count * depth * width,
            bytes_accessed=2 * depth * (row_count + width),
            transcendentals=0,
        ),
    )(
        *[
            pltpu.with_memory_space_constraint(array, pltpu.HBM)
            for array in (
                embeddings,
                basis,
                owner_ids.reshape(tag_shape),
                sub_cluster.reshape(tag_shape),
            )
        ]
    )


def score_kernel(key_count, cols, row_parts, known, own_first, *refs):
    refs = list(refs)
    group = len(row_parts) // 2
    key_refs = [refs.pop(0) for _ in range(key_count)]
    row_refs = [[refs.pop(0) for _ in range(parts)] for parts in row_parts]
    known_refs = [refs.pop(0) for _ in range(known)]
    col_refs = [refs.pop(0) for _ in range(cols)]
    row_outs = refs
    row_count = key_refs[0].shape[0] - TAG_ROWS
    tiles = row_count // LANES
    best = [
        [jnp.full((8, LANES), ABSENT, jnp.float32) for _ in range(tiles)]
        for _ in range(key_count if own_first else cols)
    ]
    for block, part_refs in enumerate(row_refs):
        tag_ref = part_refs[-1]
        row_tags = tag_ref[tag_ref.shape[0] - TAG_ROWS :, :LANES].astype(jnp.float32)
        place = 0
        for part_ref in part_refs:
            count = part_ref.shape[0] // LANES * LANES
            tags = [
                jnp.broadcast_to(row_tags[at : at + 1, :], (LANES, LANES)).T
                for at in range(place, place + count // LANES)
            ]
            across = [None] * len(tags)
            for key, key_ref in enumerate(key_refs):
                key_tags = key_ref[row_count:, :LANES].astype(jnp.float32)
                scores = lax.dot_general(
                    part_ref[:count, :],
                    key_ref[:row_count, :],
                    (((1,), (1,)), ((), ())),
                    preferred_element_type=jnp.float32,
                )
                for tile, tag in enumerate(tags):
                    for at in range(tiles):
                        same = tag == key_tags[at : at + 1, :]
                        if own_first and block == 0 and at == place + tile:
                            same = same & (
                                lax.broadcasted_iota(jnp.int32, (LANES, LANES), 0)
                                != lax.broadcasted_iota(jnp.int32, (LANES, LANES), 1)
                            )
                        kept = scores[
                            tile * LANES : (tile + 1) * LANES, at * LANES : (at + 1) * LANES
                        ]
                        kept = jnp.where(same, kept, ABSENT)
                        if key < len(best):
                            best[key][at] = jnp.maximum(
                                best[key][at], jnp.max(kept.reshape(LANES // 8, 8, LANES), axis=0)
                            )
                        if not own_first:
                            across[tile] = (
                                kept if across[tile] is None else jnp.maximum(across[tile], kept)
                            )
            if not own_first:
                for tile in range(len(tags)):
                    at = block % group * tiles + place + tile
                    found = jnp.max(across[tile].T, axis=0, keepdims=True)
                    if block // group < known:
                        found = jnp.maximum(found, known_refs[block // group][at : at + 1, :])
                    row_outs[block // group][at : at + 1, :] = found
            place += len(tags)
    for key, found in enumerate(best):
        for at in range(tiles):
            highest = jnp.max(found[at], axis=0, keepdims=True)
            if own_first:
                row_outs[0][at : at + 1, :] = highest
            else:
                col_refs[key][at : at + 1, :] = highest
    if own_first:
        rest = row_outs[0].shape[0] - tiles
        row_outs[0][tiles:, :] = jnp.full((rest, LANES), ABSENT, jnp.float32)


def score(keys, rows, cols=0, known=(), own_first=False):
    parts = [row if isinstance(row, tuple) else (row,) for row in rows]
    operands = [*keys, *(part for row in parts for part in row)]
    operands += known
    tiles = keys[0].shape[0] // LANES
    best = jax.ShapeDtypeStruct((tiles, LANES), jnp.float32)
    group = jax.ShapeDtypeStruct((len(rows) // 2 * tiles, LANES), jnp.float32)
    out_shape = [best] * cols + [group] * (1 if own_first else 2)
    inside = pl.BlockSpec(memory_space=pltpu.VMEM)
    found = pl.pallas_call(
        functools.partial(
            score_kernel,
            len(keys),
            cols,
            [len(row) for row in parts],
            len(known),
            own_first,
        ),
        in_specs=[inside] * len(operands),
        out_specs=[inside] * len(out_shape),
        out_shape=out_shape,
        compiler_params=pltpu.CompilerParams(vmem_limit_bytes=VMEM_LIMIT),
        cost_estimate=pl.CostEstimate(flops=0, bytes_accessed=0, transcendentals=0),
    )(*operands)
    return list(found[:cols]), list(found[cols:])


def owner_steps(count):
    half = count // 2
    circle = [count - 1 - 2 * i for i in range(half)] + [count - 2 - 2 * i for i in range(half)]
    return [
        [(circle[(i + step) % count], circle[i]) for i in range(count)]
        for step in range(1, half + 1)
    ]


def per_device(embeddings, basis, owner_ids, sub_cluster):
    row_count = embeddings.shape[0]
    tiles = row_count // LANES
    split_count, owner_count = lax.axis_size("split"), lax.axis_size("owners")

    def swap(block, offset):
        return lax.ppermute(block, "split", [(s, s ^ offset) for s in range(split_count)])

    def halves(block):
        return block[: row_count // 2], block[row_count // 2 :]

    own = project(embeddings, basis, owner_ids, sub_cluster)
    both = ("owners", "split")
    *steps, last = [
        [(a * split_count + s, b * split_count + (s ^ 1)) for a, b in step for s in range(split_count)]
        for step in owner_steps(owner_count)
    ]
    keys = [lax.ppermute(own, both, step) for step in steps]
    nearby = lax.ppermute(own, both, last)
    offsets = range(2, split_count, 2)
    one_turn = 1 + (lax.axis_index("groups") >> 16)
    besides = lax.fori_loop(
        0,
        one_turn,
        lambda _, blocks: [swap(block, offset) for block, offset in zip(blocks, offsets)],
        [own] * len(offsets),
    )
    core, *across = [tuple(swap(part, 1) for part in halves(block)) for block in [own, *besides]]
    rows = [own, *across, core, *besides]
    row_best, backs = [], []
    for key, step in zip(keys, steps):
        (found,), row_best = score([key], rows, cols=1, known=row_best)
        backs.append(lax.ppermute(found, both, [(b, a) for a, b in step]))
    _, row_best = score([nearby], rows, known=row_best)
    _, (own_best,) = score([own], rows, own_first=True)
    local = jnp.maximum(row_best[0], swap(row_best[1], 1))
    best = jnp.maximum(local[:tiles], own_best[:tiles])
    for at, offset in enumerate(offsets, start=1):
        best = jnp.maximum(best, swap(local[at * tiles : (at + 1) * tiles], offset + 1))
    for back in backs:
        best = jnp.maximum(best, back)
    return jnp.maximum(best, -1.0).reshape(row_count)


def solution(mesh):
    placed = (
        P(("groups", "owners", "split"), None),
        P(),
        P(("groups", "owners", "split"), None),
        P(("groups", "owners", "split")),
    )
    return jax.shard_map(
        per_device,
        mesh=mesh,
        in_specs=placed,
        out_specs=P(("groups", "owners", "split")),
        check_vma=False,
    )
```

```python
import functools

import jax
import jax.numpy as jnp
from jax import lax
from jax.experimental import pallas as pl
from jax.experimental.pallas import tpu as pltpu
from jax.sharding import PartitionSpec as P

CPO = 8
LANES = 128
TAG_ROWS = 16
ABSENT = -2.0
STEPS = 8
ROW_PARTS = 4
RUN = 2 * LANES
VMEM_LIMIT = 48 * 1024 * 1024


def project_kernel(source_hbm, basis_hbm, owner_hbm, sub_hbm, packed_ref, *scratch):
    source, basis, owner, sub, sems, tag_sems = scratch
    row_count, depth = source.shape
    width = basis.shape[1]
    spans = cut(depth, STEPS)
    copies = [
        (
            pltpu.make_async_copy(basis_hbm.at[span, :], basis.at[span, :], sems.at[0, step]),
            pltpu.make_async_copy(source_hbm.at[:, span], source.at[:, span], sems.at[1, step]),
        )
        for step, span in enumerate(spans)
    ]
    tag_copies = [
        pltpu.make_async_copy(owner_hbm, owner, tag_sems.at[0]),
        pltpu.make_async_copy(sub_hbm, sub, tag_sems.at[1]),
    ]
    for copy in [copy for pair in copies for copy in pair] + tag_copies:
        copy.start()
    totals = [None] * ROW_PARTS
    for span, pair in zip(spans, copies):
        for copy in pair:
            copy.wait()
        for at, rows in enumerate(cut(row_count, ROW_PARTS)):
            part = jnp.dot(source[rows, span], basis[span, :], preferred_element_type=jnp.float32)
            totals[at] = part if totals[at] is None else totals[at] + part
    for projected, rows in zip(totals, cut(row_count, ROW_PARTS)):
        norms = jnp.sum(projected * projected, axis=1, keepdims=True)
        packed_ref[rows, :] = (projected * lax.rsqrt(norms + 1e-06)).astype(jnp.bfloat16)
    for copy in tag_copies:
        copy.wait()
    tags = (owner[...] * CPO + sub[...] + 1).astype(jnp.float32)
    tags = jnp.concatenate(
        [tags, jnp.zeros((TAG_ROWS - tags.shape[0], LANES), jnp.float32)], axis=0
    )
    tags = jnp.concatenate([tags, jnp.zeros((TAG_ROWS, width - LANES), jnp.float32)], axis=1)
    packed_ref[row_count:, :] = tags.astype(jnp.bfloat16)


def cut(size, steps):
    return [pl.ds(size // steps * step, size // steps) for step in range(steps)]


def project(embeddings, basis, owner_ids, sub_cluster):
    row_count, depth = embeddings.shape
    width = basis.shape[1]
    tag_shape = (row_count // LANES, LANES)
    return pl.pallas_call(
        project_kernel,
        in_specs=[pl.BlockSpec(memory_space=pltpu.HBM)] * 4,
        out_specs=pl.BlockSpec(memory_space=pltpu.VMEM),
        out_shape=jax.ShapeDtypeStruct((row_count + TAG_ROWS, width), jnp.bfloat16),
        scratch_shapes=[
            pltpu.VMEM((row_count, depth), jnp.bfloat16),
            pltpu.VMEM((depth, width), jnp.bfloat16),
            pltpu.VMEM(tag_shape, jnp.int32),
            pltpu.VMEM(tag_shape, jnp.int32),
            pltpu.SemaphoreType.DMA((2, STEPS)),
            pltpu.SemaphoreType.DMA((2,)),
        ],
        compiler_params=pltpu.CompilerParams(vmem_limit_bytes=VMEM_LIMIT),
        cost_estimate=pl.CostEstimate(
            flops=2 * row_count * depth * width,
            bytes_accessed=2 * depth * (row_count + width),
            transcendentals=0,
        ),
    )(
        *[
            pltpu.with_memory_space_constraint(array, pltpu.HBM)
            for array in (
                embeddings,
                basis,
                owner_ids.reshape(tag_shape),
                sub_cluster.reshape(tag_shape),
            )
        ]
    )


def score_kernel(key_count, cols, row_parts, known, own_first, *refs):
    refs = list(refs)
    group = len(row_parts) // 2
    key_refs = [refs.pop(0) for _ in range(key_count)]
    row_refs = [[refs.pop(0) for _ in range(parts)] for parts in row_parts]
    known_refs = [refs.pop(0) for _ in range(known)]
    col_refs = [refs.pop(0) for _ in range(cols)]
    row_outs = refs
    row_count = key_refs[0].shape[0] - TAG_ROWS
    tiles = row_count // LANES
    best = [
        [jnp.full((8, LANES), ABSENT, jnp.float32) for _ in range(tiles)]
        for _ in range(key_count if own_first else cols)
    ]
    for block, part_refs in enumerate(row_refs):
        tag_ref = part_refs[-1]
        row_tags = tag_ref[tag_ref.shape[0] - TAG_ROWS :, :LANES].astype(jnp.float32)
        place = 0
        runs = [
            (part_ref, first)
            for part_ref in part_refs
            for first in range(0, part_ref.shape[0] // LANES * LANES, RUN)
        ]
        for part_ref, first in runs:
            count = RUN
            tags = [
                jnp.broadcast_to(row_tags[at : at + 1, :], (LANES, LANES)).T
                for at in range(place, place + count // LANES)
            ]
            across = [None] * len(tags)
            for key, key_ref in enumerate(key_refs):
                key_tags = key_ref[row_count:, :LANES].astype(jnp.float32)
                scores = lax.dot_general(
                    part_ref[first : first + count, :],
                    key_ref[:row_count, :],
                    (((1,), (1,)), ((), ())),
                    preferred_element_type=jnp.float32,
                )
                for tile, tag in enumerate(tags):
                    for at in range(tiles):
                        same = tag == key_tags[at : at + 1, :]
                        if own_first and block == 0 and at == place + tile:
                            same = same & (
                                lax.broadcasted_iota(jnp.int32, (LANES, LANES), 0)
                                != lax.broadcasted_iota(jnp.int32, (LANES, LANES), 1)
                            )
                        kept = scores[
                            tile * LANES : (tile + 1) * LANES, at * LANES : (at + 1) * LANES
                        ]
                        kept = jnp.where(same, kept, ABSENT)
                        if key < len(best):
                            best[key][at] = jnp.maximum(
                                best[key][at], jnp.max(kept.reshape(LANES // 8, 8, LANES), axis=0)
                            )
                        if not own_first:
                            across[tile] = (
                                kept if across[tile] is None else jnp.maximum(across[tile], kept)
                            )
            if not own_first:
                for tile in range(len(tags)):
                    at = block % group * tiles + place + tile
                    found = jnp.max(across[tile].T, axis=0, keepdims=True)
                    if block // group < known:
                        found = jnp.maximum(found, known_refs[block // group][at : at + 1, :])
                    row_outs[block // group][at : at + 1, :] = found
            place += len(tags)
    for key, found in enumerate(best):
        for at in range(tiles):
            highest = jnp.max(found[at], axis=0, keepdims=True)
            if own_first:
                row_outs[0][at : at + 1, :] = highest
            else:
                col_refs[key][at : at + 1, :] = highest
    if own_first:
        rest = row_outs[0].shape[0] - tiles
        row_outs[0][tiles:, :] = jnp.full((rest, LANES), ABSENT, jnp.float32)


def score(keys, rows, cols=0, known=(), own_first=False):
    parts = [row if isinstance(row, tuple) else (row,) for row in rows]
    operands = [*keys, *(part for row in parts for part in row)]
    operands += known
    tiles = keys[0].shape[0] // LANES
    best = jax.ShapeDtypeStruct((tiles, LANES), jnp.float32)
    group = jax.ShapeDtypeStruct((len(rows) // 2 * tiles, LANES), jnp.float32)
    out_shape = [best] * cols + [group] * (1 if own_first else 2)
    inside = pl.BlockSpec(memory_space=pltpu.VMEM)
    found = pl.pallas_call(
        functools.partial(
            score_kernel,
            len(keys),
            cols,
            [len(row) for row in parts],
            len(known),
            own_first,
        ),
        in_specs=[inside] * len(operands),
        out_specs=[inside] * len(out_shape),
        out_shape=out_shape,
        compiler_params=pltpu.CompilerParams(vmem_limit_bytes=VMEM_LIMIT),
        cost_estimate=pl.CostEstimate(flops=0, bytes_accessed=0, transcendentals=0),
    )(*operands)
    return list(found[:cols]), list(found[cols:])


def owner_steps(count):
    half = count // 2
    circle = [count - 1 - 2 * i for i in range(half)] + [count - 2 - 2 * i for i in range(half)]
    return [
        [(circle[i], circle[(i + step) % count]) for i in range(count)]
        for step in range(1, half + 1)
    ]


def per_device(embeddings, basis, owner_ids, sub_cluster):
    row_count = embeddings.shape[0]
    tiles = row_count // LANES
    split_count, owner_count = lax.axis_size("split"), lax.axis_size("owners")

    def swap(block, offset):
        return lax.ppermute(block, "split", [(s, s ^ offset) for s in range(split_count)])

    def halves(block):
        return block[: row_count // 2], block[row_count // 2 :]

    own = project(embeddings, basis, owner_ids, sub_cluster)
    both = ("owners", "split")
    *steps, last = [
        [(a * split_count + s, b * split_count + (s ^ 1)) for a, b in step for s in range(split_count)]
        for step in owner_steps(owner_count)
    ]
    keys = [lax.ppermute(own, both, step) for step in steps]
    nearby = lax.ppermute(own, both, last)
    offsets = range(2, split_count, 2)
    one_turn = 1 + (lax.axis_index("groups") >> 16)
    besides = lax.fori_loop(
        0,
        one_turn,
        lambda _, blocks: [swap(block, offset) for block, offset in zip(blocks, offsets)],
        [own] * len(offsets),
    )
    core, *across = [tuple(swap(part, 1) for part in halves(block)) for block in [own, *besides]]
    rows = [own, *across, core, *besides]
    row_best, backs = [], []
    for key, step in zip(keys, steps):
        (found,), row_best = score([key], rows, cols=1, known=row_best)
        backs.append(lax.ppermute(found, both, [(b, a) for a, b in step]))
    _, row_best = score([nearby], rows, known=row_best)
    _, (own_best,) = score([own], rows, own_first=True)
    local = jnp.maximum(row_best[0], swap(row_best[1], 1))
    best = jnp.maximum(local[:tiles], own_best[:tiles])
    for at, offset in enumerate(offsets, start=1):
        best = jnp.maximum(best, swap(local[at * tiles : (at + 1) * tiles], offset + 1))
    for back in backs:
        best = jnp.maximum(best, back)
    return jnp.maximum(best, -1.0).reshape(row_count)


def solution(mesh):
    placed = (
        P(("groups", "owners", "split"), None),
        P(),
        P(("groups", "owners", "split"), None),
        P(("groups", "owners", "split")),
    )
    return jax.shard_map(
        per_device,
        mesh=mesh,
        in_specs=placed,
        out_specs=P(("groups", "owners", "split")),
        check_vma=False,
    )
```

```python
import functools

import jax
import jax.numpy as jnp
from jax import lax
from jax.experimental import pallas as pl
from jax.experimental.pallas import tpu as pltpu
from jax.sharding import PartitionSpec as P

CPO = 8
LANES = 128
TAG_ROWS = 16
ABSENT = -2.0
STEPS = 8
ROW_PARTS = 4
VMEM_LIMIT = 48 * 1024 * 1024


def project_kernel(source_hbm, basis_hbm, owner_hbm, sub_hbm, packed_ref, *scratch):
    source, basis, owner, sub, sems, tag_sems = scratch
    row_count, depth = source.shape
    width = basis.shape[1]
    spans = cut(depth, STEPS)
    copies = [
        (
            pltpu.make_async_copy(basis_hbm.at[span, :], basis.at[span, :], sems.at[0, step]),
            pltpu.make_async_copy(source_hbm.at[:, span], source.at[:, span], sems.at[1, step]),
        )
        for step, span in enumerate(spans)
    ]
    tag_copies = [
        pltpu.make_async_copy(owner_hbm, owner, tag_sems.at[0]),
        pltpu.make_async_copy(sub_hbm, sub, tag_sems.at[1]),
    ]
    for copy in [copy for pair in copies for copy in pair] + tag_copies:
        copy.start()
    totals = [None] * ROW_PARTS
    for span, pair in zip(spans, copies):
        for copy in pair:
            copy.wait()
        for at, rows in enumerate(cut(row_count, ROW_PARTS)):
            part = jnp.dot(source[rows, span], basis[span, :], preferred_element_type=jnp.float32)
            totals[at] = part if totals[at] is None else totals[at] + part
    for projected, rows in zip(totals, cut(row_count, ROW_PARTS)):
        norms = jnp.sum(projected * projected, axis=1, keepdims=True)
        packed_ref[rows, :] = (projected * lax.rsqrt(norms + 1e-06)).astype(jnp.bfloat16)
    for copy in tag_copies:
        copy.wait()
    tags = (owner[...] * CPO + sub[...] + 1).astype(jnp.float32)
    tags = jnp.concatenate(
        [tags, jnp.zeros((TAG_ROWS - tags.shape[0], LANES), jnp.float32)], axis=0
    )
    tags = jnp.concatenate([tags, jnp.zeros((TAG_ROWS, width - LANES), jnp.float32)], axis=1)
    packed_ref[row_count:, :] = tags.astype(jnp.bfloat16)


def cut(size, steps):
    return [pl.ds(size // steps * step, size // steps) for step in range(steps)]


def project(embeddings, basis, owner_ids, sub_cluster):
    row_count, depth = embeddings.shape
    width = basis.shape[1]
    tag_shape = (row_count // LANES, LANES)
    return pl.pallas_call(
        project_kernel,
        in_specs=[pl.BlockSpec(memory_space=pltpu.HBM)] * 4,
        out_specs=pl.BlockSpec(memory_space=pltpu.VMEM),
        out_shape=jax.ShapeDtypeStruct((row_count + TAG_ROWS, width), jnp.bfloat16),
        scratch_shapes=[
            pltpu.VMEM((row_count, depth), jnp.bfloat16),
            pltpu.VMEM((depth, width), jnp.bfloat16),
            pltpu.VMEM(tag_shape, jnp.int32),
            pltpu.VMEM(tag_shape, jnp.int32),
            pltpu.SemaphoreType.DMA((2, STEPS)),
            pltpu.SemaphoreType.DMA((2,)),
        ],
        compiler_params=pltpu.CompilerParams(vmem_limit_bytes=VMEM_LIMIT),
        cost_estimate=pl.CostEstimate(
            flops=2 * row_count * depth * width,
            bytes_accessed=2 * depth * (row_count + width),
            transcendentals=0,
        ),
    )(
        *[
            pltpu.with_memory_space_constraint(array, pltpu.HBM)
            for array in (
                embeddings,
                basis,
                owner_ids.reshape(tag_shape),
                sub_cluster.reshape(tag_shape),
            )
        ]
    )


def score_kernel(key_count, cols, row_parts, known, own_first, *refs):
    refs = list(refs)
    group = len(row_parts) // 2
    key_refs = [refs.pop(0) for _ in range(key_count)]
    row_refs = [[refs.pop(0) for _ in range(parts)] for parts in row_parts]
    known_refs = [refs.pop(0) for _ in range(known)]
    col_refs = [refs.pop(0) for _ in range(cols)]
    row_outs = refs
    row_count = key_refs[0].shape[0] - TAG_ROWS
    tiles = row_count // LANES
    columns = [key_ref[:row_count, :].T for key_ref in key_refs]
    best = [
        [jnp.full((8, LANES), ABSENT, jnp.float32) for _ in range(tiles)]
        for _ in range(key_count if own_first else cols)
    ]
    for block, part_refs in enumerate(row_refs):
        tag_ref = part_refs[-1]
        row_tags = tag_ref[tag_ref.shape[0] - TAG_ROWS :, :LANES].astype(jnp.float32)
        place = 0
        for part_ref in part_refs:
            count = part_ref.shape[0] // LANES * LANES
            tags = [
                jnp.broadcast_to(row_tags[at : at + 1, :], (LANES, LANES)).T
                for at in range(place, place + count // LANES)
            ]
            across = [None] * len(tags)
            for key, key_ref in enumerate(key_refs):
                key_tags = key_ref[row_count:, :LANES].astype(jnp.float32)
                scores = jnp.dot(
                    part_ref[:count, :], columns[key], preferred_element_type=jnp.float32
                )
                for tile, tag in enumerate(tags):
                    for at in range(tiles):
                        same = tag == key_tags[at : at + 1, :]
                        if own_first and block == 0 and at == place + tile:
                            same = same & (
                                lax.broadcasted_iota(jnp.int32, (LANES, LANES), 0)
                                != lax.broadcasted_iota(jnp.int32, (LANES, LANES), 1)
                            )
                        kept = scores[
                            tile * LANES : (tile + 1) * LANES, at * LANES : (at + 1) * LANES
                        ]
                        kept = jnp.where(same, kept, ABSENT)
                        if key < len(best):
                            best[key][at] = jnp.maximum(
                                best[key][at], jnp.max(kept.reshape(LANES // 8, 8, LANES), axis=0)
                            )
                        if not own_first:
                            across[tile] = (
                                kept if across[tile] is None else jnp.maximum(across[tile], kept)
                            )
            if not own_first:
                for tile in range(len(tags)):
                    at = block % group * tiles + place + tile
                    found = jnp.max(across[tile].T, axis=0, keepdims=True)
                    if block // group < known:
                        found = jnp.maximum(found, known_refs[block // group][at : at + 1, :])
                    row_outs[block // group][at : at + 1, :] = found
            place += len(tags)
    for key, found in enumerate(best):
        for at in range(tiles):
            highest = jnp.max(found[at], axis=0, keepdims=True)
            if own_first:
                row_outs[0][at : at + 1, :] = highest
            else:
                col_refs[key][at : at + 1, :] = highest
    if own_first:
        rest = row_outs[0].shape[0] - tiles
        row_outs[0][tiles:, :] = jnp.full((rest, LANES), ABSENT, jnp.float32)


def score(keys, rows, cols=0, known=(), own_first=False):
    parts = [row if isinstance(row, tuple) else (row,) for row in rows]
    operands = [*keys, *(part for row in parts for part in row)]
    operands += known
    tiles = keys[0].shape[0] // LANES
    best = jax.ShapeDtypeStruct((tiles, LANES), jnp.float32)
    group = jax.ShapeDtypeStruct((len(rows) // 2 * tiles, LANES), jnp.float32)
    out_shape = [best] * cols + [group] * (1 if own_first else 2)
    inside = pl.BlockSpec(memory_space=pltpu.VMEM)
    found = pl.pallas_call(
        functools.partial(
            score_kernel,
            len(keys),
            cols,
            [len(row) for row in parts],
            len(known),
            own_first,
        ),
        in_specs=[inside] * len(operands),
        out_specs=[inside] * len(out_shape),
        out_shape=out_shape,
        compiler_params=pltpu.CompilerParams(vmem_limit_bytes=VMEM_LIMIT),
        cost_estimate=pl.CostEstimate(flops=0, bytes_accessed=0, transcendentals=0),
    )(*operands)
    return list(found[:cols]), list(found[cols:])


def owner_steps(count):
    half = count // 2
    circle = [count - 1 - 2 * i for i in range(half)] + [count - 2 - 2 * i for i in range(half)]
    return [
        [(circle[i], circle[(i + step) % count]) for i in range(count)]
        for step in range(1, half + 1)
    ]


def per_device(embeddings, basis, owner_ids, sub_cluster):
    row_count = embeddings.shape[0]
    tiles = row_count // LANES
    split_count, owner_count = lax.axis_size("split"), lax.axis_size("owners")

    def swap(block, offset):
        return lax.ppermute(block, "split", [(s, s ^ offset) for s in range(split_count)])

    def halves(block):
        return block[: row_count // 2], block[row_count // 2 :]

    own = project(embeddings, basis, owner_ids, sub_cluster)
    both = ("owners", "split")
    *steps, last = [
        [(a * split_count + s, b * split_count + (s ^ 1)) for a, b in step for s in range(split_count)]
        for step in owner_steps(owner_count)
    ]
    keys = [lax.ppermute(own, both, step) for step in steps]
    nearby = lax.ppermute(own, both, last)
    offsets = range(2, split_count, 2)
    one_turn = 1 + (lax.axis_index("groups") >> 16)
    besides = lax.fori_loop(
        0,
        one_turn,
        lambda _, blocks: [swap(block, offset) for block, offset in zip(blocks, offsets)],
        [own] * len(offsets),
    )
    core, *across = [tuple(swap(part, 1) for part in halves(block)) for block in [own, *besides]]
    rows = [own, *across, core, *besides]
    row_best, backs = [], []
    for key, step in zip(keys, steps):
        (found,), row_best = score([key], rows, cols=1, known=row_best)
        backs.append(lax.ppermute(found, both, [(b, a) for a, b in step]))
    _, row_best = score([nearby], rows, known=row_best)
    _, (own_best,) = score([own], rows, own_first=True)
    local = jnp.maximum(row_best[0], swap(row_best[1], 1))
    best = jnp.maximum(local[:tiles], own_best[:tiles])
    for at, offset in enumerate(offsets, start=1):
        best = jnp.maximum(best, swap(local[at * tiles : (at + 1) * tiles], offset + 1))
    for back in backs:
        best = jnp.maximum(best, back)
    return jnp.maximum(best, -1.0).reshape(row_count)


def solution(mesh):
    placed = (
        P(("groups", "owners", "split"), None),
        P(),
        P(("groups", "owners", "split"), None),
        P(("groups", "owners", "split")),
    )
    return jax.shard_map(
        per_device,
        mesh=mesh,
        in_specs=placed,
        out_specs=P(("groups", "owners", "split")),
        check_vma=False,
    )
```

```python
import functools

import jax
import jax.numpy as jnp
from jax import lax
from jax.experimental import pallas as pl
from jax.experimental.pallas import tpu as pltpu
from jax.sharding import PartitionSpec as P

CPO = 8
LANES = 128
TAG_ROWS = 16
ABSENT = -2.0
STEPS = 8
ROW_PARTS = 2
VMEM_LIMIT = 48 * 1024 * 1024


def project_kernel(source_hbm, basis_hbm, owner_hbm, sub_hbm, packed_ref, *scratch):
    source, basis, owner, sub, sems, tag_sems = scratch
    row_count, depth = source.shape
    width = basis.shape[1]
    spans = cut(depth, STEPS)
    copies = [
        (
            pltpu.make_async_copy(basis_hbm.at[span, :], basis.at[span, :], sems.at[0, step]),
            pltpu.make_async_copy(source_hbm.at[:, span], source.at[:, span], sems.at[1, step]),
        )
        for step, span in enumerate(spans)
    ]
    tag_copies = [
        pltpu.make_async_copy(owner_hbm, owner, tag_sems.at[0]),
        pltpu.make_async_copy(sub_hbm, sub, tag_sems.at[1]),
    ]
    for copy in [copy for pair in copies for copy in pair] + tag_copies:
        copy.start()
    totals = [None] * ROW_PARTS
    for span, pair in zip(spans, copies):
        for copy in pair:
            copy.wait()
        for at, rows in enumerate(cut(row_count, ROW_PARTS)):
            part = jnp.dot(source[rows, span], basis[span, :], preferred_element_type=jnp.float32)
            totals[at] = part if totals[at] is None else totals[at] + part
    for projected, rows in zip(totals, cut(row_count, ROW_PARTS)):
        norms = jnp.sum(projected * projected, axis=1, keepdims=True)
        packed_ref[rows, :] = (projected * lax.rsqrt(norms + 1e-06)).astype(jnp.bfloat16)
    for copy in tag_copies:
        copy.wait()
    tags = (owner[...] * CPO + sub[...] + 1).astype(jnp.float32)
    tags = jnp.concatenate(
        [tags, jnp.zeros((TAG_ROWS - tags.shape[0], LANES), jnp.float32)], axis=0
    )
    tags = jnp.concatenate([tags, jnp.zeros((TAG_ROWS, width - LANES), jnp.float32)], axis=1)
    packed_ref[row_count:, :] = tags.astype(jnp.bfloat16)


def cut(size, steps):
    return [pl.ds(size // steps * step, size // steps) for step in range(steps)]


def project(embeddings, basis, owner_ids, sub_cluster):
    row_count, depth = embeddings.shape
    width = basis.shape[1]
    tag_shape = (row_count // LANES, LANES)
    return pl.pallas_call(
        project_kernel,
        in_specs=[pl.BlockSpec(memory_space=pltpu.HBM)] * 4,
        out_specs=pl.BlockSpec(memory_space=pltpu.VMEM),
        out_shape=jax.ShapeDtypeStruct((row_count + TAG_ROWS, width), jnp.bfloat16),
        scratch_shapes=[
            pltpu.VMEM((row_count, depth), jnp.bfloat16),
            pltpu.VMEM((depth, width), jnp.bfloat16),
            pltpu.VMEM(tag_shape, jnp.int32),
            pltpu.VMEM(tag_shape, jnp.int32),
            pltpu.SemaphoreType.DMA((2, STEPS)),
            pltpu.SemaphoreType.DMA((2,)),
        ],
        compiler_params=pltpu.CompilerParams(vmem_limit_bytes=VMEM_LIMIT),
        cost_estimate=pl.CostEstimate(
            flops=2 * row_count * depth * width,
            bytes_accessed=2 * depth * (row_count + width),
            transcendentals=0,
        ),
    )(
        *[
            pltpu.with_memory_space_constraint(array, pltpu.HBM)
            for array in (
                embeddings,
                basis,
                owner_ids.reshape(tag_shape),
                sub_cluster.reshape(tag_shape),
            )
        ]
    )


def score_kernel(key_count, cols, row_parts, known, own_first, *refs):
    refs = list(refs)
    group = len(row_parts) // 2
    key_refs = [refs.pop(0) for _ in range(key_count)]
    row_refs = [[refs.pop(0) for _ in range(parts)] for parts in row_parts]
    known_refs = [refs.pop(0) for _ in range(known)]
    col_refs = [refs.pop(0) for _ in range(cols)]
    row_outs = refs
    row_count = key_refs[0].shape[0] - TAG_ROWS
    tiles = row_count // LANES
    best = [
        [jnp.full((8, LANES), ABSENT, jnp.float32) for _ in range(tiles)]
        for _ in range(key_count if own_first else cols)
    ]
    for block, part_refs in enumerate(row_refs):
        tag_ref = part_refs[-1]
        row_tags = tag_ref[tag_ref.shape[0] - TAG_ROWS :, :LANES].astype(jnp.float32)
        place = 0
        for part_ref in part_refs:
            count = part_ref.shape[0] // LANES * LANES
            tags = [
                jnp.broadcast_to(row_tags[at : at + 1, :], (LANES, LANES)).T
                for at in range(place, place + count // LANES)
            ]
            across = [None] * len(tags)
            for key, key_ref in enumerate(key_refs):
                key_tags = key_ref[row_count:, :LANES].astype(jnp.float32)
                scores = lax.dot_general(
                    part_ref[:count, :],
                    key_ref[:row_count, :],
                    (((1,), (1,)), ((), ())),
                    preferred_element_type=jnp.float32,
                )
                for tile, tag in enumerate(tags):
                    for at in range(tiles):
                        same = tag == key_tags[at : at + 1, :]
                        if own_first and block == 0 and at == place + tile:
                            same = same & (
                                lax.broadcasted_iota(jnp.int32, (LANES, LANES), 0)
                                != lax.broadcasted_iota(jnp.int32, (LANES, LANES), 1)
                            )
                        kept = scores[
                            tile * LANES : (tile + 1) * LANES, at * LANES : (at + 1) * LANES
                        ]
                        kept = jnp.where(same, kept, ABSENT)
                        if key < len(best):
                            best[key][at] = jnp.maximum(
                                best[key][at], jnp.max(kept.reshape(LANES // 8, 8, LANES), axis=0)
                            )
                        if not own_first:
                            across[tile] = (
                                kept if across[tile] is None else jnp.maximum(across[tile], kept)
                            )
            if not own_first:
                for tile in range(len(tags)):
                    at = block % group * tiles + place + tile
                    found = jnp.max(across[tile].T, axis=0, keepdims=True)
                    if block // group < known:
                        found = jnp.maximum(found, known_refs[block // group][at : at + 1, :])
                    row_outs[block // group][at : at + 1, :] = found
            place += len(tags)
    for key, found in enumerate(best):
        for at in range(tiles):
            highest = jnp.max(found[at], axis=0, keepdims=True)
            if own_first:
                row_outs[0][at : at + 1, :] = highest
            else:
                col_refs[key][at : at + 1, :] = highest
    if own_first:
        rest = row_outs[0].shape[0] - tiles
        row_outs[0][tiles:, :] = jnp.full((rest, LANES), ABSENT, jnp.float32)


def score(keys, rows, cols=0, known=(), own_first=False):
    parts = [row if isinstance(row, tuple) else (row,) for row in rows]
    operands = [*keys, *(part for row in parts for part in row)]
    operands += known
    tiles = keys[0].shape[0] // LANES
    best = jax.ShapeDtypeStruct((tiles, LANES), jnp.float32)
    group = jax.ShapeDtypeStruct((len(rows) // 2 * tiles, LANES), jnp.float32)
    out_shape = [best] * cols + [group] * (1 if own_first else 2)
    inside = pl.BlockSpec(memory_space=pltpu.VMEM)
    found = pl.pallas_call(
        functools.partial(
            score_kernel,
            len(keys),
            cols,
            [len(row) for row in parts],
            len(known),
            own_first,
        ),
        in_specs=[inside] * len(operands),
        out_specs=[inside] * len(out_shape),
        out_shape=out_shape,
        compiler_params=pltpu.CompilerParams(vmem_limit_bytes=VMEM_LIMIT),
        cost_estimate=pl.CostEstimate(flops=0, bytes_accessed=0, transcendentals=0),
    )(*operands)
    return list(found[:cols]), list(found[cols:])


def owner_steps(count):
    half = count // 2
    circle = [count - 1 - 2 * i for i in range(half)] + [count - 2 - 2 * i for i in range(half)]
    return [
        [(circle[i], circle[(i + step) % count]) for i in range(count)]
        for step in range(1, half + 1)
    ]


def per_device(embeddings, basis, owner_ids, sub_cluster):
    row_count = embeddings.shape[0]
    tiles = row_count // LANES
    split_count, owner_count = lax.axis_size("split"), lax.axis_size("owners")

    def swap(block, offset):
        return lax.ppermute(block, "split", [(s, s ^ offset) for s in range(split_count)])

    def halves(block):
        return block[: row_count // 2], block[row_count // 2 :]

    own = project(embeddings, basis, owner_ids, sub_cluster)
    both = ("owners", "split")
    *steps, last = [
        [(a * split_count + s, b * split_count + (s ^ 1)) for a, b in step for s in range(split_count)]
        for step in owner_steps(owner_count)
    ]
    keys = [lax.ppermute(own, both, step) for step in steps]
    nearby = lax.ppermute(own, both, last)
    offsets = range(2, split_count, 2)
    one_turn = 1 + (lax.axis_index("groups") >> 16)
    besides = lax.fori_loop(
        0,
        one_turn,
        lambda _, blocks: [swap(block, offset) for block, offset in zip(blocks, offsets)],
        [own] * len(offsets),
    )
    core, *across = [tuple(swap(part, 1) for part in halves(block)) for block in [own, *besides]]
    rows = [own, *across, core, *besides]
    row_best, backs = [], []
    for key, step in zip(keys, steps):
        (found,), row_best = score([key], rows, cols=1, known=row_best)
        backs.append(lax.ppermute(found, both, [(b, a) for a, b in step]))
    _, row_best = score([nearby], rows, known=row_best)
    _, (own_best,) = score([own], rows, own_first=True)
    local = jnp.maximum(row_best[0], swap(row_best[1], 1))
    best = jnp.maximum(local[:tiles], own_best[:tiles])
    for at, offset in enumerate(offsets, start=1):
        best = jnp.maximum(best, swap(local[at * tiles : (at + 1) * tiles], offset + 1))
    for back in backs:
        best = jnp.maximum(best, back)
    return jnp.maximum(best, -1.0).reshape(row_count)


def solution(mesh):
    placed = (
        P(("groups", "owners", "split"), None),
        P(),
        P(("groups", "owners", "split"), None),
        P(("groups", "owners", "split")),
    )
    return jax.shard_map(
        per_device,
        mesh=mesh,
        in_specs=placed,
        out_specs=P(("groups", "owners", "split")),
        check_vma=False,
    )
```
